32 devices in a mesh: bank: 8 (over z, x), box: 4 (over y, core).
Axes of the slice: x: 2, y: 2, z: 4, core: 2. Of those that a mesh axis runs over, the one named last changes fastest.
Arguments:
- roi_features: bfloat16 [1024, 7, 7, 1024], P(('bank', 'box')), may hold values from -6 to 6
- box_seconds: int32 [1024], P(('bank', 'box')), may hold values from 0 to 511, as said below
- video_lengths: int32 [3], replicated, may hold values from 1 to 256, 512 in all
- bank_features: bfloat16 [4096, 2048], P(('bank', 'box')), may hold values from -6 to 6
- reduce_weight: bfloat16 [1024, 512], replicated, may hold values from -0.1875 to 0.1875
- reduce_gain: bfloat16 [512], replicated, may hold values from 0.099609375 to 1.8984375
- reduce_shift: bfloat16 [512], replicated, may hold values from -2.5 to 2.5
- spatial_weight: bfloat16 [3, 3, 512, 512], replicated, may hold values from -0.09375 to 0.09375
- spatial_gain: bfloat16 [512], replicated, may hold values from 0.099609375 to 1.8984375
- spatial_shift: bfloat16 [512], replicated, may hold values from -2.5 to 2.5
- expand_weight: bfloat16 [512, 2048], replicated, may hold values from -0.25 to 0.25
- expand_gain: bfloat16 [2048], replicated, may hold values from 0.099609375 to 1.8984375
- expand_shift: bfloat16 [2048], replicated, may hold values from -2.5 to 2.5
- shortcut_weight: bfloat16 [1024, 2048], replicated, may hold values from -0.1875 to 0.1875
- shortcut_gain: bfloat16 [2048], replicated, may hold values from 0.099609375 to 1.8984375
- shortcut_shift: bfloat16 [2048], replicated, may hold values from -2.5 to 2.5
- query_weight: bfloat16 [2048, 512], replicated, may hold values from -0.375 to 0.375
- key_weight: bfloat16 [2048, 512], replicated, may hold values from -0.125 to 0.125
- value_weight: bfloat16 [2048, 512], replicated, may hold values from -0.125 to 0.125
- norm_gain: bfloat16 [512], replicated, may hold values from 0.099609375 to 1.8984375
- norm_shift: bfloat16 [512], replicated, may hold values from -2.5 to 2.5
- output_weight: bfloat16 [512, 2048], replicated, may hold values from -0.25 to 0.25
- output_bias: bfloat16 [2048], replicated, may hold values from -2.5 to 2.5
- class_weight: bfloat16 [4096, 80], replicated, may hold values from -0.09375 to 0.09375
- class_bias: bfloat16 [80], replicated, may hold values from -2.5 to 2.5
- logit_cotangent: float32 [1024, 80], P(('bank', 'box')), may hold values from -6 to 6
Outputs:
- logits: float32 [1024, 80], P(('bank', 'box'))
- roi_gradient: bfloat16 [1024, 7, 7, 1024], P(('bank', 'box'))
- reduce_weight_gradient: float32 [1024, 512], P(None, 'box')
- reduce_gain_gradient: float32 [512], P('box')
- reduce_shift_gradient: float32 [512], P('box')
- spatial_weight_gradient: float32 [3, 3, 512, 512], P(None, None, None, 'box')
- spatial_gain_gradient: float32 [512], P('box')
- spatial_shift_gradient: float32 [512], P('box')
- expand_weight_gradient: float32 [512, 2048], P(None, 'box')
- expand_gain_gradient: float32 [2048], P('box')
- expand_shift_gradient: float32 [2048], P('box')
- shortcut_weight_gradient: float32 [1024, 2048], P(None, 'box')
- shortcut_gain_gradient: float32 [2048], P('box')
- shortcut_shift_gradient: float32 [2048], P('box')
- query_weight_gradient: float32 [2048, 512], P(None, 'box')
- key_weight_gradient: float32 [2048, 512], P(None, 'box')
- value_weight_gradient: float32 [2048, 512], P(None, 'box')
- norm_gain_gradient: float32 [512], P('box')
- norm_shift_gradient: float32 [512], P('box')
- output_weight_gradient: float32 [512, 2048], P(None, 'box')
- output_bias_gradient: float32 [2048], P('box')
- class_weight_gradient: float32 [4096, 80], P('box')
- class_bias_gradient: float32 [80], replicated
The draws below stay inside these ranges and needn't reach their ends.
Inputs may be any that keep to these rules, and one draw needn't show every extreme that they name: `box_seconds`: box i lies at a second from (i // 32) * 16 to (i // 32) * 16 + 15; box 0 at second 0 and the last box at second 512 - 1.
All inputs are finite; a program needn't handle non-finite values.
Results may differ from the reference program's by a relative error of at most 0.03.
Values may be sent and summed in bfloat16 or wider, within the bound.
No kernel may reach another device: no remote copies, remote signals or barrier semaphores. Data moves between devices by JAX's collectives and lax.ppermute only.
A program may use at most 192 MiB of HBM per device.

```python
import math
import jax
import jax.numpy as jnp
import numpy as np
from jax import lax

IN = 1024
MID = 512
OUT = 2048
ATT = 512
CLASSES = 80
GRID = 7
HALF = 30
PER_SEC = 8
BOX_DEV = 32
SEC_DEV = 16
BOXES = 1024
SECONDS = 512
VIDEOS = 3
BANK_DEV = 128
BANK_ROWS = 4096
REACH = 2
N_BANK = 8
N_BOX = 4


def draw_box_seconds(key, part):
    key = jax.random.fold_in(key, 11)
    index = jnp.arange(BOXES, dtype=jnp.int32)
    within = jax.random.randint(key, (BOXES,), 0, SEC_DEV, dtype=jnp.int32)
    seconds = index // BOX_DEV * SEC_DEV + within
    seconds = jnp.where(index == 0, 0, seconds)
    seconds = jnp.where(index == BOXES - 1, SECONDS - 1, seconds)
    return seconds.astype(jnp.int32)


def levels(stream_key, extent, split, smallest, top_value):
    loudness = 1.0
    for axis_at, parts in split:
        draws = jax.random.uniform(jax.random.fold_in(jax.random.fold_in(stream_key, 6), axis_at), (parts,), jnp.float32, smallest / len(split), top_value / len(split))
        loudness = loudness * jnp.repeat(jnp.exp(draws), extent[axis_at] // parts).reshape((-1,) + (1,) * (len(extent) - 1 - axis_at))
    return loudness


def profile(number_of, total, bound, lean):
    loads = [(1 << 20) // math.isqrt(standing ** lean) + 1 for standing in range(2, number_of + 1)]
    spare, counts = total - bound - (number_of - 1), [1] * (number_of - 1)
    while spare > 0:
        movable = [i for i in range(number_of - 1) if counts[i] < bound]
        pool, remaining = sum([loads[i] for i in movable]), spare
        for i in movable:
            more = min(bound - counts[i], max(1, remaining * loads[i] // pool), spare)
            counts[i] = counts[i] + more
            spare = spare - more
    return np.array([bound] + counts)


def uneven(stream_key, amount, total, limit, slope):
    if amount == 2:
        one = jax.random.randint(stream_key, (), max(1, total - limit), min(limit, total - 1) + 1)
        return jnp.stack([one, total - one])
    lengths = jnp.asarray(profile(amount, total, limit, slope), jnp.int32)
    twos = (amount - 1) // 2
    donor, taker = lengths[1:1 + 2 * twos:2], lengths[2:2 + 2 * twos:2]
    room = jnp.minimum(donor - 1, limit - taker)
    shifted = jax.random.randint(jax.random.fold_in(stream_key, 1), (twos,), 0, 1 << 20) % (room + 1)
    lengths = lengths.at[1:1 + 2 * twos:2].set(donor - shifted).at[2:2 + 2 * twos:2].set(taker + shifted)
    return lengths[jax.random.permutation(jax.random.fold_in(stream_key, 2), amount)]


def noise(rng, dims, spread, most, pieces=(), kind=jnp.bfloat16):
    gain = levels(rng, dims, pieces, -0.22, 0.18) if pieces else 1.0
    values = jax.random.normal(rng, dims, jnp.float32) * spread * gain
    return jnp.minimum(jnp.maximum(values, -most), most).astype(kind)


def setup_inputs(seed: int = 0) -> dict:
    arg_keys = jax.random.split(jax.random.key(seed), 27)
    roi_features = noise(arg_keys[0], (BOXES, GRID, GRID, IN), 1.0, 6.0, ((0, 32),))
    box_seconds = draw_box_seconds(jax.random.fold_in(arg_keys[26], 71), 0)
    video_lengths = uneven(arg_keys[2], VIDEOS, SECONDS, min(1200, SECONDS // 2), 1).astype(jnp.int32)
    bank_features = noise(arg_keys[3], (BANK_ROWS, OUT), 1.0, 6.0, ((0, 32),))
    reduce_weight = noise(arg_keys[4], (IN, MID), IN ** -0.5, 0.1875)
    reduce_gain = jnp.clip(1.0 + 0.18 * jax.random.normal(arg_keys[5], (MID,), jnp.float32), 0.099609375, 1.8984375).astype(jnp.bfloat16)
    reduce_shift = noise(arg_keys[6], (MID,), 0.3, 2.5)
    spatial_weight = noise(arg_keys[7], (3, 3, MID, MID), (9 * MID) ** -0.5, 0.09375)
    spatial_gain = jnp.clip(1.0 + 0.18 * jax.random.normal(arg_keys[8], (MID,), jnp.float32), 0.099609375, 1.8984375).astype(jnp.bfloat16)
    spatial_shift = noise(arg_keys[9], (MID,), 0.3, 2.5)
    expand_weight = noise(arg_keys[10], (MID, OUT), MID ** -0.5, 0.25)
    expand_gain = jnp.clip(1.0 + 0.18 * jax.random.normal(arg_keys[11], (OUT,), jnp.float32), 0.099609375, 1.8984375).astype(jnp.bfloat16)
    expand_shift = noise(arg_keys[12], (OUT,), 0.3, 2.5)
    shortcut_weight = noise(arg_keys[13], (IN, OUT), IN ** -0.5, 0.1875)
    shortcut_gain = jnp.clip(1.0 + 0.18 * jax.random.normal(arg_keys[14], (OUT,), jnp.float32), 0.099609375, 1.8984375).astype(jnp.bfloat16)
    shortcut_shift = noise(arg_keys[15], (OUT,), 0.3, 2.5)
    query_weight = noise(arg_keys[16], (OUT, ATT), (OUT // 8) ** -0.5, 0.375)
    key_weight = noise(arg_keys[17], (OUT, ATT), OUT ** -0.5, 0.125)
    value_weight = noise(arg_keys[18], (OUT, ATT), OUT ** -0.5, 0.125)
    norm_gain = jnp.clip(1.0 + 0.18 * jax.random.normal(arg_keys[19], (ATT,), jnp.float32), 0.099609375, 1.8984375).astype(jnp.bfloat16)
    norm_shift = noise(arg_keys[20], (ATT,), 0.3, 2.5)
    output_weight = noise(arg_keys[21], (ATT, OUT), ATT ** -0.5, 0.25)
    output_bias = noise(arg_keys[22], (OUT,), 0.3, 2.5)
    class_weight = noise(arg_keys[23], (2 * OUT, CLASSES), (2 * OUT) ** -0.5, 0.09375)
    class_bias = noise(arg_keys[24], (CLASSES,), 0.3, 2.5)
    logit_cotangent = noise(arg_keys[25], (BOXES, CLASSES), 1.0, 6.0, ((0, 32),), jnp.float32)
    return dict(roi_features=roi_features, box_seconds=box_seconds, video_lengths=video_lengths, bank_features=bank_features, reduce_weight=reduce_weight, reduce_gain=reduce_gain, reduce_shift=reduce_shift, spatial_weight=spatial_weight, spatial_gain=spatial_gain, spatial_shift=spatial_shift, expand_weight=expand_weight, expand_gain=expand_gain, expand_shift=expand_shift, shortcut_weight=shortcut_weight, shortcut_gain=shortcut_gain, shortcut_shift=shortcut_shift, query_weight=query_weight, key_weight=key_weight, value_weight=value_weight, norm_gain=norm_gain, norm_shift=norm_shift, output_weight=output_weight, output_bias=output_bias, class_weight=class_weight, class_bias=class_bias, logit_cotangent=logit_cotangent)


@jax.custom_vjp
def low(v):
    return lax.optimization_barrier(v.astype(jnp.bfloat16)).astype(jnp.float32)

@jax.custom_vjp
def low_back(v):
    return v

def low_keep(v):
    return (low(v), None)

def low_pass(kept, grad):
    return (grad,)

def back_keep(v):
    return (v, None)

def back_low(kept, grad):
    return (low(grad),)
low.defvjp(low_keep, low_pass)
low_back.defvjp(back_keep, back_low)
epsilon = 1e-05
masked_score = -1e+30
highest = lax.Precision.HIGHEST

def matmul(left, right):
    return jnp.dot(left, right, precision=highest)

def segment_of(seconds, video_lengths):
    video_ends = jnp.cumsum(video_lengths).astype(jnp.int32)
    return lax.optimization_barrier(jnp.sum((video_ends[None, :] <= seconds[:, None]).astype(jnp.int32), axis=1)).astype(jnp.int32)

def batch_norm(entries, gain_vector, shift_vector):
    mean_value = lax.optimization_barrier(jnp.mean(entries, axis=0))
    centred = entries - mean_value
    inv_std = lax.rsqrt(lax.optimization_barrier(jnp.mean(centred * centred, axis=0)) + epsilon)
    return centred * inv_std * gain_vector + shift_vector

def spatial_conv(hidden, weight):
    grid_side = hidden.shape[1]
    padded = jnp.pad(hidden, ((0, 0), (1, 1), (1, 1), (0, 0)))
    running = jnp.zeros(hidden.shape[:3] + (weight.shape[3],), jnp.float32)
    for row_step in range(3):
        for column in range(3):
            window = padded[:, row_step:row_step + grid_side, column:column + grid_side, :]
            running = running + jnp.einsum('bhwc,cd->bhwd', window, weight[row_step, column], precision=highest)
    return running

def bottleneck(block, reduce_weight, reduce_gain, reduce_shift, spatial_weight, spatial_gain, spatial_shift, expand_weight, expand_gain, expand_shift, shortcut_weight, shortcut_gain, shortcut_shift):
    box_count, grid_side = (block.shape[0], block.shape[1])
    row_count = box_count * grid_side * grid_side
    roi_rows = block.reshape(row_count, block.shape[3])
    reduced = low_back(matmul(roi_rows, reduce_weight))
    hidden = low(jax.nn.silu(batch_norm(reduced, reduce_gain, reduce_shift)))
    convolved = low_back(spatial_conv(hidden.reshape(box_count, grid_side, grid_side, -1), spatial_weight).reshape(row_count, -1))
    middle = low(jax.nn.silu(batch_norm(convolved, spatial_gain, spatial_shift)))
    expanded = low_back(matmul(middle, expand_weight))
    projected = low_back(matmul(roi_rows, shortcut_weight))
    summed = batch_norm(expanded, expand_gain, expand_shift) + batch_norm(projected, shortcut_gain, shortcut_shift)
    return lax.optimization_barrier(jnp.mean(jax.nn.silu(summed).reshape(box_count, grid_side * grid_side, -1), axis=1))

def reference(roi_features, box_seconds, video_lengths, bank_features, reduce_weight, reduce_gain, reduce_shift, spatial_weight, spatial_gain, spatial_shift, expand_weight, expand_gain, expand_shift, shortcut_weight, shortcut_gain, shortcut_shift, query_weight, key_weight, value_weight, norm_gain, norm_shift, output_weight, output_bias, class_weight, class_bias, logit_cotangent):
    devices = N_BANK * N_BOX
    score_scale = ATT ** (-0.5)
    margin_rows = REACH * BANK_DEV
    span_rows = (2 * REACH + 1) * BANK_DEV
    bank = bank_features.astype(jnp.float32)
    bank_seconds = (jnp.arange(BANK_ROWS, dtype=jnp.int32) // PER_SEC).astype(jnp.int32)
    bank_segments = segment_of(bank_seconds, video_lengths)
    box_segments = segment_of(box_seconds, video_lengths)
    far_rows = jnp.full((margin_rows,), -1000000, jnp.int32)
    padded_seconds = jnp.concatenate([far_rows, bank_seconds, far_rows])
    padded_segments = jnp.concatenate([far_rows, bank_segments, far_rows])
    block_index = jnp.arange(devices, dtype=jnp.int32)
    second_blocks = box_seconds.reshape(devices, BOX_DEV)
    segment_blocks = box_segments.reshape(devices, BOX_DEV)

    def forward(roi, reduce_weight, reduce_gain, reduce_shift, spatial_weight, spatial_gain, spatial_shift, expand_weight, expand_gain, expand_shift, shortcut_weight, shortcut_gain, shortcut_shift, query_weight, key_weight, value_weight, norm_gain, norm_shift, output_weight, output_bias, class_weight, class_bias):

        def block_features(block):
            return bottleneck(block, reduce_weight, reduce_gain, reduce_shift, spatial_weight, spatial_gain, spatial_shift, expand_weight, expand_gain, expand_shift, shortcut_weight, shortcut_gain, shortcut_shift)
        blocks = roi.reshape((devices, BOX_DEV) + roi.shape[1:])
        feature = lax.map(jax.checkpoint(block_features), blocks).reshape(BOXES, OUT)
        feature_low = low(feature)
        queries = low(low_back(matmul(feature_low, query_weight)))
        key_rows = low(low_back(matmul(bank, key_weight)))
        value_rows = low(low_back(matmul(bank, value_weight)))
        zero_rows = jnp.zeros((margin_rows, ATT), jnp.float32)
        keys_padded = jnp.concatenate([zero_rows, key_rows, zero_rows])
        values_padded = jnp.concatenate([zero_rows, value_rows, zero_rows])

        def attend(packed):
            index, query_block, second_block, segment_block = packed
            start = (index * BANK_DEV).astype(jnp.int32)
            key_window = lax.dynamic_slice_in_dim(keys_padded, start, span_rows, 0)
            value_window = lax.dynamic_slice_in_dim(values_padded, start, span_rows, 0)
            window_seconds = lax.dynamic_slice_in_dim(padded_seconds, start, span_rows, 0)
            window_segments = lax.dynamic_slice_in_dim(padded_segments, start, span_rows, 0)
            scores = low_back(matmul(query_block, key_window.T) * score_scale)
            paired = (segment_block[:, None] == window_segments[None, :]) & (jnp.abs(second_block[:, None] - window_seconds[None, :]) <= HALF)
            row_max = lax.optimization_barrier(jnp.max(jnp.where(paired, scores, masked_score), axis=1, keepdims=True))
            row_total = lax.optimization_barrier(jnp.sum(jnp.where(paired, jnp.exp(jnp.where(paired, scores - row_max, 0.0)), 0.0), axis=1, keepdims=True))
            logsum = row_max + jnp.log(row_total)
            attention = low(jnp.where(paired, jnp.exp(jnp.where(paired, scores - logsum, 0.0)), 0.0))
            return matmul(attention, value_window)
        attended = lax.map(jax.checkpoint(attend), (block_index, queries.reshape(devices, BOX_DEV, ATT), second_blocks, segment_blocks)).reshape(BOXES, ATT)
        attended = low_back(attended)
        pre = attended + queries
        centred = pre - lax.optimization_barrier(jnp.mean(pre, axis=1, keepdims=True))
        normed = centred * lax.rsqrt(lax.optimization_barrier(jnp.mean(centred * centred, axis=1, keepdims=True)) + epsilon)
        activated = low(jax.nn.silu(normed * norm_gain + norm_shift))
        branch = low_back(matmul(activated, output_weight) + output_bias)
        combined = feature + branch
        joined = jnp.concatenate([feature_low, low(combined)], axis=1)
        return low_back(matmul(joined, class_weight) + class_bias)
    logits, pullback = jax.vjp(forward, roi_features.astype(jnp.float32), reduce_weight.astype(jnp.float32), reduce_gain.astype(jnp.float32), reduce_shift.astype(jnp.float32), spatial_weight.astype(jnp.float32), spatial_gain.astype(jnp.float32), spatial_shift.astype(jnp.float32), expand_weight.astype(jnp.float32), expand_gain.astype(jnp.float32), expand_shift.astype(jnp.float32), shortcut_weight.astype(jnp.float32), shortcut_gain.astype(jnp.float32), shortcut_shift.astype(jnp.float32), query_weight.astype(jnp.float32), key_weight.astype(jnp.float32), value_weight.astype(jnp.float32), norm_gain.astype(jnp.float32), norm_shift.astype(jnp.float32), output_weight.astype(jnp.float32), output_bias.astype(jnp.float32), class_weight.astype(jnp.float32), class_bias.astype(jnp.float32))
    gradients = pullback(logit_cotangent.astype(jnp.float32))
    return (logits, gradients[0].astype(jnp.bfloat16), gradients[1], gradients[2], gradients[3], gradients[4], gradients[5], gradients[6], gradients[7], gradients[8], gradients[9], gradients[10], gradients[11], gradients[12], gradients[13], gradients[14], gradients[15], gradients[16], gradients[17], gradients[18], gradients[19], gradients[20], gradients[21])
```

```python
import functools
import jax
import jax.numpy as jnp
from jax import lax
from jax.experimental import pallas as pl
from jax.experimental.pallas import tpu as pltpu
from jax.sharding import PartitionSpec as P

HALF = 30
PER_SEC = 8
SEC_DEV = 16
REACH = 2

EPSILON = 1e-05
VMEM_LIMIT = 56 * 2**20
F32, BF16 = jnp.float32, jnp.bfloat16


def params():
    return pltpu.CompilerParams(vmem_limit_bytes=VMEM_LIMIT)


def whole(shape):
    return pl.BlockSpec(shape, lambda *_: (0,) * len(shape), pipeline_mode=pl.Buffered(1))


def column_stats(source, grid_side):
    rows, width = source.shape
    step = rows // grid_side

    def add(k, total):
        return total + jnp.sum(source[pl.ds(k * step, step), :].reshape(step // 8, 8, width), axis=0)

    mean = jnp.sum(lax.fori_loop(0, grid_side, add, jnp.zeros((8, width), F32)), axis=0, keepdims=True) / rows

    def add_square(k, total):
        centred = source[pl.ds(k * step, step), :] - mean
        return total + jnp.sum((centred * centred).reshape(step // 8, 8, width), axis=0)

    var = jnp.sum(lax.fori_loop(0, grid_side, add_square, jnp.zeros((8, width), F32)), axis=0, keepdims=True) / rows
    return mean, lax.rsqrt(var + EPSILON)


def trunk_kernel(grid_side, boxes, roi, wr, w9, affine, x1, inv1, hidden, x2, inv2, middle, acc):
    cells = grid_side * grid_side
    width = acc.shape[1]
    acc[...] = jnp.dot(roi[...], wr[...], preferred_element_type=F32)
    mean, inv = column_stats(acc, grid_side)
    inv1[...] = inv
    gain, shift = 0.5 * affine[0:1, :], 0.5 * affine[1:2, :]
    zeros = jnp.zeros((boxes, width), BF16)
    side = grid_side + 2
    for k in range(side):
        hidden[0, k] = zeros
        hidden[side - 1, k] = zeros
        hidden[k, 0] = zeros
        hidden[k, side - 1] = zeros

    def first(k, carry):
        for w in range(grid_side):
            rows = pl.ds((k * grid_side + w) * boxes, boxes)
            x = (acc[rows, :] - mean) * inv
            x1[rows, :] = x.astype(BF16)
            h = x * gain + shift
            hidden[k + 1, w + 1] = (h + h * jnp.tanh(h)).astype(BF16)
        return carry

    lax.fori_loop(0, grid_side, first, 0)
    for p in range(3):
        for q in range(3):
            window = hidden[p : p + grid_side, q : q + grid_side].reshape(cells * boxes, width)
            product = jnp.dot(window, w9[p * 3 + q], preferred_element_type=F32)
            if p + q == 0:
                acc[...] = product
            else:
                acc[...] += product
    mean2, inv_2 = column_stats(acc, grid_side)
    inv2[...] = inv_2
    gain2, shift2 = 0.5 * affine[2:3, :], 0.5 * affine[3:4, :]

    def second(k, carry):
        for w in range(grid_side):
            rows = pl.ds((k * grid_side + w) * boxes, boxes)
            x = (acc[rows, :] - mean2) * inv_2
            x2[rows, :] = x.astype(BF16)
            h = x * gain2 + shift2
            middle[rows, :] = (h + h * jnp.tanh(h)).astype(BF16)
        return carry

    lax.fori_loop(0, grid_side, second, 0)


def trunk(roi, wr, w9, affine, grid_side, boxes):
    rows = roi.shape[0]
    mid = wr.shape[1]
    side = grid_side + 2
    vm = pl.BlockSpec(memory_space=pltpu.VMEM)
    return pl.pallas_call(
        functools.partial(trunk_kernel, grid_side, boxes),
        in_specs=[vm] * 4,
        out_specs=[vm] * 6,
        out_shape=[
            jax.ShapeDtypeStruct((rows, mid), BF16),
            jax.ShapeDtypeStruct((1, mid), F32),
            jax.ShapeDtypeStruct((side, side, boxes, mid), BF16),
            jax.ShapeDtypeStruct((rows, mid), BF16),
            jax.ShapeDtypeStruct((1, mid), F32),
            jax.ShapeDtypeStruct((rows, mid), BF16),
        ],
        scratch_shapes=[pltpu.VMEM((rows, mid), F32)],
        compiler_params=params(),
        name="trunk",
    )(roi, wr, w9, affine)


def widen_kernel(grid_side, boxes, roi, middle, ws, we, affine, xe, xp, inv, feature, acc_e, acc_p):
    cells = grid_side * grid_side
    width = acc_e.shape[1]
    acc_p[...] = jnp.dot(roi[...], ws[...], preferred_element_type=F32)
    acc_e[...] = jnp.dot(middle[...], we[...], preferred_element_type=F32)
    mean_e, inv_e = column_stats(acc_e, grid_side)
    mean_p, inv_p = column_stats(acc_p, grid_side)
    inv[0:1, :] = inv_e
    inv[1:2, :] = inv_p
    gain_e, gain_p = 0.5 * affine[0:1, :], 0.5 * affine[2:3, :]
    shift = 0.5 * (affine[1:2, :] + affine[3:4, :])

    def cell(k, total):
        for w in range(grid_side):
            rows = pl.ds((k * grid_side + w) * boxes, boxes)
            e = (acc_e[rows, :] - mean_e) * inv_e
            p = (acc_p[rows, :] - mean_p) * inv_p
            xe[rows, :] = e.astype(BF16)
            xp[rows, :] = p.astype(BF16)
            h = e * gain_e + p * gain_p + shift
            total = total + (h + h * jnp.tanh(h))
        return total

    total = lax.fori_loop(0, grid_side, cell, jnp.zeros((boxes, width), F32))
    feature[...] = total / cells


def widen(roi, middle, ws, we, affine, grid_side, boxes, tile=512):
    rows, width_in = roi.shape
    mid, out = we.shape
    column = lambda j: (0, j)
    return pl.pallas_call(
        functools.partial(widen_kernel, grid_side, boxes),
        grid=(out // tile,),
        in_specs=[
            whole((rows, width_in)),
            whole((rows, mid)),
            pl.BlockSpec((width_in, tile), column),
            pl.BlockSpec((mid, tile), column),
            pl.BlockSpec((4, tile), column),
        ],
        out_specs=[
            pl.BlockSpec((rows, tile), column),
            pl.BlockSpec((rows, tile), column),
            pl.BlockSpec((2, tile), column),
            pl.BlockSpec((boxes, tile), column),
        ],
        out_shape=[
            jax.ShapeDtypeStruct((rows, out), BF16),
            jax.ShapeDtypeStruct((rows, out), BF16),
            jax.ShapeDtypeStruct((2, out), F32),
            jax.ShapeDtypeStruct((boxes, out), F32),
        ],
        scratch_shapes=[pltpu.VMEM((rows, tile), F32)] * 2,
        compiler_params=params(),
        name="widen",
    )(roi, middle, ws, we, affine)


def silu_parts(x, gain, shift):
    h = x * gain + shift
    t = jnp.tanh(h)
    return (1.0 + t) * (1.0 + h * (1.0 - t))


def narrow_kernel(
    grid_side, boxes, order, roi, middle, xe, xp, we, inv, affine, dfeature, before,
    away, keep, dprojected, dmiddle, sums, upstream, dexpanded,
):
    j = pl.program_id(0)
    rows, width = upstream.shape
    gain_e, gain_p = affine[0:1, :], affine[2:3, :]
    shift = 0.5 * (affine[1:2, :] + affine[3:4, :])
    half_e, half_p = 0.5 * gain_e, 0.5 * gain_p
    slope_scale = dfeature[...] * (0.5 / (grid_side * grid_side))

    def fold(values):
        return jnp.sum(values.reshape(boxes // 8, 8, width), axis=0)

    def first(k, carry):
        total, total_e, total_p = carry
        for w in range(grid_side):
            at = pl.ds((k * grid_side + w) * boxes, boxes)
            e, p = xe[at, :].astype(F32), xp[at, :].astype(F32)
            h = e * half_e + p * half_p + shift
            t = jnp.tanh(h)
            u = (1.0 + t) * (1.0 + h * (1.0 - t)) * slope_scale
            upstream[at, :] = u
            total = total + fold(u)
            total_e = total_e + fold(u * e)
            total_p = total_p + fold(u * p)
        return total, total_e, total_p

    zero = jnp.zeros((8, width), F32)
    total, total_e, total_p = [
        jnp.sum(v, axis=0, keepdims=True)
        for v in lax.fori_loop(0, grid_side, first, (zero, zero, zero))
    ]
    sums[0:1, :] = total_e
    sums[1:2, :] = total
    sums[2:3, :] = total_p
    scale_e, scale_p = inv[0:1, :] * gain_e, inv[1:2, :] * gain_p
    mean, mean_e, mean_p = total / rows, total_e / rows, total_p / rows

    def second(k, carry):
        for w in range(grid_side):
            at = pl.ds((k * grid_side + w) * boxes, boxes)
            centred = upstream[at, :] - mean
            e, p = xe[at, :].astype(F32), xp[at, :].astype(F32)
            dexpanded[at, :] = (scale_e * (centred - e * mean_e)).astype(BF16)
            dprojected[at, :] = (scale_p * (centred - p * mean_p)).astype(BF16)
        return carry

    lax.fori_loop(0, grid_side, second, 0)
    over_rows = (((0,), (0,)), ((), ()))
    shortcut_part = lax.dot_general(roi[...], dprojected[...], over_rows, preferred_element_type=F32)
    expand_part = lax.dot_general(middle[...], dexpanded[...], over_rows, preferred_element_type=F32)
    back = lax.dot_general(
        dexpanded[...], we[...], (((1,), (1,)), ((), ())), preferred_element_type=F32
    )
    split = roi.shape[1]

    @pl.when(j == 0)
    def _():
        away[0:split, :] = shortcut_part.astype(BF16)
        away[split:, :] = expand_part.astype(BF16)
        dmiddle[...] = before[...] + back

    @pl.when(j == 1)
    def _():
        keep[0:split, :] = shortcut_part.astype(BF16)
        keep[split:, :] = expand_part.astype(BF16)
        dmiddle[...] += back


def narrow(order, roi, middle, xe, xp, we, inv, affine, dfeature, before, grid_side, boxes):
    rows, width_in = roi.shape
    mid, out = we.shape
    tile = out // 4
    column = lambda j, order: (0, order[j])
    local = lambda j, order: (0, j)
    return pl.pallas_call(
        functools.partial(narrow_kernel, grid_side, boxes),
        grid_spec=pltpu.PrefetchScalarGridSpec(
            num_scalar_prefetch=1,
            grid=(2,),
            in_specs=[
                whole((rows, width_in)),
                whole((rows, mid)),
                pl.BlockSpec((rows, tile), column),
                pl.BlockSpec((rows, tile), column),
                pl.BlockSpec((mid, tile), column),
                pl.BlockSpec((2, tile), column),
                pl.BlockSpec((4, tile), column),
                pl.BlockSpec((boxes, tile), column),
                whole((rows, mid)),
            ],
            out_specs=[
                whole((width_in + mid, tile)),
                whole((width_in + mid, tile)),
                pl.BlockSpec((rows, tile), local),
                whole((rows, mid)),
                pl.BlockSpec((3, tile), local),
            ],
            scratch_shapes=[pltpu.VMEM((rows, tile), F32), pltpu.VMEM((rows, tile), BF16)],
        ),
        out_shape=[
            jax.ShapeDtypeStruct((width_in + mid, tile), BF16),
            jax.ShapeDtypeStruct((width_in + mid, tile), BF16),
            jax.ShapeDtypeStruct((rows, 2 * tile), BF16),
            jax.ShapeDtypeStruct((rows, mid), F32),
            jax.ShapeDtypeStruct((3, 2 * tile), F32),
        ],
        compiler_params=params(),
        name="narrow",
    )(order, roi, middle, xe, xp, we, inv, affine, dfeature, before)


def norm_back(grid_side, boxes, upstream, x_ref, inv, affine, row, sums, store):
    rows, width = upstream.shape
    gain = affine[row : row + 1, :]
    half, shift = 0.5 * gain, 0.5 * affine[row + 1 : row + 2, :]

    def fold(values):
        return jnp.sum(values.reshape(boxes // 8, 8, width), axis=0)

    def first(k, carry):
        total, total_x = carry
        for w in range(grid_side):
            at = pl.ds((k * grid_side + w) * boxes, boxes)
            x = x_ref[at, :].astype(F32)
            u = upstream[at, :] * (0.5 * silu_parts(x, half, shift))
            upstream[at, :] = u
            total = total + fold(u)
            total_x = total_x + fold(u * x)
        return total, total_x

    zero = jnp.zeros((8, width), F32)
    total, total_x = [
        jnp.sum(v, axis=0, keepdims=True) for v in lax.fori_loop(0, grid_side, first, (zero, zero))
    ]
    sums[0:1, :] = total_x
    sums[1:2, :] = total
    scale = inv[...] * gain
    mean, mean_x = total / rows, total_x / rows

    def second(k, carry):
        for w in range(grid_side):
            at = pl.ds((k * grid_side + w) * boxes, boxes)
            x = x_ref[at, :].astype(F32)
            store(k, w, at, (scale * (upstream[at, :] - mean - x * mean_x)).astype(BF16))
        return carry

    lax.fori_loop(0, grid_side, second, 0)


def spatial_back_kernel(
    grid_side, boxes, place, dmiddle, x2, inv2, affine, hidden,
    away_far, keep_far, away_near, keep_near, dconv, sums, upstream, dflat, part,
):
    cells = grid_side * grid_side
    width = upstream.shape[1]
    side = grid_side + 2
    zeros = jnp.zeros((boxes, width), BF16)
    for k in range(side):
        dconv[0, k] = zeros
        dconv[side - 1, k] = zeros
        dconv[k, 0] = zeros
        dconv[k, side - 1] = zeros
    upstream[...] = dmiddle[...]

    def store(k, w, at, value):
        dconv[k + 1, w + 1] = value
        dflat[at, :] = value

    norm_back(grid_side, boxes, upstream, x2, inv2, affine, 2, sums, store)
    half, quarter = width // 2, width // 4
    for far, away, keep in ((1, away_far, keep_far), (0, away_near, keep_near)):
        start = pl.multiple_of((place[0] ^ far) * half, half)
        columns = dflat[:, pl.ds(start, half)]
        for p in range(3):
            for q in range(3):
                window = hidden[p : p + grid_side, q : q + grid_side].reshape(cells * boxes, width)
                part[...] = lax.dot_general(
                    window, columns, (((0,), (0,)), ((), ())), preferred_element_type=F32
                ).astype(BF16)
                mine = pl.multiple_of(place[1] * quarter, quarter)
                other = pl.multiple_of((1 - place[1]) * quarter, quarter)
                keep[p * 3 + q] = part[:, pl.ds(mine, quarter)]
                away[p * 3 + q] = part[:, pl.ds(other, quarter)]


def spatial_back(place, dmiddle, x2, inv2, affine, hidden, grid_side, boxes):
    rows, mid = dmiddle.shape
    side = grid_side + 2
    vm = pl.BlockSpec(memory_space=pltpu.VMEM)
    part = jax.ShapeDtypeStruct((9, mid, mid // 4), BF16)
    return pl.pallas_call(
        functools.partial(spatial_back_kernel, grid_side, boxes),
        in_specs=[pl.BlockSpec(memory_space=pltpu.SMEM)] + [vm] * 5,
        out_specs=[vm] * 6,
        out_shape=[part] * 4
        + [
            jax.ShapeDtypeStruct((side, side, boxes, mid), BF16),
            jax.ShapeDtypeStruct((2, mid), F32),
        ],
        scratch_shapes=[
            pltpu.VMEM((rows, mid), F32),
            pltpu.VMEM((rows, mid), BF16),
            pltpu.VMEM((mid, mid // 2), BF16),
        ],
        compiler_params=params(),
        name="spatial_back",
    )(place, dmiddle, x2, inv2, affine, hidden)


def reduce_back_kernel(grid_side, boxes, dconv, w9, x1, inv1, affine, roi, dreduced, weight, sums, upstream):
    cells = grid_side * grid_side
    width = upstream.shape[1]
    for p in range(3):
        for q in range(3):
            window = dconv[2 - p : 2 - p + grid_side, 2 - q : 2 - q + grid_side].reshape(cells * boxes, width)
            product = lax.dot_general(
                window, w9[p * 3 + q], (((1,), (1,)), ((), ())), preferred_element_type=F32
            )
            if p + q == 0:
                upstream[...] = product
            else:
                upstream[...] += product

    def store(k, w, at, value):
        dreduced[at, :] = value

    norm_back(grid_side, boxes, upstream, x1, inv1, affine, 0, sums, store)
    weight[...] = lax.dot_general(
        dreduced[...], roi[...], (((0,), (0,)), ((), ())), preferred_element_type=F32
    ).astype(BF16)


def reduce_back(dconv, w9, x1, inv1, affine, roi, grid_side, boxes):
    rows, width_in = roi.shape
    mid = w9.shape[1]
    vm = pl.BlockSpec(memory_space=pltpu.VMEM)
    return pl.pallas_call(
        functools.partial(reduce_back_kernel, grid_side, boxes),
        in_specs=[vm] * 6,
        out_specs=[vm] * 3,
        out_shape=[
            jax.ShapeDtypeStruct((rows, mid), BF16),
            jax.ShapeDtypeStruct((mid, width_in), BF16),
            jax.ShapeDtypeStruct((2, mid), F32),
        ],
        scratch_shapes=[pltpu.VMEM((rows, mid), F32)],
        compiler_params=params(),
        name="reduce_back",
    )(dconv, w9, x1, inv1, affine, roi)


def roi_back_kernel(order, dreduced, dfar, dnear, wr, ws_a, ws_b, ws_c, ws_d, out):
    tile = ws_a.shape[1]
    nt = lambda a, b: lax.dot_general(a, b, (((1,), (1,)), ((), ())), preferred_element_type=F32)
    total = nt(dreduced[...], wr[...])
    total += nt(dfar[:, :tile], ws_a[...])
    total += nt(dfar[:, tile:], ws_b[...])
    total += nt(dnear[:, :tile], ws_c[...])
    total += nt(dnear[:, tile:], ws_d[...])
    out[...] = total.astype(BF16)


def roi_back(order, dreduced, dfar, dnear, wr, ws):
    rows, mid = dreduced.shape
    width_in, out = ws.shape
    tile, block = out // 4, width_in // 2
    return pl.pallas_call(
        roi_back_kernel,
        grid_spec=pltpu.PrefetchScalarGridSpec(
            num_scalar_prefetch=1,
            grid=(width_in // block,),
            in_specs=[
                whole((rows, mid)),
                whole((rows, 2 * tile)),
                whole((rows, 2 * tile)),
                pl.BlockSpec((block, mid), lambda j, order: (j, 0)),
            ]
            + [pl.BlockSpec((block, tile), lambda j, order, s=s: (j, order[s])) for s in range(4)],
            out_specs=pl.BlockSpec((rows, block), lambda j, order: (0, j)),
        ),
        out_shape=jax.ShapeDtypeStruct((rows, width_in), BF16),
        compiler_params=params(),
        name="roi_back",
    )(order, dreduced, dfar, dnear, wr, ws, ws, ws, ws)


def head_kernel(
    scale, feature, window, paired, wq, wo, wc, norm_gain, norm_shift, out_bias, class_bias, cotangent,
    logits, dfeature, dwindow, low, combined_low, dbranch, narrow_pack, norm_sums, wide_sums, class_sums,
):
    att = wq.shape[1]
    boxes, out = feature.shape
    dot = lambda a, b: jnp.dot(a, b, preferred_element_type=F32)
    nt = lambda a, b: lax.dot_general(a, b, (((1,), (1,)), ((), ())), preferred_element_type=F32)
    tn = lambda a, b: lax.dot_general(a, b, (((0,), (0,)), ((), ())), preferred_element_type=F32)
    feature_low = feature[...].astype(BF16)
    low[...] = feature_low
    queries = dot(feature_low, wq[...]).astype(BF16)
    keys, values = window[:, :att], window[:, att:]
    live = paired[...] > 0.0
    scores = nt(queries, keys) * scale
    top = jnp.max(jnp.where(live, scores, -1e30), axis=1, keepdims=True)
    exps = jnp.where(live, jnp.exp(jnp.where(live, scores - top, 0.0)), 0.0)
    probs = exps / jnp.sum(exps, axis=1, keepdims=True)
    probs_low = probs.astype(BF16)
    pre = dot(probs_low, values) + queries.astype(F32)
    centred = pre - jnp.mean(pre, axis=1, keepdims=True)
    inv = lax.rsqrt(jnp.mean(centred * centred, axis=1, keepdims=True) + EPSILON)
    x = centred * inv
    gain = norm_gain[...]
    h = 0.5 * (x * gain + norm_shift[...])
    t = jnp.tanh(h)
    activated = (h + h * t).astype(BF16)
    combined = feature[...] + dot(activated, wo[...]) + out_bias[...]
    comb_low = combined.astype(BF16)
    combined_low[...] = comb_low
    logits[...] = nt(feature_low, wc[:, :out]) + nt(comb_low, wc[:, out:]) + class_bias[...]
    g = cotangent[...].astype(BF16)
    class_sums[...] = jnp.sum(g.astype(F32), axis=0, keepdims=True)
    first = dot(g, wc[:, :out])
    second = dot(g, wc[:, out:])
    gb = second.astype(BF16)
    dbranch[...] = gb
    wide_sums[...] = jnp.sum(gb.astype(F32), axis=0, keepdims=True)
    u = nt(gb, wo[...]) * (0.5 * (1.0 + t) * (1.0 + h * (1.0 - t)))
    norm_sums[0:1, :] = jnp.sum(u * x, axis=0, keepdims=True)
    norm_sums[1:2, :] = jnp.sum(u, axis=0, keepdims=True)
    e = u * gain
    dpre = inv * (e - jnp.mean(e, axis=1, keepdims=True) - x * jnp.mean(e * x, axis=1, keepdims=True))
    da = dpre.astype(BF16)
    dprobs = nt(da, values)
    delta = jnp.sum(probs * dprobs, axis=1, keepdims=True)
    ds = (probs * (dprobs - delta)).astype(BF16)
    dq = (dot(ds, keys) * scale + dpre).astype(BF16)
    dwindow[:, :att] = (tn(ds, queries) * scale).astype(BF16)
    dwindow[:, att:] = tn(probs_low, da).astype(BF16)
    narrow_pack[:, :att] = dq
    narrow_pack[:, att : 2 * att] = activated
    narrow_pack[:, 2 * att :] = jnp.zeros((boxes, narrow_pack.shape[1] - 2 * att), BF16)
    narrow_pack[:, 2 * att : 2 * att + g.shape[1]] = g
    dfeature[...] = first + second + nt(dq, wq[...])


def head(feature, window, paired, wq, wo, wc, norm_gain, norm_shift, out_bias, class_bias, cotangent):
    boxes, out = feature.shape
    att = wq.shape[1]
    classes = wc.shape[0]
    span = window.shape[0]
    vm = pl.BlockSpec(memory_space=pltpu.VMEM)
    shapes = [
        ((boxes, classes), F32),
        ((boxes, out), F32),
        ((span, 2 * att), BF16),
        ((boxes, out), BF16),
        ((boxes, out), BF16),
        ((boxes, out), BF16),
        ((boxes, 2 * att + 128), BF16),
        ((2, att), F32),
        ((1, out), F32),
        ((1, classes), F32),
    ]
    return pl.pallas_call(
        functools.partial(head_kernel, att ** (-0.5)),
        in_specs=[vm] * 11,
        out_specs=[vm] * len(shapes),
        out_shape=[jax.ShapeDtypeStruct(s, d) for s, d in shapes],
        compiler_params=params(),
        name="head",
    )(feature, window, paired, wq, wo, wc, norm_gain, norm_shift, out_bias, class_bias, cotangent)


def small_weights_kernel(quarter, low, combined, dbranch, pack, bank, dbank, out):
    att = dbank.shape[1] // 2
    width = out.shape[1]
    piece = att // 4
    tn = lambda a, b: lax.dot_general(a, b, (((0,), (0,)), ((), ())), preferred_element_type=F32).astype(BF16)
    q = quarter[0]
    at = pl.ds(pl.multiple_of(q * piece, piece), piece)
    blocks = low.shape[1] // width
    row = 0
    for left, right in (
        (pack[:, at], low),
        (dbank[:, at], bank),
        (dbank[:, pl.ds(pl.multiple_of(att + q * piece, piece), piece)], bank),
    ):
        product = tn(left, right[...])
        for k in range(blocks):
            out[row : row + piece, :] = product[:, k * width : (k + 1) * width]
            row += piece
    wide = dbranch.shape[1] // 4
    out[row : row + att, :] = tn(pack[:, att : 2 * att], dbranch[:, pl.ds(pl.multiple_of(q * wide, wide), wide)])
    row += att
    half = low.shape[1] // 2
    columns = pl.ds(pl.multiple_of((q % 2) * half, half), half)
    joined = jnp.where(q < 2, low[:, columns], combined[:, columns])
    product = tn(pack[:, 2 * att :], joined)
    classes = (out.shape[0] - row) // 2
    for k in range(half // width):
        out[row : row + classes, :] = product[:classes, k * width : (k + 1) * width]
        row += classes


def small_weights(quarter, low, combined, dbranch, pack, bank, dbank):
    att = dbank.shape[1] // 2
    vm = pl.BlockSpec(memory_space=pltpu.VMEM)
    return pl.pallas_call(
        small_weights_kernel,
        in_specs=[pl.BlockSpec(memory_space=pltpu.SMEM)] + [vm] * 6,
        out_specs=vm,
        out_shape=jax.ShapeDtypeStruct((4 * att + 256, 512), BF16),
        compiler_params=params(),
        name="small_weights",
    )(quarter, low, combined, dbranch, pack, bank, dbank)


def pair_swap(value, axis, bit):
    size = lax.axis_size(axis)
    return lax.ppermute(value, axis, [(i, i ^ bit) for i in range(size)])


def piece(value, index, count, axis):
    size = value.shape[axis] // count
    return lax.dynamic_slice_in_dim(value, index * size, size, axis)


def bank_total(value, axis):
    size = lax.axis_size("bank")
    index = lax.axis_index("bank")
    bits = []
    bit = 1
    while bit < size:
        bits.append(bit)
        bit *= 2
    for bit in bits:
        side = (index // bit) % 2
        sent = piece(value, 1 - side, 2, axis)
        value = piece(value, side, 2, axis) + pair_swap(sent, "bank", bit)
    for bit in reversed(bits):
        side = (index // bit) % 2
        other = pair_swap(value, "bank", bit)
        low = jnp.where(side == 0, value, other)
        high = jnp.where(side == 0, other, value)
        value = jnp.concatenate([low, high], axis=axis)
    return value


def passed_along(value, by):
    devices = lax.axis_size(("bank", "box"))
    pairs = [(i, i + by) for i in range(devices) if 0 <= i + by < devices]
    return lax.ppermute(value, ("bank", "box"), pairs)


def segment_of(seconds, video_lengths):
    video_ends = jnp.cumsum(video_lengths)
    return jnp.sum((video_ends[None, :] <= seconds[:, None]).astype(jnp.int32), axis=1)


def group_rows(value):
    pair = jnp.concatenate([value, pair_swap(value, "box", 2)], axis=0)
    return jnp.concatenate([pair, pair_swap(pair, "box", 1)], axis=0)


def local(
    roi_features,
    box_seconds,
    video_lengths,
    bank_features,
    reduce_weight,
    reduce_gain,
    reduce_shift,
    spatial_weight,
    spatial_gain,
    spatial_shift,
    expand_weight,
    expand_gain,
    expand_shift,
    shortcut_weight,
    shortcut_gain,
    shortcut_shift,
    query_weight,
    key_weight,
    value_weight,
    norm_gain,
    norm_shift,
    output_weight,
    output_bias,
    class_weight,
    class_bias,
    logit_cotangent,
):
    boxes, grid_side = roi_features.shape[:2]
    in_width = roi_features.shape[3]
    rows = boxes * grid_side * grid_side
    mid = reduce_weight.shape[1]
    out = expand_weight.shape[1]
    att = query_weight.shape[1]
    classes = class_weight.shape[1]
    bank_rows = bank_features.shape[0]
    bank_total_seconds = lax.axis_size(("bank", "box")) * SEC_DEV
    my_index = lax.axis_index(("bank", "box"))
    box_index = lax.axis_index("box")
    core, far_side = box_index % 2, box_index // 2
    wide = lambda *vectors: jnp.stack([v.astype(F32) for v in vectors])

    roi = roi_features.transpose(1, 2, 0, 3).reshape(rows, in_width)
    w9 = spatial_weight.reshape(9, mid, mid)
    mid_affine = wide(reduce_gain, reduce_shift, spatial_gain, spatial_shift)
    out_affine = wide(expand_gain, expand_shift, shortcut_gain, shortcut_shift)

    own_window = jnp.concatenate(
        [
            jnp.dot(bank_features, key_weight, preferred_element_type=F32).astype(BF16),
            jnp.dot(bank_features, value_weight, preferred_element_type=F32).astype(BF16),
        ],
        axis=1,
    )
    window = jnp.concatenate(
        [own_window if by == 0 else passed_along(own_window, -by) for by in range(-REACH, REACH + 1)]
    )
    group_bank = group_rows(bank_features)
    span = (2 * REACH + 1) * bank_rows
    window_seconds = (my_index - REACH) * SEC_DEV + jnp.arange(span, dtype=jnp.int32) // PER_SEC
    inside = (window_seconds >= 0) & (window_seconds < bank_total_seconds)
    paired = (
        inside[None, :]
        & (segment_of(box_seconds, video_lengths)[:, None] == segment_of(window_seconds, video_lengths)[None, :])
        & (jnp.abs(box_seconds[:, None] - window_seconds[None, :]) <= HALF)
    ).astype(F32)

    x1, inv1, hidden, x2, inv2, middle = trunk(roi, reduce_weight, w9, mid_affine, grid_side, boxes)
    xe, xp, inv_out, feature = widen(roi, middle, shortcut_weight, expand_weight, out_affine, grid_side, boxes)
    (
        logits, dfeature, dwindow, feature_low, combined_low, dbranch, pack, norm_sums, wide_sums, class_sums,
    ) = head(
        feature, window, paired, query_weight, output_weight, class_weight.T,
        norm_gain.astype(F32)[None], norm_shift.astype(F32)[None], output_bias.astype(F32)[None],
        class_bias.astype(F32)[None], logit_cotangent,
    )

    dbank = None
    for by in range(-REACH, REACH + 1):
        part = dwindow[(by + REACH) * bank_rows : (by + REACH + 1) * bank_rows]
        part = (part if by == 0 else passed_along(part, by)).astype(F32)
        dbank = part if dbank is None else dbank + part
    small = small_weights(
        box_index.reshape(1), group_rows(feature_low), group_rows(combined_low), group_rows(dbranch),
        group_rows(pack), group_bank, group_rows(dbank.astype(BF16)),
    )
    small = bank_total(small, 0)

    far_order = jnp.stack([(1 - far_side) * 2 + 1 - core, (1 - far_side) * 2 + core])
    near_order = jnp.stack([far_side * 2 + 1 - core, far_side * 2 + core])
    shared = (roi, middle, xe, xp, expand_weight, inv_out, out_affine, dfeature)
    away_far, keep_far, dfar, dmiddle, sums_far = narrow(
        far_order, *shared, jnp.zeros((rows, mid), F32), grid_side, boxes
    )
    away_near, keep_near, dnear, dmiddle, sums_near = narrow(near_order, *shared, dmiddle, grid_side, boxes)
    wide_total = pair_total(away_far, keep_far, away_near, keep_near)
    wide_total = bank_total(wide_total, 0)

    place = jnp.stack([far_side, core])
    *spatial_parts, dconv, spatial_sums = spatial_back(
        place, dmiddle, x2, inv2, mid_affine, hidden, grid_side, boxes
    )
    spatial_total = bank_total(pair_total(*[v.reshape(9 * mid, mid // 4) for v in spatial_parts]), 0)

    dreduced, reduce_part, reduce_sums = reduce_back(dconv, w9, x1, inv1, mid_affine, roi, grid_side, boxes)
    orders = jnp.concatenate([far_order, near_order])
    tile = out // 4
    expand_sums = jnp.concatenate([sums_far, sums_near], axis=1).reshape(3, 4, tile)

    def last_parts(k):
        q = orders[k]
        vectors = [piece(v, q, 4, 1).reshape(-1) for v in (reduce_sums, spatial_sums, norm_sums, wide_sums)]
        vectors += [expand_sums[:, k].reshape(-1), class_sums.reshape(-1)]
        flat = jnp.concatenate(vectors)
        tail = jnp.pad(flat, (0, 16 * in_width - flat.shape[0])).reshape(16, in_width)
        return jnp.concatenate([piece(reduce_part, q, 4, 0), tail.astype(BF16)])

    last_total = bank_total(pair_total(*[last_parts(k) for k in range(4)]), 1)
    roi_gradient = roi_back(orders, dreduced, dfar, dnear, reduce_weight, shortcut_weight)
    roi_gradient = roi_gradient.reshape(grid_side, grid_side, boxes, in_width).transpose(2, 0, 1, 3)

    quarter = mid // 4
    vectors = last_total[quarter:].astype(F32).reshape(-1)
    taken = 0
    got = []
    for size in [quarter] * 6 + [tile] * 4 + [classes]:
        got.append(vectors[taken : taken + size])
        taken += size
    reduce_gain_g, reduce_shift_g, spatial_gain_g, spatial_shift_g, norm_gain_g, norm_shift_g = got[:6]
    bias_g, expand_gain_g, expand_shift_g, shortcut_gain_g, class_bias_g = got[6:]
    small = small.astype(F32)
    stacked = [
        small[k * att : (k + 1) * att].reshape(4, att // 4, att).transpose(0, 2, 1).reshape(out, att // 4)
        for k in range(3)
    ]
    class_rows = (small.shape[0] - 4 * att) // 2
    class_g = (
        small[4 * att :].reshape(2, class_rows, att)[:, :classes].transpose(0, 2, 1).reshape(2 * att, classes)
    )
    wide_total = wide_total.astype(F32)
    return (
        logits,
        roi_gradient,
        last_total[:quarter].astype(F32).T,
        reduce_gain_g,
        reduce_shift_g,
        spatial_total.astype(F32).reshape(3, 3, mid, quarter),
        spatial_gain_g,
        spatial_shift_g,
        wide_total[in_width:],
        expand_gain_g,
        expand_shift_g,
        wide_total[:in_width],
        shortcut_gain_g,
        expand_shift_g,
        stacked[0],
        stacked[1],
        stacked[2],
        norm_gain_g,
        norm_shift_g,
        small[3 * att : 4 * att],
        bias_g,
        class_g,
        class_bias_g,
    )


def pair_total(away_far, keep_far, away_near, keep_near):
    far = keep_far + pair_swap(away_far, "box", 1)
    near = keep_near + pair_swap(away_near, "box", 1)
    return near + pair_swap(far, "box", 2)


def solution(mesh):
    split = ("bank", "box")
    in_specs = (P(split), P(split), P(), P(split)) + (P(),) * 21 + (P(split),)
    column, vector = P(None, "box"), P("box")
    out_specs = (
        P(split),
        P(split),
        column,
        vector,
        vector,
        P(None, None, None, "box"),
        vector,
        vector,
        column,
        vector,
        vector,
        column,
        vector,
        vector,
        column,
        column,
        column,
        vector,
        vector,
        column,
        vector,
        P("box", None),
        P(),
    )
    return jax.shard_map(local, mesh=mesh, in_specs=in_specs, out_specs=out_specs, check_vma=False)
```

```python
import functools
import jax
import jax.numpy as jnp
from jax import lax
from jax.experimental import pallas as pl
from jax.experimental.pallas import tpu as pltpu
from jax.sharding import PartitionSpec as P

HALF = 30
PER_SEC = 8
SEC_DEV = 16
REACH = 2
EPSILON = 1e-05
MIB = 2**20
F32, BF16 = jnp.float32, jnp.bfloat16
ON_CHIP = pl.BlockSpec(memory_space=pltpu.VMEM)
SCALARS = pl.BlockSpec(memory_space=pltpu.SMEM)
FAR = pl.BlockSpec(memory_space=pl.ANY)
OVER_ROWS = (((0,), (0,)), ((), ()))
OVER_COLUMNS = (((1,), (1,)), ((), ()))


def plain(a, b):
    return jnp.dot(a, b, preferred_element_type=F32)


def over_rows(a, b):
    return lax.dot_general(a, b, OVER_ROWS, preferred_element_type=F32)


def over_columns(a, b):
    return lax.dot_general(a, b, OVER_COLUMNS, preferred_element_type=F32)


def params(mebibytes):
    return pltpu.CompilerParams(vmem_limit_bytes=mebibytes * MIB)


def lasting(microseconds):
    return pl.CostEstimate(
        flops=int(microseconds * 1.1e9), bytes_accessed=int(microseconds * 3.0e6), transcendentals=0
    )


def kept(*arrays):
    return [pltpu.with_memory_space_constraint(v, pltpu.VMEM) for v in arrays]


def outside(*arrays):
    return [pltpu.with_memory_space_constraint(v, pltpu.HBM) for v in arrays]


def start_copies(pairs, sems):
    copies = [pltpu.make_async_copy(source, target, sems.at[k]) for k, (source, target) in enumerate(pairs)]
    for copy in copies:
        copy.start()
    return copies


def column_stats(acc, grid_side):
    rows, width = acc.shape
    step = rows // grid_side

    def fold(values):
        return jnp.sum(values.reshape(step // 8, 8, width), axis=0)

    shift = jnp.sum(fold(acc[0:step, :]), axis=0, keepdims=True) / step

    def add(k, carry):
        total, square = carry
        centred = acc[pl.ds(k * step, step), :] - shift
        return total + fold(centred), square + fold(centred * centred)

    zero = jnp.zeros((8, width), F32)
    total, square = lax.fori_loop(0, grid_side, add, (zero, zero))
    offset = jnp.sum(total, axis=0, keepdims=True) / rows
    var = jnp.sum(square, axis=0, keepdims=True) / rows - offset * offset
    return shift + offset, lax.rsqrt(var + EPSILON)


def clear_border(padded):
    side, _, boxes, width = padded.shape
    zeros = jnp.zeros((boxes, width), BF16)
    for k in range(side):
        padded[0, k] = zeros
        padded[side - 1, k] = zeros
        padded[k, 0] = zeros
        padded[k, side - 1] = zeros


def by_cells(grid_side, boxes, body, carry):
    def line(k, carry):
        for w in range(grid_side):
            carry = body(k, w, pl.ds((k * grid_side + w) * boxes, boxes), carry)
        return carry

    return lax.fori_loop(0, grid_side, line, carry)


def trunk_kernel(
    grid_side, boxes, roi_far, wr_far, w9_far, bank_far, kw_far, vw_far, vectors,
    roi, x1, hidden, x2, middle, inv, window, wr, w9, bank, kw, vw, acc, sems,
):
    width = acc.shape[1]
    copies = start_copies(
        [(roi_far, roi), (wr_far, wr), (w9_far, w9), (bank_far, bank), (kw_far, kw), (vw_far, vw)], sems
    )
    clear_border(hidden)
    gain1, shift1, gain2, shift2 = [0.5 * vectors[k : k + 1, :] for k in range(4)]
    copies[0].wait()
    copies[1].wait()
    acc[...] = plain(roi[...], wr[...])
    mean, inv1 = column_stats(acc, grid_side)
    inv[0:1, :] = inv1

    def first(k, w, rows, carry):
        x = (acc[rows, :] - mean) * inv1
        x1[rows, :] = x.astype(BF16)
        h = x * gain1 + shift1
        hidden[k + 1, w + 1] = (h + h * jnp.tanh(h)).astype(BF16)
        return carry

    by_cells(grid_side, boxes, first, 0)
    copies[2].wait()
    for p in range(3):
        for q in range(3):
            taps = hidden[p : p + grid_side, q : q + grid_side].reshape(acc.shape)
            product = plain(taps, w9[p * 3 + q])
            if p + q == 0:
                acc[...] = product
            else:
                acc[...] += product
    mean2, inv2 = column_stats(acc, grid_side)
    inv[1:2, :] = inv2

    def second(k, w, rows, carry):
        x = (acc[rows, :] - mean2) * inv2
        x2[rows, :] = x.astype(BF16)
        h = x * gain2 + shift2
        middle[rows, :] = (h + h * jnp.tanh(h)).astype(BF16)
        return carry

    by_cells(grid_side, boxes, second, 0)
    for copy in copies[3:]:
        copy.wait()
    att = kw.shape[1]
    window[:, :att] = plain(bank[...], kw[...]).astype(BF16)
    window[:, att:] = plain(bank[...], vw[...]).astype(BF16)


def trunk(roi, wr, w9, bank, kw, vw, vectors, grid_side, boxes):
    rows, mid = roi.shape[0], wr.shape[1]
    side = grid_side + 2
    return pl.pallas_call(
        functools.partial(trunk_kernel, grid_side, boxes),
        in_specs=[FAR] * 6 + [ON_CHIP],
        out_specs=[ON_CHIP] * 7,
        out_shape=[
            pltpu.VMEM(roi.shape, BF16),
            pltpu.VMEM((rows, mid), BF16),
            pltpu.VMEM((side, side, boxes, mid), BF16),
            pltpu.VMEM((rows, mid), BF16),
            pltpu.VMEM((rows, mid), BF16),
            jax.ShapeDtypeStruct((2, mid), F32),
            jax.ShapeDtypeStruct((bank.shape[0], 2 * kw.shape[1]), BF16),
        ],
        scratch_shapes=[pltpu.VMEM(v.shape, BF16) for v in (wr, w9, bank, kw, vw)]
        + [pltpu.VMEM((rows, mid), F32), pltpu.SemaphoreType.DMA((6,))],
        compiler_params=params(18),
        cost_estimate=lasting(17),
        name="trunk",
    )(*outside(roi, wr, w9, bank, kw, vw), vectors)


def widen_kernel(grid_side, boxes, order, roi, middle, ws_far, we_far, vectors, *rest):
    xs, (inv, feature, ws, we, acc_e, acc_p, sems) = rest[:8], rest[8:]
    width = acc_e.shape[1]
    at = [pl.ds(pl.multiple_of(order[k] * width, width), width) for k in range(4)]
    copies = start_copies(
        [pair for k in range(4) for pair in ((ws_far.at[:, at[k]], ws.at[k]), (we_far.at[:, at[k]], we.at[k]))],
        sems,
    )
    for k in range(4):
        xe, xp = xs[2 * k], xs[2 * k + 1]
        copies[2 * k].wait()
        acc_p[...] = plain(roi[...], ws[k])
        copies[2 * k + 1].wait()
        acc_e[...] = plain(middle[...], we[k])
        mean_e, inv_e = column_stats(acc_e, grid_side)
        mean_p, inv_p = column_stats(acc_p, grid_side)
        inv[k, 0:1, :] = inv_e
        inv[k, 1:2, :] = inv_p
        gain_e, gain_p = 0.5 * vectors[0:1, at[k]], 0.5 * vectors[2:3, at[k]]
        bias = 0.5 * (vectors[1:2, at[k]] + vectors[3:4, at[k]])

        def cell(row, w, rows, total):
            e = (acc_e[rows, :] - mean_e) * inv_e
            p = (acc_p[rows, :] - mean_p) * inv_p
            xe[rows, :] = e.astype(BF16)
            xp[rows, :] = p.astype(BF16)
            h = e * gain_e + p * gain_p + bias
            return total + (h + h * jnp.tanh(h))

        total = by_cells(grid_side, boxes, cell, jnp.zeros((boxes, width), F32))
        feature[:, at[k]] = total / (grid_side * grid_side)


def widen(order, roi, middle, ws, we, vectors, grid_side, boxes):
    rows, width_in = roi.shape
    mid, out = we.shape
    tile = out // 4
    return pl.pallas_call(
        functools.partial(widen_kernel, grid_side, boxes),
        in_specs=[SCALARS, ON_CHIP, ON_CHIP, FAR, FAR, ON_CHIP],
        out_specs=[ON_CHIP] * 10,
        out_shape=[pltpu.VMEM((rows, tile), BF16)] * 8
        + [jax.ShapeDtypeStruct((4, 2, tile), F32), jax.ShapeDtypeStruct((boxes, out), F32)],
        scratch_shapes=[
            pltpu.VMEM((4, width_in, tile), BF16),
            pltpu.VMEM((4, mid, tile), BF16),
            pltpu.VMEM((rows, tile), F32),
            pltpu.VMEM((rows, tile), F32),
            pltpu.SemaphoreType.DMA((8,)),
        ],
        compiler_params=params(18),
        cost_estimate=lasting(20),
        name="widen",
    )(order, *kept(roi, middle), *outside(ws, we), vectors)


def doubled_slope(h):
    t = jnp.tanh(h)
    return (1.0 + t) * (1.0 + h * (1.0 - t))


def narrow_kernel(
    grid_side, boxes, k, order, roi, middle, xe, xp, we_far, inv, vectors, dfeature, *rest
):
    *before, part, dprojected, dmiddle, sums, we, upstream, dexpanded, sems = rest
    rows, width = upstream.shape
    columns = pl.ds(pl.multiple_of(order[k] * width, width), width)
    copies = start_copies([(we_far.at[:, columns], we)], sems)
    gain_e, gain_p = vectors[0:1, columns], vectors[2:3, columns]
    half_e, half_p = 0.5 * gain_e, 0.5 * gain_p
    bias = 0.5 * (vectors[1:2, columns] + vectors[3:4, columns])
    slope_scale = dfeature[:, columns] * (0.5 / (grid_side * grid_side))

    def fold(values):
        return jnp.sum(values.reshape(boxes // 8, 8, width), axis=0)

    def first(row, w, at, carry):
        total, total_e, total_p = carry
        e, p = xe[at, :].astype(F32), xp[at, :].astype(F32)
        u = doubled_slope(e * half_e + p * half_p + bias) * slope_scale
        upstream[at, :] = u
        return total + fold(u), total_e + fold(u * e), total_p + fold(u * p)

    zero = jnp.zeros((8, width), F32)
    total, total_e, total_p = [
        jnp.sum(v, axis=0, keepdims=True) for v in by_cells(grid_side, boxes, first, (zero, zero, zero))
    ]
    sums[0:1, :] = total_e
    sums[1:2, :] = total
    sums[2:3, :] = total_p
    scale_e, scale_p = inv[k, 0:1, :] * gain_e, inv[k, 1:2, :] * gain_p
    mean, mean_e, mean_p = total / rows, total_e / rows, total_p / rows

    def second(row, w, at, carry):
        centred = upstream[at, :] - mean
        e, p = xe[at, :].astype(F32), xp[at, :].astype(F32)
        dexpanded[at, :] = (scale_e * (centred - e * mean_e)).astype(BF16)
        dprojected[at, :] = (scale_p * (centred - p * mean_p)).astype(BF16)
        return carry

    by_cells(grid_side, boxes, second, 0)
    split = roi.shape[1]
    part[0:split, :] = over_rows(roi[...], dprojected[...]).astype(BF16)
    part[split:, :] = over_rows(middle[...], dexpanded[...]).astype(BF16)
    copies[0].wait()
    back = over_columns(dexpanded[...], we[...])
    dmiddle[...] = before[0][...] + back if before else back


def narrow(order, roi, middle, xe, xp, we, inv, vectors, dfeature, *before, k, grid_side, boxes):
    rows, width_in = roi.shape
    mid, out = we.shape
    tile = out // 4
    return pl.pallas_call(
        functools.partial(narrow_kernel, grid_side, boxes, k),
        in_specs=[SCALARS] + [ON_CHIP] * 4 + [FAR] + [ON_CHIP] * (3 + len(before)),
        out_specs=[ON_CHIP] * 4,
        out_shape=[
            jax.ShapeDtypeStruct((width_in + mid, tile), BF16),
            pltpu.VMEM((rows, tile), BF16),
            pltpu.VMEM((rows, mid), F32),
            jax.ShapeDtypeStruct((3, tile), F32),
        ],
        input_output_aliases={9: 2} if before else {},
        scratch_shapes=[
            pltpu.VMEM((mid, tile), BF16),
            pltpu.VMEM((rows, tile), F32),
            pltpu.VMEM((rows, tile), BF16),
            pltpu.SemaphoreType.DMA((1,)),
        ],
        compiler_params=params(14),
        cost_estimate=lasting(8),
        name="narrow",
    )(order, *kept(roi, middle, xe, xp), *outside(we), inv, vectors, dfeature, *kept(*before))


def norm_back(grid_side, boxes, upstream, x_ref, inv, gain, shift, sums, store):
    rows, width = upstream.shape
    half_gain, half_shift = 0.5 * gain, 0.5 * shift

    def fold(values):
        return jnp.sum(values.reshape(boxes // 8, 8, width), axis=0)

    def first(row, w, at, carry):
        total, total_x = carry
        x = x_ref[at, :].astype(F32)
        u = upstream[at, :] * (0.5 * doubled_slope(x * half_gain + half_shift))
        upstream[at, :] = u
        return total + fold(u), total_x + fold(u * x)

    zero = jnp.zeros((8, width), F32)
    total, total_x = [
        jnp.sum(v, axis=0, keepdims=True) for v in by_cells(grid_side, boxes, first, (zero, zero))
    ]
    sums[0:1, :] = total_x
    sums[1:2, :] = total
    scale = inv * gain
    mean, mean_x = total / rows, total_x / rows

    def second(row, w, at, carry):
        x = x_ref[at, :].astype(F32)
        store(row, w, at, (scale * (upstream[at, :] - mean - x * mean_x)).astype(BF16))
        return carry

    by_cells(grid_side, boxes, second, 0)


def spatial_back_kernel(
    grid_side, boxes, place, dmiddle, x2, hidden, inv, vectors, away, keep, dconv, sums, upstream, dflat, part
):
    rows, width = upstream.shape
    clear_border(dconv)
    upstream[...] = dmiddle[...]

    def store(row, w, at, value):
        dconv[row + 1, w + 1] = value
        dflat[at, :] = value

    norm_back(grid_side, boxes, upstream, x2, inv[1:2, :], vectors[2:3, :], vectors[3:4, :], sums, store)
    quarter = width // 4
    for p in range(3):
        for q in range(3):
            taps = hidden[p : p + grid_side, q : q + grid_side].reshape(rows, width)
            part[...] = over_rows(taps, dflat[...]).astype(BF16)
            for half in range(2):
                side = 1 - place[2] if half == 0 else place[2]
                mine = pl.ds(pl.multiple_of((2 * side + place[3]) * quarter, quarter), quarter)
                other = pl.ds(pl.multiple_of((2 * side + 1 - place[3]) * quarter, quarter), quarter)
                at = (half * 9 + p * 3 + q) * quarter
                for k in range(4):
                    lines, columns = slice(at, at + quarter), slice(k * quarter, (k + 1) * quarter)
                    keep[lines, columns] = part[columns, mine]
                    away[lines, columns] = part[columns, other]


def spatial_back(place, dmiddle, x2, hidden, inv, vectors, grid_side, boxes):
    rows, mid = dmiddle.shape
    side = grid_side + 2
    part = jax.ShapeDtypeStruct((2 * 9 * (mid // 4), mid), BF16)
    return pl.pallas_call(
        functools.partial(spatial_back_kernel, grid_side, boxes),
        in_specs=[SCALARS] + [ON_CHIP] * 5,
        out_specs=[ON_CHIP] * 4,
        out_shape=[part] * 2 + [pltpu.VMEM((side, side, boxes, mid), BF16), jax.ShapeDtypeStruct((2, mid), F32)],
        scratch_shapes=[
            pltpu.VMEM((rows, mid), F32),
            pltpu.VMEM((rows, mid), BF16),
            pltpu.VMEM((mid, mid), BF16),
        ],
        compiler_params=params(16),
        cost_estimate=lasting(13),
        name="spatial_back",
    )(place, *kept(dmiddle, x2, hidden), inv, vectors)


def reduce_back_kernel(
    grid_side, boxes, order, dconv, x1, roi, w9_far, inv, vectors, spatial_sums, norm_sums, bias_sums, class_sums,
    s0, s1, s2, s3, dreduced, away, keep, upstream, w9, weight, sums, sems,
):
    rows, width = upstream.shape
    copies = start_copies([(w9_far.at[k], w9.at[k]) for k in range(9)], sems)
    for p in range(3):
        for q in range(3):
            copies[p * 3 + q].wait()
            taps = dconv[2 - p : 2 - p + grid_side, 2 - q : 2 - q + grid_side].reshape(rows, width)
            product = over_columns(taps, w9[p * 3 + q])
            if p + q == 0:
                upstream[...] = product
            else:
                upstream[...] += product

    def store(row, w, at, value):
        dreduced[at, :] = value

    norm_back(grid_side, boxes, upstream, x1, inv[0:1, :], vectors[0:1, :], vectors[1:2, :], sums, store)
    weight[...] = over_rows(dreduced[...], roi[...]).astype(BF16)
    quarter, classes = width // 4, class_sums.shape[1]
    size = away.shape[0] // 2
    for k, (target, wide_sums) in enumerate(((away, s0), (keep, s1), (away, s2), (keep, s3))):
        base = (k // 2) * size
        lines = pl.ds(pl.multiple_of(order[k] * quarter, quarter), quarter)
        wide = pl.ds(pl.multiple_of(order[k] * width, width), width)
        target[base : base + quarter, :] = weight[lines, :width]
        target[base + quarter : base + 2 * quarter, :] = weight[lines, width:]
        line0 = [v[r : r + 1, lines] for v in (sums, spatial_sums) for r in range(2)]
        line1 = [norm_sums[r : r + 1, lines] for r in range(2)]
        line1 += [class_sums[...], jnp.zeros((1, width - 2 * quarter - classes), F32)]
        tail = jnp.concatenate(
            [
                jnp.concatenate(line0, axis=1),
                jnp.concatenate(line1, axis=1),
                wide_sums[...],
                bias_sums[:, wide],
                jnp.zeros((10, width), F32),
            ]
        )
        target[base + 2 * quarter : base + size, :] = tail.astype(BF16)


def reduce_back(order, dconv, x1, roi, w9, inv, vectors, *sums, grid_side, boxes):
    rows, width_in = roi.shape
    mid = w9.shape[1]
    part = jax.ShapeDtypeStruct((2 * (mid // 2 + 16), mid), BF16)
    return pl.pallas_call(
        functools.partial(reduce_back_kernel, grid_side, boxes),
        in_specs=[SCALARS] + [ON_CHIP] * 3 + [FAR] + [ON_CHIP] * 10,
        out_specs=[ON_CHIP] * 3,
        out_shape=[pltpu.VMEM((rows, mid), BF16), part, part],
        scratch_shapes=[
            pltpu.VMEM((rows, mid), F32),
            pltpu.VMEM(w9.shape, BF16),
            pltpu.VMEM((mid, width_in), BF16),
            pltpu.VMEM((2, mid), F32),
            pltpu.SemaphoreType.DMA((9,)),
        ],
        compiler_params=params(16),
        cost_estimate=lasting(13),
        name="reduce_back",
    )(order, *kept(dconv, x1, roi), *outside(w9), inv, vectors, *sums)


def roi_back_kernel(order, dreduced, d0, d1, d2, d3, wr_far, ws_far, out, wr, ws, acc, sems):
    tile = d0.shape[1]
    copies = start_copies(
        [(wr_far, wr)]
        + [(ws_far.at[:, pl.ds(pl.multiple_of(order[k] * tile, tile), tile)], ws.at[k]) for k in range(4)],
        sems,
    )
    for copy in copies:
        copy.wait()
    for start in range(0, out.shape[1], tile):
        columns = slice(start, start + tile)
        acc[...] = over_columns(dreduced[...], wr[columns, :])
        for k, d in enumerate((d0, d1, d2, d3)):
            acc[...] += over_columns(d[...], ws[k, columns, :])
        out[:, columns] = acc[...].astype(BF16)


def roi_back(order, dreduced, dprojected, wr, ws):
    rows, mid = dreduced.shape
    width_in, out = ws.shape
    return pl.pallas_call(
        roi_back_kernel,
        in_specs=[SCALARS] + [ON_CHIP] * 5 + [FAR] * 2,
        out_specs=ON_CHIP,
        out_shape=jax.ShapeDtypeStruct((rows, width_in), BF16),
        scratch_shapes=[
            pltpu.VMEM(wr.shape, BF16),
            pltpu.VMEM((4, width_in, out // 4), BF16),
            pltpu.VMEM((rows, out // 4), F32),
            pltpu.SemaphoreType.DMA((5,)),
        ],
        compiler_params=params(18),
        cost_estimate=lasting(11),
        name="roi_back",
    )(order, *kept(dreduced, *dprojected), *outside(wr, ws))


def head_kernel(
    all_seconds, place, seconds, lengths, feature, w0, w1, w2, w3, w4, wq_far, wo_far, wc_far,
    mid_vectors, vectors, class_bias, cotangent,
    logits, dfeature, dw0, dw1, dw2, dw3, dw4, pack, norm_sums, bias_sums, class_sums, window, wq, wo, wc, sems,
):
    copies = start_copies([(wq_far, wq), (wo_far, wo), (wc_far, wc)], sems)
    att = wq.shape[1]
    boxes, out = feature.shape
    classes = cotangent.shape[1]
    span = window.shape[0]
    rows = w0.shape[0]
    for k, w in enumerate((w0, w1, w2, w3, w4)):
        window[k * rows : (k + 1) * rows, :] = w[...]
    scale = att ** (-0.5)
    norm_gain, norm_shift = mid_vectors[4:5, :], mid_vectors[5:6, :]

    row_seconds = lax.broadcasted_iota(jnp.int32, (boxes, span), 1) // PER_SEC + (place[0] - REACH) * SEC_DEV
    line = lax.broadcasted_iota(jnp.int32, (boxes, 128), 0)
    box_seconds = jnp.zeros((boxes, 128), jnp.int32)
    for k in range(boxes):
        box_seconds = jnp.where(line == k, seconds[k], box_seconds)
    box_seconds = box_seconds[:, 0:1]
    live = (row_seconds >= 0) & (row_seconds < all_seconds) & (jnp.abs(box_seconds - row_seconds) <= HALF)
    end = 0
    for k in range(lengths.shape[0]):
        end = end + lengths[k]
        live = live & ((end <= row_seconds) == (end <= box_seconds))

    copies[0].wait()
    feature_low = feature[...].astype(BF16)
    pack[:, :out] = feature_low
    queries = plain(feature_low, wq[...]).astype(BF16)
    keys, values = window[:, :att], window[:, att:]
    scores = over_columns(queries, keys) * scale
    top = jnp.max(jnp.where(live, scores, -1e30), axis=1, keepdims=True)
    exps = jnp.where(live, jnp.exp(jnp.where(live, scores - top, 0.0)), 0.0)
    probs = exps / jnp.sum(exps, axis=1, keepdims=True)
    probs_low = probs.astype(BF16)
    pre = plain(probs_low, values) + queries.astype(F32)
    centred = pre - jnp.mean(pre, axis=1, keepdims=True)
    inv = lax.rsqrt(jnp.mean(centred * centred, axis=1, keepdims=True) + EPSILON)
    x = centred * inv
    h = 0.5 * (x * norm_gain + norm_shift)
    activated = (h + h * jnp.tanh(h)).astype(BF16)
    copies[1].wait()
    combined_low = (feature[...] + plain(activated, wo[...]) + vectors[4:5, :]).astype(BF16)
    pack[:, out : 2 * out] = combined_low
    copies[2].wait()
    logits[...] = over_columns(feature_low, wc[:, :out]) + over_columns(combined_low, wc[:, out:]) + class_bias[...]
    g = cotangent[...].astype(BF16)
    class_sums[...] = jnp.sum(g.astype(F32), axis=0, keepdims=True)
    first = plain(g, wc[:, :out])
    second = plain(g, wc[:, out:])
    gb = second.astype(BF16)
    pack[:, 2 * out : 3 * out] = gb
    bias_sums[...] = jnp.sum(gb.astype(F32), axis=0, keepdims=True)
    u = over_columns(gb, wo[...]) * (0.5 * doubled_slope(h))
    norm_sums[0:1, :] = jnp.sum(u * x, axis=0, keepdims=True)
    norm_sums[1:2, :] = jnp.sum(u, axis=0, keepdims=True)
    e = u * norm_gain
    dpre = inv * (e - jnp.mean(e, axis=1, keepdims=True) - x * jnp.mean(e * x, axis=1, keepdims=True))
    da = dpre.astype(BF16)
    dprobs = over_columns(da, values)
    delta = jnp.sum(probs * dprobs, axis=1, keepdims=True)
    ds = (probs * (dprobs - delta)).astype(BF16)
    dq = (plain(ds, keys) * scale + dpre).astype(BF16)
    dkeys = (over_rows(ds, queries) * scale).astype(BF16)
    dvalues = over_rows(probs_low, da).astype(BF16)
    for k, dw in enumerate((dw0, dw1, dw2, dw3, dw4)):
        dw[:, :att] = dkeys[k * rows : (k + 1) * rows, :]
        dw[:, att:] = dvalues[k * rows : (k + 1) * rows, :]
    base = 3 * out
    pack[:, base : base + att] = dq
    pack[:, base + att : base + 2 * att] = activated
    pack[:, base + 2 * att :] = jnp.zeros((boxes, pack.shape[1] - base - 2 * att), BF16)
    pack[:, base + 2 * att : base + 2 * att + classes] = g
    dfeature[...] = first + second + over_columns(dq, wq[...])


def head(place, seconds, lengths, feature, windows, wq, wo, wc, mid_vectors, vectors, class_bias, cotangent, all_seconds):
    boxes, out = feature.shape
    att = wq.shape[1]
    classes = wc.shape[0]
    span = sum(w.shape[0] for w in windows)
    shapes = [
        ((boxes, classes), F32),
        ((boxes, out), F32),
        *[((span // 5, 2 * att), BF16)] * 5,
        ((boxes, 3 * out + 2 * att + 128), BF16),
        ((2, att), F32),
        ((1, out), F32),
        ((1, classes), F32),
    ]
    return pl.pallas_call(
        functools.partial(head_kernel, all_seconds),
        in_specs=[SCALARS] * 3 + [ON_CHIP] * 6 + [FAR] * 3 + [ON_CHIP] * 4,
        out_specs=[ON_CHIP] * len(shapes),
        out_shape=[jax.ShapeDtypeStruct(s, d) for s, d in shapes],
        scratch_shapes=[
            pltpu.VMEM((span, 2 * att), BF16),
            pltpu.VMEM(wq.shape, BF16),
            pltpu.VMEM(wo.shape, BF16),
            pltpu.VMEM(wc.shape, BF16),
            pltpu.SemaphoreType.DMA((3,)),
        ],
        compiler_params=params(16),
        cost_estimate=lasting(7),
        name="head",
    )(place, seconds, lengths, feature, *windows, *outside(wq, wo, wc), mid_vectors, vectors, class_bias, cotangent)


def halves(place, bit, value, sent, kept):
    size = sent.shape[0]
    mine = place[4 + bit]
    sent[...] = value[pl.ds(pl.multiple_of((1 - mine) * size, 16), size), :]
    kept[...] = value[pl.ds(pl.multiple_of(mine * size, 16), size), :]


def small_weights_kernel(place, *rest):
    packs, banks, dbanks = rest[0:2], rest[2:6], rest[6:8]
    sent_a, kept_a, sent_b, kept_b, pack, bank, dbank, first, second = rest[8:]
    for parts, whole in ((packs, pack), (banks, bank), (dbanks, dbank)):
        size = parts[0].shape[0]
        for k, part in enumerate(parts):
            whole[k * size : (k + 1) * size, :] = part[...]
    att = dbank.shape[1] // 2
    out = bank.shape[1]
    width = first.shape[1]
    piece = att // 4
    q = place[1]
    columns = lambda base, size: pl.ds(pl.multiple_of(base + q * size, size), size)
    base = 3 * out
    for left, right, target, row in (
        (pack[:, columns(base, piece)], pack[:, :out], first, 0),
        (dbank[:, columns(0, piece)], bank[...], first, att),
        (dbank[:, columns(att, piece)], bank[...], second, 0),
    ):
        product = over_rows(left, right).astype(BF16)
        for k in range(out // width):
            target[row + k * piece : row + (k + 1) * piece, :] = product[:, k * width : (k + 1) * width]
    second[att : 2 * att, :] = over_rows(
        pack[:, base + att : base + 2 * att], pack[:, columns(2 * out, out // 4)]
    ).astype(BF16)
    product = over_rows(pack[:, base + 2 * att :], pack[:, columns(0, out // 2)]).astype(BF16)
    first[2 * att :, :] = product[:, :width]
    second[2 * att :, :] = product[:, width:]
    halves(place, 0, first, sent_a, kept_a)
    halves(place, 1, second, sent_b, kept_b)


def small_weights(place, packs, banks, dbanks):
    att = dbanks[0].shape[1] // 2
    rows = 2 * att + 128
    joined = [pltpu.VMEM((len(v) * v[0].shape[0], v[0].shape[1]), BF16) for v in (packs, banks, dbanks)]
    return pl.pallas_call(
        small_weights_kernel,
        in_specs=[SCALARS] + [ON_CHIP] * 8,
        out_specs=[ON_CHIP] * 4,
        out_shape=[jax.ShapeDtypeStruct((rows // 2, att), BF16)] * 4,
        scratch_shapes=joined + [pltpu.VMEM((rows, att), BF16)] * 2,
        compiler_params=params(16),
        cost_estimate=lasting(4),
        name="small_weights",
    )(place, *packs, *banks, *dbanks)


class Task:
    def __init__(self, run, inputs, outputs, scratch=()):
        self.run, self.inputs, self.outputs, self.scratch = run, list(inputs), list(outputs), list(scratch)


def step(place, tasks):
    counts = [(len(t.inputs), len(t.outputs), len(t.scratch)) for t in tasks]
    n_in, n_out = sum(c[0] for c in counts), sum(c[1] for c in counts)

    def kernel(place_ref, *refs):
        ins, outs, scratch = refs[:n_in], refs[n_in : n_in + n_out], refs[n_in + n_out :]
        for task, (i, o, s) in zip(tasks, counts):
            task.run(place_ref, *ins[:i], *outs[:o], *scratch[:s])
            ins, outs, scratch = ins[i:], outs[o:], scratch[s:]

    results = pl.pallas_call(
        kernel,
        in_specs=[SCALARS] + [ON_CHIP] * n_in,
        out_specs=[ON_CHIP] * n_out,
        out_shape=[jax.ShapeDtypeStruct(shape, BF16) for t in tasks for shape in t.outputs],
        scratch_shapes=[pltpu.VMEM(shape, BF16) for t in tasks for shape in t.scratch],
        compiler_params=params(16),
        cost_estimate=lasting(2),
        name="step",
    )(place, *[v for t in tasks for v in t.inputs])
    grouped = []
    for _, o, _ in counts:
        grouped.append(results[:o])
        results = results[o:]
    return grouped


def add_task(a, b):
    def run(place, x, y, total):
        total[...] = x[...] + y[...]

    return Task(run, (a, b), [a.shape])


class BankTotal:
    def __init__(self, sent, kept, bits):
        self.sent, self.kept, self.bits, self.stage = sent, kept, bits, 0

    @property
    def done(self):
        return self.stage == 6

    def moves(self):
        if self.stage < 3:
            return [(self.sent, ("bank", 1 << self.bits[self.stage]))]
        return [(self.kept, ("bank", 1 << self.bits[5 - self.stage]))]

    def arrival(self, other):
        stage, size, width = self.stage, self.kept.shape[0], self.kept.shape[1]
        if stage < 2:
            bit = self.bits[stage + 1]

            def run(place, kept, other, sent, left, total):
                total[...] = kept[...] + other[...]
                halves(place, bit, total, sent, left)

            return Task(run, (self.kept, other), [(size // 2, width)] * 2, [(size, width)])
        if stage == 2:
            return add_task(self.kept, other)
        if stage == 5:
            return None
        bit = self.bits[5 - stage]

        def run(place, mine, other, joined):
            join(place, bit, mine, other, joined)

        return Task(run, (self.kept, other), [(2 * size, width)])

    def land(self, other, results):
        if self.stage < 2:
            self.sent, self.kept = results
        elif self.stage < 5:
            (self.kept,) = results
            if self.stage == 2:
                self.kept = beyond(self.kept)
        else:
            self.other = other
        self.stage += 1


def beyond(value):
    size = lax.axis_size("bank")
    if size == 8:
        return value
    return lax.psum(value, "bank", axis_index_groups=[list(range(k, size, 8)) for k in range(8)])


def join(place, bit, mine, other, joined):
    size = mine.shape[0]
    at = place[4 + bit]
    joined[pl.ds(pl.multiple_of(at * size, 16), size), :] = mine[...]
    joined[pl.ds(pl.multiple_of((1 - at) * size, 16), size), :] = other[...]


def emit(place, run, inputs, outputs, scratch, name):
    return pl.pallas_call(
        run,
        in_specs=[SCALARS] + [ON_CHIP] * len(inputs),
        out_specs=[ON_CHIP] * len(outputs),
        out_shape=[jax.ShapeDtypeStruct(shape, F32) for shape in outputs],
        scratch_shapes=[pltpu.VMEM(shape, BF16) for shape in scratch],
        compiler_params=params(20),
        cost_estimate=lasting(3),
        name=name,
    )(place, *inputs)


def emit_small(place, flow_a, flow_b, out, att, classes):
    piece = att // 4
    rows = 2 * att + 128

    def run(place, a, other_a, b, other_b, dquery, dkey, dvalue, doutput, dclass, first, second):
        join(place, 0, a, other_a, first)
        join(place, 1, b, other_b, second)
        for source, row, target in ((first, 0, dquery), (first, att, dkey), (second, 0, dvalue)):
            for k in range(out // att):
                block = source[row + k * piece : row + (k + 1) * piece, :].astype(F32)
                target[k * att : (k + 1) * att, :] = block.T
        doutput[...] = second[att : 2 * att, :].astype(F32)
        dclass[:, :att] = first[2 * att :, :].astype(F32)[:classes]
        dclass[:, att:] = second[2 * att :, :].astype(F32)[:classes]

    return emit(
        place,
        run,
        (flow_a.kept, flow_a.other, flow_b.kept, flow_b.other),
        [(out, piece)] * 3 + [(att, att), (classes, 2 * att)],
        [(rows, att)] * 2,
        "emit_small",
    )


def emit_wide(place, flow, width_in, mid, tile):
    def run(place, mine, other, shortcut, expand, joined):
        join(place, 0, mine, other, joined)
        shortcut[...] = joined[:width_in, :].astype(F32)
        expand[...] = joined[width_in:, :].astype(F32)

    shapes = [(width_in, tile), (mid, tile)]
    return emit(place, run, (flow.kept, flow.other), shapes, [(width_in + mid, tile)], "emit_wide")


def emit_last(place, flow_a, flow_b, width_in, mid, tile, classes):
    quarter = mid // 4
    rows = 2 * flow_a.kept.shape[0]

    def run(place, a, other_a, b, other_b, spatial, reduce, *rest):
        targets, (joined,) = rest[:-1], rest[-1:]
        join(place, 0, a, other_a, joined.at[:rows])
        join(place, 1, b, other_b, joined.at[rows:])
        for tap in range(9):
            for k in range(4):
                spatial[tap, k * quarter : (k + 1) * quarter, :] = joined[
                    tap * quarter : (tap + 1) * quarter, k * quarter : (k + 1) * quarter
                ].astype(F32)
        base = 9 * quarter
        for k in range(2):
            reduce[k * mid : (k + 1) * mid, :] = joined[base + k * quarter : base + (k + 1) * quarter, :].astype(F32).T
        tail = joined[base + 2 * quarter : base + 2 * quarter + 16, :].astype(F32)
        for k in range(4):
            targets[k][...] = tail[0:1, k * quarter : (k + 1) * quarter]
        for k in range(2):
            targets[4 + k][...] = tail[1:2, k * quarter : (k + 1) * quarter]
        targets[6][...] = tail[1:2, 2 * quarter : 2 * quarter + classes]
        for k in range(4):
            targets[7 + k][...] = tail[2 + k : 3 + k, :]

    return emit(
        place,
        run,
        (flow_a.kept, flow_a.other, flow_b.kept, flow_b.other),
        [(9, mid, quarter), (width_in, quarter)] + [(1, quarter)] * 6 + [(1, classes)] + [(1, tile)] * 4,
        [(2 * rows, mid)],
        "emit_last",
    )


def move(value, how):
    kind, by = how
    if kind == "along":
        axis = ("bank", "box")
        size = lax.axis_size(axis)
        return lax.ppermute(value, axis, [(i, i + by) for i in range(size) if 0 <= i + by < size])
    return lax.ppermute(value, kind, [(i, i ^ by) for i in range(lax.axis_size(kind))])


def slot(place, kernel, inputs, moves=(), flows=(), tasks=None):
    sent = [value for value, _ in moves] + [m[0] for flow in flows for m in flow.moves()]
    hows = [how for _, how in moves] + [m[1] for flow in flows for m in flow.moves()]
    inputs, sent = lax.optimization_barrier((inputs, sent))
    received = [move(value, how) for value, how in zip(sent, hows)]
    results = kernel(*inputs) if kernel else ()
    results, received = lax.optimization_barrier((results, received))
    arrivals, flow_arrivals = received[: len(moves)], received[len(moves) :]
    own = tasks(results, arrivals) if tasks else []
    pending = [flow.arrival(other) for flow, other in zip(flows, flow_arrivals)]
    needed = own + [task for task in pending if task]
    outputs = step(place, needed) if needed else []
    made, outputs = outputs[: len(own)], outputs[len(own) :]
    for flow, task, other in zip(flows, pending, flow_arrivals):
        flow.land(other, outputs.pop(0) if task else None)
    return results, arrivals, made


def local(
    roi_features,
    box_seconds,
    video_lengths,
    bank_features,
    reduce_weight,
    reduce_gain,
    reduce_shift,
    spatial_weight,
    spatial_gain,
    spatial_shift,
    expand_weight,
    expand_gain,
    expand_shift,
    shortcut_weight,
    shortcut_gain,
    shortcut_shift,
    query_weight,
    key_weight,
    value_weight,
    norm_gain,
    norm_shift,
    output_weight,
    output_bias,
    class_weight,
    class_bias,
    logit_cotangent,
):
    boxes, grid_side = roi_features.shape[:2]
    in_width = roi_features.shape[3]
    rows = boxes * grid_side * grid_side
    mid = reduce_weight.shape[1]
    out = expand_weight.shape[1]
    att = query_weight.shape[1]
    classes = class_weight.shape[1]
    tile, quarter = out // 4, mid // 4
    all_seconds = lax.axis_size(("bank", "box")) * SEC_DEV
    my_index = lax.axis_index(("bank", "box"))
    bank_index, box_index = lax.axis_index("bank"), lax.axis_index("box")
    core, side = box_index % 2, box_index // 2
    place = jnp.stack([my_index, box_index, side, core] + [(bank_index >> k) & 1 for k in range(3)])
    order = jnp.stack([(1 - side) * 2 + 1 - core, (1 - side) * 2 + core, side * 2 + 1 - core, side * 2 + core])
    shape = dict(grid_side=grid_side, boxes=boxes)
    stacked = lambda *vectors: jnp.stack([v.astype(F32) for v in vectors])
    mid_vectors = stacked(reduce_gain, reduce_shift, spatial_gain, spatial_shift, norm_gain, norm_shift)
    vectors = stacked(expand_gain, expand_shift, shortcut_gain, shortcut_shift, output_bias)
    class_bias = class_bias.astype(F32)[None]
    on = functools.partial(slot, place)

    roi = roi_features.transpose(1, 2, 0, 3).reshape(rows, in_width)
    w9 = spatial_weight.reshape(9, mid, mid)
    place, order, mid_vectors, vectors, class_bias, roi = lax.optimization_barrier(
        (place, order, mid_vectors, vectors, class_bias, roi)
    )
    roi, x1, hidden, x2, middle, inv_mid, own_window = trunk(
        roi, reduce_weight, w9, bank_features, key_weight, value_weight, mid_vectors, **shape
    )
    around = [by for by in range(-REACH, REACH + 1) if by != 0]
    (*xs, inv_out, feature), (*windows, bank1, bank2, bank3), _ = on(
        functools.partial(widen, **shape),
        (order, roi, middle, shortcut_weight, expand_weight, vectors),
        [(own_window, ("along", -by)) for by in around] + [(bank_features, ("box", bit)) for bit in (1, 2, 3)],
    )
    windows.insert(REACH, own_window)
    (logits, dfeature, *dwindows, pack, norm_sums, bias_sums, class_sums), _, _ = on(
        functools.partial(head, all_seconds=all_seconds),
        (
            place, box_seconds, video_lengths, feature, windows, query_weight, output_weight, class_weight.T,
            mid_vectors, vectors, class_bias, logit_cotangent,
        ),
    )

    def narrow_slot(k, before, *rest):
        operands = (order, roi, middle, xs[2 * k], xs[2 * k + 1], expand_weight, inv_out, vectors, dfeature)
        return on(functools.partial(narrow, k=k, **shape), operands + before, *rest)

    own_dwindow = dwindows.pop(REACH)

    def sum_windows(results, arrivals):
        def run(place, own, a, b, c, d, total):
            parts = [v[...].astype(F32) for v in (own, a, b, c, d)]
            total[...] = (parts[0] + parts[1] + parts[2] + parts[3] + parts[4]).astype(BF16)

        return [Task(run, (own_dwindow, *arrivals[:4]), [own_dwindow.shape])]

    (away_far, d0, dmiddle, sums0), (*_, far_pack), ((dbank,),) = narrow_slot(
        0, (), [(v, ("along", by)) for v, by in zip(dwindows, around)] + [(pack, ("box", 2))], (), sum_windows
    )

    def pairs_and_far(results, arrivals):
        def run(place, pack, far_pack, dbank, far_dbank, keep, away, both_packs, both_banks, t0, t1, t2):
            for a, b, both in ((pack, far_pack, both_packs), (dbank, far_dbank, both_banks)):
                both[: a.shape[0], :] = a[...]
                both[a.shape[0] :, :] = b[...]
            for k, third in enumerate((t0, t1, t2)):
                lines = slice(k * mid, (k + 1) * mid)
                third[...] = keep[lines, :] + away[lines, :]

        double = lambda v: (2 * v.shape[0], v.shape[1])
        inputs = (pack, far_pack, dbank, arrivals[0], results[0], arrivals[1])
        return [Task(run, inputs, [double(pack), double(dbank)] + [(mid, tile)] * 3)]

    (keep_far, d1, dmiddle, sums1), _, ((packs, dbanks, *thirds),) = narrow_slot(
        1, (dmiddle,), [(dbank, ("box", 2)), (away_far, ("box", 1))], (), pairs_and_far
    )
    (away_near, d2, dmiddle, sums2), (far_packs, far_dbanks, third0), _ = narrow_slot(
        2, (dmiddle,), [(packs, ("box", 1)), (dbanks, ("box", 1)), (thirds[0], ("box", 2))]
    )
    sent_a, kept_a, sent_b, kept_b = small_weights(
        place, (packs, far_packs), (bank_features, bank2, bank1, bank3), (dbanks, far_dbanks)
    )
    small = [BankTotal(sent_a, kept_a, [0, 1, 2]), BankTotal(sent_b, kept_b, [1, 2, 0])]

    (keep_near, d3, dmiddle, sums3), (near, third1), _ = narrow_slot(
        3, (dmiddle,), [(away_near, ("box", 1)), (thirds[1], ("box", 2))], small
    )

    def wide_halves(results, arrivals):
        def run(place, keep, away, t0, t1, t2, sent, kept, total):
            for k, third in enumerate((t0, t1, t2)):
                lines = slice(k * mid, (k + 1) * mid)
                total[lines, :] = keep[lines, :] + away[lines, :] + third[...]
            halves(place, 0, total, sent, kept)

        size = keep_near.shape
        return [
            Task(run, (keep_near, near, third0, third1, arrivals[0]), [(size[0] // 2, size[1])] * 2, [size])
        ]

    (away, keep, dconv, spatial_sums), _, ((sent, kept),) = on(
        functools.partial(spatial_back, **shape),
        (place, dmiddle, x2, hidden, inv_mid, mid_vectors),
        [(thirds[2], ("box", 2))],
        small,
        wide_halves,
    )
    wide = BankTotal(sent, kept, [0, 1, 2])

    def sides(keep, away):
        def run(place, keep, away, far, near):
            size = far.shape[0]
            far[...] = keep[:size, :] + away[:size, :]
            near[...] = keep[size:, :] + away[size:, :]

        return Task(run, (keep, away), [(keep.shape[0] // 2, keep.shape[1])] * 2)

    (dreduced, last_away, last_keep), _, ((spatial_out, spatial_near),) = on(
        functools.partial(reduce_back, **shape),
        (
            order, dconv, x1, roi, w9, inv_mid, mid_vectors, spatial_sums, norm_sums, bias_sums, class_sums,
            sums0, sums1, sums2, sums3,
        ),
        [(away, ("box", 1))],
        small + [wide],
        lambda results, arrivals: [sides(keep, arrivals[0])],
    )
    roi_gradient, (spatial_far, _), ((last_out, last_near),) = on(
        roi_back,
        (order, dreduced, (d0, d1, d2, d3), reduce_weight, shortcut_weight),
        [(spatial_out, ("box", 2)), (last_away, ("box", 1))],
        small + [wide],
        lambda results, arrivals: [sides(last_keep, arrivals[1])],
    )

    def last_halves(results, arrivals):
        def run(place, spatial_near, spatial_far, near, far, sent_a, kept_a, sent_b, kept_b, total):
            size, more = spatial_near.shape[0], near.shape[0]
            total[:size, :] = spatial_near[...] + spatial_far[...]
            total[size : size + more, :] = near[...] + far[...]
            total[size + more :, :] = jnp.zeros((total.shape[0] - size - more, total.shape[1]), BF16)
            middle = total.shape[0] // 2
            halves(place, 0, total.at[:middle], sent_a, kept_a)
            halves(place, 1, total.at[middle:], sent_b, kept_b)

        length = -(-(spatial_near.shape[0] + last_near.shape[0]) // 256) * 256
        inputs = (spatial_near, spatial_far, last_near, arrivals[0])
        return [Task(run, inputs, [(length // 4, mid)] * 4, [(length, mid)])]

    _, _, ((sent_a, kept_a, sent_b, kept_b),) = on(None, (), [(last_out, ("box", 2))], small + [wide], last_halves)
    last = [BankTotal(sent_a, kept_a, [0, 1, 2]), BankTotal(sent_b, kept_b, [1, 2, 0])]
    flows = small + [wide] + last
    while any(not flow.done for flow in flows):
        on(None, (), (), [flow for flow in flows if not flow.done])

    query_g, key_g, value_g, output_g, class_g = emit_small(place, *small, out, att, classes)
    shortcut_g, expand_g = emit_wide(place, wide, in_width, mid, tile)
    spatial_g, reduce_g, *sums = emit_last(place, *last, in_width, mid, tile, classes)
    (
        reduce_gain_g, reduce_shift_g, spatial_gain_g, spatial_shift_g, norm_gain_g, norm_shift_g, class_bias_g,
        expand_gain_g, expand_shift_g, shortcut_gain_g, bias_g,
    ) = [v.reshape(v.shape[1]) for v in sums]
    return (
        logits,
        roi_gradient.reshape(grid_side, grid_side, boxes, in_width).transpose(2, 0, 1, 3),
        reduce_g,
        reduce_gain_g,
        reduce_shift_g,
        spatial_g.reshape(3, 3, mid, quarter),
        spatial_gain_g,
        spatial_shift_g,
        expand_g,
        expand_gain_g,
        expand_shift_g,
        shortcut_g,
        shortcut_gain_g,
        expand_shift_g,
        query_g,
        key_g,
        value_g,
        norm_gain_g,
        norm_shift_g,
        output_g,
        bias_g,
        class_g.T,
        class_bias_g,
    )


def solution(mesh):
    split = ("bank", "box")
    in_specs = (P(split), P(split), P(), P(split)) + (P(),) * 21 + (P(split),)
    column, vector = P(None, "box"), P("box")
    out_specs = (
        P(split),
        P(split),
        column,
        vector,
        vector,
        P(None, None, None, "box"),
        vector,
        vector,
        column,
        vector,
        vector,
        column,
        vector,
        vector,
        column,
        column,
        column,
        vector,
        vector,
        column,
        vector,
        P("box", None),
        P(),
    )
    return jax.shard_map(local, mesh=mesh, in_specs=in_specs, out_specs=out_specs, check_vma=False)
```

```python
import functools
import jax
import jax.numpy as jnp
from jax import lax
from jax.experimental import pallas as pl
from jax.experimental.pallas import tpu as pltpu
from jax.sharding import PartitionSpec as P

HALF = 30
PER_SEC = 8
SEC_DEV = 16
REACH = 2
EPSILON = 1e-05
MIB = 2**20
F32, BF16 = jnp.float32, jnp.bfloat16
BRIEF = pl.CostEstimate(flops=1, bytes_accessed=1, transcendentals=0)
ON_CHIP = pl.BlockSpec(memory_space=pltpu.VMEM)
SCALARS = pl.BlockSpec(memory_space=pltpu.SMEM)
FAR = pl.BlockSpec(memory_space=pl.ANY)
OVER_ROWS = (((0,), (0,)), ((), ()))
OVER_COLUMNS = (((1,), (1,)), ((), ()))


def plain(a, b):
    return jnp.dot(a, b, preferred_element_type=F32)


def over_rows(a, b):
    return lax.dot_general(a, b, OVER_ROWS, preferred_element_type=F32)


def over_columns(a, b):
    return lax.dot_general(a, b, OVER_COLUMNS, preferred_element_type=F32)


def params(mebibytes):
    return pltpu.CompilerParams(vmem_limit_bytes=mebibytes * MIB)


def kept(*arrays):
    return [pltpu.with_memory_space_constraint(v, pltpu.VMEM) for v in arrays]


def outside(*arrays):
    return [pltpu.with_memory_space_constraint(v, pltpu.HBM) for v in arrays]


def start_copies(pairs, sems):
    copies = [pltpu.make_async_copy(source, target, sems.at[k]) for k, (source, target) in enumerate(pairs)]
    for copy in copies:
        copy.start()
    return copies


def fold(values):
    values = values.astype(F32)
    return jnp.sum(values.reshape(values.shape[0] // 8, 8, values.shape[1]), axis=0)


def total_rows(values):
    return jnp.sum(values, axis=0, keepdims=True)


def centre(acc, centred, grid_side, boxes):
    rows, width = acc.shape
    step = grid_side * boxes
    first = acc[0:step, :]
    shift = total_rows(jnp.sum(first.reshape(step // 8, 8, width), axis=0)) / step

    def line(k, carry):
        total, square = carry
        sums = squares = None
        for w in range(grid_side):
            at = pl.ds((k * grid_side + w) * boxes, boxes)
            value = (acc[at, :] - shift).astype(BF16)
            centred[at, :] = value
            sums = value if sums is None else sums + value
            squares = value * value if squares is None else squares + value * value
        return total + fold(sums), square + fold(squares)

    zero = jnp.zeros((8, width), F32)
    total, square = lax.fori_loop(0, grid_side, line, (zero, zero))
    offset = total_rows(total) / rows
    var = total_rows(square) / rows - offset * offset
    return lax.rsqrt(jnp.maximum(var, 0.0) + EPSILON), offset, shift


def scaled(inv, offset, gain, shift):
    factor = 0.5 * gain * inv
    return factor, 0.5 * shift - factor * offset


def input_gradient(inv, offset, gain, total, total_c, rows):
    gain_gradient = inv * (total_c - offset * total)
    of_upstream = inv * gain
    of_centred = -of_upstream * inv * gain_gradient / rows
    term = -of_upstream * total / rows - of_centred * offset
    return of_upstream, of_centred, term, gain_gradient


def clear_border(padded):
    side, _, boxes, width = padded.shape
    zeros = jnp.zeros((boxes, width), BF16)
    for k in range(side):
        padded[0, k] = zeros
        padded[side - 1, k] = zeros
        padded[k, 0] = zeros
        padded[k, side - 1] = zeros


def by_cells(grid_side, boxes, body, carry):
    def line(k, carry):
        for w in range(grid_side):
            carry = body(k, w, pl.ds((k * grid_side + w) * boxes, boxes), carry)
        return carry

    return lax.fori_loop(0, grid_side, line, carry)


def trunk_kernel(
    grid_side, boxes, roi_far, wr_far, w9_far, bank_far, kw_far, vw_far, *rest
):
    far_vectors, rest = rest[:12], rest[12:]
    roi, x1, hidden, x2, middle, inv, window, vectors, wide_vectors, class_bias = rest[:10]
    wr, w9, bank, kw, vw, acc, sems = rest[10:17]
    near_vectors = rest[17:]
    copies = start_copies(
        [(roi_far, roi), (wr_far, wr), (w9_far, w9), (bank_far, bank), (kw_far, kw), (vw_far, vw)]
        + list(zip(far_vectors, near_vectors)),
        sems,
    )
    clear_border(hidden)
    for k, copy in enumerate(copies[6:]):
        copy.wait()
        value = near_vectors[k][...].astype(F32)
        value = value.reshape(1, value.shape[0])
        if k < 6:
            vectors[k : k + 1, :] = value
        elif k < 11:
            wide_vectors[k - 6 : k - 5, :] = value
        else:
            class_bias[...] = value
    copies[0].wait()
    copies[1].wait()
    acc[...] = plain(roi[...], wr[...])
    inv1, offset1, base = centre(acc, x1, grid_side, boxes)
    inv[0:1, :], inv[1:2, :] = inv1, offset1
    factor, term = scaled(inv1, base + offset1, vectors[0:1, :], vectors[1:2, :])

    def first(k, w, rows, carry):
        h = acc[rows, :] * factor + term
        hidden[k + 1, w + 1] = (h + h * jnp.tanh(h)).astype(BF16)
        return carry

    by_cells(grid_side, boxes, first, 0)
    copies[2].wait()
    for p in range(3):
        for q in range(3):
            taps = hidden[p : p + grid_side, q : q + grid_side].reshape(acc.shape)
            product = plain(taps, w9[p * 3 + q])
            if p + q == 0:
                acc[...] = product
            else:
                acc[...] += product
    inv2, offset2, base2 = centre(acc, x2, grid_side, boxes)
    inv[2:3, :], inv[3:4, :] = inv2, offset2
    factor2, term2 = scaled(inv2, base2 + offset2, vectors[2:3, :], vectors[3:4, :])

    def second(k, w, rows, carry):
        h = acc[rows, :] * factor2 + term2
        middle[rows, :] = (h + h * jnp.tanh(h)).astype(BF16)
        return carry

    by_cells(grid_side, boxes, second, 0)
    for copy in copies[3:6]:
        copy.wait()
    att = kw.shape[1]
    window[:, :att] = plain(bank[...], kw[...]).astype(BF16)
    window[:, att:] = plain(bank[...], vw[...]).astype(BF16)


def trunk(roi, wr, w9, bank, kw, vw, *vectors, grid_side, boxes):
    rows, mid = roi.shape[0], wr.shape[1]
    side = grid_side + 2
    return pl.pallas_call(
        functools.partial(trunk_kernel, grid_side, boxes),
        in_specs=[FAR] * 18,
        out_specs=[ON_CHIP] * 10,
        out_shape=[
            pltpu.VMEM(roi.shape, BF16),
            pltpu.VMEM((rows, mid), BF16),
            pltpu.VMEM((side, side, boxes, mid), BF16),
            pltpu.VMEM((rows, mid), BF16),
            pltpu.VMEM((rows, mid), BF16),
            jax.ShapeDtypeStruct((4, mid), F32),
            jax.ShapeDtypeStruct((bank.shape[0], 2 * kw.shape[1]), BF16),
            jax.ShapeDtypeStruct((6, mid), F32),
            jax.ShapeDtypeStruct((5, vectors[6].shape[0]), F32),
            jax.ShapeDtypeStruct((1, vectors[11].shape[0]), F32),
        ],
        scratch_shapes=[pltpu.VMEM(v.shape, BF16) for v in (wr, w9, bank, kw, vw)]
        + [pltpu.VMEM((rows, mid), F32), pltpu.SemaphoreType.DMA((18,))]
        + [pltpu.VMEM(v.shape, BF16) for v in vectors],
        compiler_params=params(18),
        cost_estimate=BRIEF,
        name="trunk",
    )(*outside(roi, wr, w9, bank, kw, vw, *vectors))


def widen_kernel(grid_side, boxes, order, roi, middle, ws_far, we_far, vectors, *rest):
    xs, (inv, feature, ws, we, acc_e, acc_p, sems) = rest[:8], rest[8:]
    width = acc_e.shape[1]
    at = [pl.ds(pl.multiple_of(order[k] * width, width), width) for k in range(4)]
    copies = start_copies(
        [pair for k in range(4) for pair in ((ws_far.at[:, at[k]], ws.at[k]), (we_far.at[:, at[k]], we.at[k]))],
        sems,
    )
    for k in range(4):
        xe, xp = xs[2 * k], xs[2 * k + 1]
        copies[2 * k].wait()
        acc_p[...] = plain(roi[...], ws[k])
        copies[2 * k + 1].wait()
        acc_e[...] = plain(middle[...], we[k])
        inv_p, offset_p, base_p = centre(acc_p, xp, grid_side, boxes)
        inv_e, offset_e, base_e = centre(acc_e, xe, grid_side, boxes)
        for row, value in enumerate((inv_e, inv_p, offset_e, offset_p)):
            inv[k, row : row + 1, :] = value
        factor_e, term_e = scaled(inv_e, base_e + offset_e, vectors[0:1, at[k]], vectors[1:2, at[k]])
        factor_p, term_p = scaled(inv_p, base_p + offset_p, vectors[2:3, at[k]], vectors[3:4, at[k]])
        term = term_e + term_p

        def line(row, total):
            for w in range(grid_side):
                rows = pl.ds((row * grid_side + w) * boxes, boxes)
                h = acc_e[rows, :] * factor_e + acc_p[rows, :] * factor_p + term
                total = total + (h + h * jnp.tanh(h))
            return total

        total = lax.fori_loop(0, grid_side, line, jnp.zeros((boxes, width), F32))
        feature[:, at[k]] = total / (grid_side * grid_side)


def widen(order, roi, middle, ws, we, vectors, grid_side, boxes):
    rows, width_in = roi.shape
    mid, out = we.shape
    tile = out // 4
    return pl.pallas_call(
        functools.partial(widen_kernel, grid_side, boxes),
        in_specs=[SCALARS, ON_CHIP, ON_CHIP, FAR, FAR, ON_CHIP],
        out_specs=[ON_CHIP] * 10,
        out_shape=[pltpu.VMEM((rows, tile), BF16)] * 8
        + [jax.ShapeDtypeStruct((4, 4, tile), F32), jax.ShapeDtypeStruct((boxes, out), F32)],
        scratch_shapes=[
            pltpu.VMEM((4, width_in, tile), BF16),
            pltpu.VMEM((4, mid, tile), BF16),
            pltpu.VMEM((rows, tile), F32),
            pltpu.VMEM((rows, tile), F32),
            pltpu.SemaphoreType.DMA((8,)),
        ],
        compiler_params=params(18),
        cost_estimate=BRIEF,
        name="widen",
    )(order, *kept(roi, middle), *outside(ws, we), vectors)


def doubled_slope(h):
    t = jnp.tanh(h)
    return (1.0 + t) * (1.0 + h * (1.0 - t))


def narrow_part(
    grid_side, boxes, k, order, roi, middle, xe, xp, we, inv, vectors, dfeature, part, dprojected, sums,
    upstream, dexpanded,
):
    rows, width = upstream.shape
    columns = pl.ds(pl.multiple_of(order[k] * width, width), width)
    gain_e, gain_p = vectors[0:1, columns], vectors[2:3, columns]
    inv_e, inv_p, offset_e, offset_p = [inv[k, row : row + 1, :] for row in range(4)]
    factor_e, term_e = scaled(inv_e, offset_e, gain_e, vectors[1:2, columns])
    factor_p, term_p = scaled(inv_p, offset_p, gain_p, vectors[3:4, columns])
    term = term_e + term_p
    slope_scale = dfeature[:, columns] * (0.5 / (grid_side * grid_side))

    def line(row, carry):
        sums = None
        for w in range(grid_side):
            at = pl.ds((row * grid_side + w) * boxes, boxes)
            e, p = xe[at, :].astype(F32), xp[at, :].astype(F32)
            u = doubled_slope(e * factor_e + p * factor_p + term) * slope_scale
            upstream[at, :] = u
            new = (u, u * e, u * p)
            sums = new if sums is None else [a + b for a, b in zip(sums, new)]
        return [a + fold(b) for a, b in zip(carry, sums)]

    zero = jnp.zeros((8, width), F32)
    total, total_e, total_p = [total_rows(v) for v in lax.fori_loop(0, grid_side, line, [zero] * 3)]
    ue, ce, te, gain_gradient_e = input_gradient(inv_e, offset_e, gain_e, total, total_e, rows)
    up, cp, tp, gain_gradient_p = input_gradient(inv_p, offset_p, gain_p, total, total_p, rows)
    sums[0:1, :] = gain_gradient_e
    sums[1:2, :] = total
    sums[2:3, :] = gain_gradient_p

    def second(row, w, at, carry):
        u = upstream[at, :]
        dexpanded[at, :] = (u * ue + xe[at, :].astype(F32) * ce + te).astype(BF16)
        dprojected[at, :] = (u * up + xp[at, :].astype(F32) * cp + tp).astype(BF16)
        return carry

    by_cells(grid_side, boxes, second, 0)
    split = roi.shape[1]
    part[0:split, :] = over_rows(roi[...], dprojected[...]).astype(BF16)
    part[split:, :] = over_rows(middle[...], dexpanded[...]).astype(BF16)
    return over_columns(dexpanded[...], we[...])


def expand_columns(order, ks, we_far, we, sems):
    width = we.shape[2]
    columns = [pl.ds(pl.multiple_of(order[k] * width, width), width) for k in ks]
    return start_copies([(we_far.at[:, at], we.at[n]) for n, at in enumerate(columns)], sems)


def narrow_kernel(grid_side, boxes, ks, order, roi, middle, inv, vectors, dfeature, we_far, *rest):
    count = len(ks)
    xs, rest = rest[: 2 * count], rest[2 * count :]
    *before, dmiddle = rest[: -4 - 3 * count]
    outs, (we, upstream, dexpanded, sems) = rest[-4 - 3 * count : -4], rest[-4:]
    copies = expand_columns(order, ks, we_far, we, sems)
    for n, k in enumerate(ks):
        copies[n].wait()
        back = narrow_part(
            grid_side, boxes, k, order, roi, middle, xs[2 * n], xs[2 * n + 1], we.at[n], inv, vectors, dfeature,
            *outs[3 * n : 3 * n + 3], upstream, dexpanded,
        )
        if n == 0:
            dmiddle[...] = before[0][...] + back if before else back
        else:
            dmiddle[...] += back


def narrow(order, roi, middle, inv, vectors, dfeature, we, *rest, ks, grid_side, boxes):
    rows, width_in = roi.shape
    mid, out = we.shape
    tile = out // 4
    xs, before = rest[: 2 * len(ks)], rest[2 * len(ks) :]
    return pl.pallas_call(
        functools.partial(narrow_kernel, grid_side, boxes, ks),
        in_specs=[SCALARS] + [ON_CHIP] * 5 + [FAR] + [ON_CHIP] * len(rest),
        out_specs=[ON_CHIP] * (1 + 3 * len(ks)),
        out_shape=[pltpu.VMEM((rows, mid), F32)]
        + [
            jax.ShapeDtypeStruct((width_in + mid, tile), BF16),
            pltpu.VMEM((rows, tile), BF16),
            jax.ShapeDtypeStruct((3, tile), F32),
        ]
        * len(ks),
        input_output_aliases={7 + 2 * len(ks): 0} if before else {},
        scratch_shapes=[
            pltpu.VMEM((len(ks), mid, tile), BF16),
            pltpu.VMEM((rows, tile), F32),
            pltpu.VMEM((rows, tile), BF16),
            pltpu.SemaphoreType.DMA((len(ks),)),
        ],
        compiler_params=params(16),
        cost_estimate=BRIEF,
        name="narrow",
    )(order, *kept(roi, middle), inv, vectors, dfeature, *outside(we), *kept(*xs, *before))


def norm_back(grid_side, boxes, upstream, centred, inv, offset, gain, shift, low, sums, store):
    rows, width = upstream.shape
    factor, term = scaled(inv, offset, gain, shift)

    def line(row, carry):
        sums = None
        for w in range(grid_side):
            at = pl.ds((row * grid_side + w) * boxes, boxes)
            c = centred[at, :].astype(F32)
            u = doubled_slope(c * factor + term) * (0.5 * upstream[at, :])
            low[at, :] = u
            new = (u, u * c)
            sums = new if sums is None else [a + b for a, b in zip(sums, new)]
        return [a + fold(b) for a, b in zip(carry, sums)]

    zero = jnp.zeros((8, width), F32)
    total, total_c = [total_rows(v) for v in lax.fori_loop(0, grid_side, line, [zero] * 2)]
    of_upstream, of_centred, term, gain_gradient = input_gradient(inv, offset, gain, total, total_c, rows)
    sums[0:1, :] = gain_gradient
    sums[1:2, :] = total

    def second(row, w, at, carry):
        value = low[at, :] * of_upstream + centred[at, :].astype(F32) * of_centred + term
        store(row, w, at, value.astype(BF16))
        return carry

    by_cells(grid_side, boxes, second, 0)


def spatial_taps(grid_side, side, core, hidden, dflat, part, away, keep):
    rows, width = dflat.shape
    half, quarter = width // 2, width // 4
    mine = pl.ds(pl.multiple_of(core * quarter, quarter), quarter)
    other = pl.ds(pl.multiple_of((1 - core) * quarter, quarter), quarter)
    columns = dflat[:, pl.ds(pl.multiple_of(side * half, half), half)]
    for p in range(3):
        for q in range(3):
            taps = hidden[p : p + grid_side, q : q + grid_side].reshape(rows, width)
            part[...] = over_rows(taps, columns).astype(BF16)
            lines = slice((p * 3 + q) * quarter, (p * 3 + q + 1) * quarter)
            for k in range(4):
                lanes = slice(k * quarter, (k + 1) * quarter)
                keep[lines, lanes] = part[lanes, mine]
                away[lines, lanes] = part[lanes, other]


def spatial_far_kernel(
    grid_side, boxes, order, place, roi, middle, inv_out, wide_vectors, dfeature, we_far, xe, xp, before,
    x2, hidden, inv, vectors, part, dprojected, wide_sums, away, keep, dconv, dflat, sums,
    we, upstream, dexpanded, taps, sems,
):
    copies = expand_columns(order, (3,), we_far, we, sems)
    clear_border(dconv)
    copies[0].wait()
    back = narrow_part(
        grid_side, boxes, 3, order, roi, middle, xe, xp, we.at[0], inv_out, wide_vectors, dfeature,
        part, dprojected, wide_sums, upstream, dexpanded,
    )
    upstream[...] = before[...] + back

    def store(row, w, at, value):
        dconv[row + 1, w + 1] = value
        dflat[at, :] = value

    norm_back(
        grid_side, boxes, upstream, x2, inv[2:3, :], inv[3:4, :], vectors[2:3, :], vectors[3:4, :], upstream, sums, store
    )
    spatial_taps(grid_side, 1 - place[2], place[3], hidden, dflat, taps, away, keep)


def spatial_far(
    order, place, roi, middle, inv_out, wide_vectors, dfeature, we, xe, xp, before, x2, hidden, inv, vectors,
    grid_side, boxes,
):
    rows, width_in = roi.shape
    mid, out = we.shape
    tile, side = out // 4, grid_side + 2
    taps = jax.ShapeDtypeStruct((9 * (mid // 4), mid), BF16)
    return pl.pallas_call(
        functools.partial(spatial_far_kernel, grid_side, boxes),
        in_specs=[SCALARS] * 2 + [ON_CHIP] * 5 + [FAR] + [ON_CHIP] * 7,
        out_specs=[ON_CHIP] * 8,
        out_shape=[
            jax.ShapeDtypeStruct((width_in + mid, tile), BF16),
            pltpu.VMEM((rows, tile), BF16),
            jax.ShapeDtypeStruct((3, tile), F32),
            taps,
            taps,
            pltpu.VMEM((side, side, boxes, mid), BF16),
            pltpu.VMEM((rows, mid), BF16),
            jax.ShapeDtypeStruct((2, mid), F32),
        ],
        scratch_shapes=[
            pltpu.VMEM((1, mid, tile), BF16),
            pltpu.VMEM((rows, tile), F32),
            pltpu.VMEM((rows, tile), BF16),
            pltpu.VMEM((mid, mid // 2), BF16),
            pltpu.SemaphoreType.DMA((1,)),
        ],
        compiler_params=params(18),
        cost_estimate=BRIEF,
        name="spatial_far",
    )(
        order, place, *kept(roi, middle), inv_out, wide_vectors, dfeature, *outside(we), *kept(xe, xp, before, x2, hidden),
        inv, vectors,
    )


def spatial_near_kernel(grid_side, place, hidden, dflat, away, keep, part):
    spatial_taps(grid_side, place[2], place[3], hidden, dflat, part, away, keep)


def spatial_near(place, hidden, dflat, grid_side):
    mid = dflat.shape[1]
    part = jax.ShapeDtypeStruct((9 * (mid // 4), mid), BF16)
    return pl.pallas_call(
        functools.partial(spatial_near_kernel, grid_side),
        in_specs=[SCALARS] + [ON_CHIP] * 2,
        out_specs=[ON_CHIP] * 2,
        out_shape=[part] * 2,
        scratch_shapes=[pltpu.VMEM((mid, mid // 2), BF16)],
        compiler_params=params(14),
        cost_estimate=BRIEF,
        name="spatial_near",
    )(place, *kept(hidden, dflat))


def reduce_back_kernel(
    grid_side, boxes, order, dconv, x1, roi, w9_far, inv, vectors, spatial_sums, norm_sums, bias_sums, class_sums,
    s0, s1, s2, s3, dreduced, away, keep, upstream, w9, weight, sums, sems,
):
    rows, width = upstream.shape
    copies = start_copies([(w9_far.at[k], w9.at[k]) for k in range(9)], sems)
    for p in range(3):
        for q in range(3):
            copies[p * 3 + q].wait()
            taps = dconv[2 - p : 2 - p + grid_side, 2 - q : 2 - q + grid_side].reshape(rows, width)
            product = over_columns(taps, w9[p * 3 + q])
            if p + q == 0:
                upstream[...] = product
            else:
                upstream[...] += product

    def store(row, w, at, value):
        dreduced[at, :] = value

    norm_back(
        grid_side, boxes, upstream, x1, inv[0:1, :], inv[1:2, :], vectors[0:1, :], vectors[1:2, :], upstream, sums, store
    )
    weight[...] = over_rows(dreduced[...], roi[...]).astype(BF16)
    quarter, classes = width // 4, class_sums.shape[1]
    size = away.shape[0] // 2
    for k, (target, wide_sums) in enumerate(((away, s0), (keep, s1), (away, s2), (keep, s3))):
        base = (k // 2) * size
        lines = pl.ds(pl.multiple_of(order[k] * quarter, quarter), quarter)
        wide = pl.ds(pl.multiple_of(order[k] * width, width), width)
        target[base : base + quarter, :] = weight[lines, :width]
        target[base + quarter : base + 2 * quarter, :] = weight[lines, width:]
        line0 = [v[r : r + 1, lines] for v in (sums, spatial_sums) for r in range(2)]
        line1 = [norm_sums[r : r + 1, lines] for r in range(2)]
        line1 += [class_sums[...], jnp.zeros((1, width - 2 * quarter - classes), F32)]
        tail = jnp.concatenate(
            [
                jnp.concatenate(line0, axis=1),
                jnp.concatenate(line1, axis=1),
                wide_sums[...],
                bias_sums[:, wide],
                jnp.zeros((10, width), F32),
            ]
        )
        target[base + 2 * quarter : base + size, :] = tail.astype(BF16)


def reduce_back(order, dconv, x1, roi, w9, inv, vectors, *sums, grid_side, boxes):
    rows, width_in = roi.shape
    mid = w9.shape[1]
    part = jax.ShapeDtypeStruct((2 * (mid // 2 + 16), mid), BF16)
    return pl.pallas_call(
        functools.partial(reduce_back_kernel, grid_side, boxes),
        in_specs=[SCALARS] + [ON_CHIP] * 3 + [FAR] + [ON_CHIP] * 10,
        out_specs=[ON_CHIP] * 3,
        out_shape=[pltpu.VMEM((rows, mid), BF16), part, part],
        scratch_shapes=[
            pltpu.VMEM((rows, mid), F32),
            pltpu.VMEM(w9.shape, BF16),
            pltpu.VMEM((mid, width_in), BF16),
            pltpu.VMEM((2, mid), F32),
            pltpu.SemaphoreType.DMA((9,)),
        ],
        compiler_params=params(16),
        cost_estimate=BRIEF,
        name="reduce_back",
    )(order, *kept(dconv, x1, roi), *outside(w9), inv, vectors, *sums)


def roi_back_kernel(half, order, dreduced, d0, d1, d2, d3, wr_far, ws_far, *rest):
    out, wr, ws, acc, low, sems = rest[-6:]
    tile = d0.shape[1]
    size = acc.shape[1]
    lines = pl.ds(half * size, size)
    columns = [pl.ds(pl.multiple_of(order[k] * tile, tile), tile) for k in range(4)]
    copies = start_copies(
        [(wr_far.at[lines, :], wr)] + [(ws_far.at[lines, columns[k]], ws.at[k]) for k in range(4)], sems
    )
    copies[0].wait()
    acc[...] = over_columns(dreduced[...], wr[...])
    for k, d in enumerate((d0, d1, d2, d3)):
        copies[k + 1].wait()
        acc[...] += over_columns(d[...], ws[k])
    low[...] = acc[...].astype(BF16)
    pltpu.sync_copy(low, out.at[:, lines])


def roi_back(order, dreduced, dprojected, wr, ws, *done, half):
    rows, mid = dreduced.shape
    width_in, out = ws.shape
    size = width_in // 2
    return pl.pallas_call(
        functools.partial(roi_back_kernel, half),
        in_specs=[SCALARS] + [ON_CHIP] * 5 + [FAR] * (2 + len(done)),
        out_specs=FAR,
        out_shape=pltpu.HBM((rows, width_in), BF16),
        input_output_aliases={8: 0} if done else {},
        scratch_shapes=[
            pltpu.VMEM((size, mid), BF16),
            pltpu.VMEM((4, size, out // 4), BF16),
            pltpu.VMEM((rows, size), F32),
            pltpu.VMEM((rows, size), BF16),
            pltpu.SemaphoreType.DMA((5,)),
        ],
        compiler_params=params(18),
        cost_estimate=BRIEF,
        name="roi_back",
    )(order, *kept(dreduced, *dprojected), *outside(wr, ws, *done))


def head_kernel(
    all_seconds, place, seconds, lengths, feature, w0, w1, w2, w3, w4, wq_far, wo_far, wc_far,
    mid_vectors, vectors, class_bias, cotangent,
    logits, dfeature, pack, norm_sums, bias_sums, class_sums, window, wq, wo, wc, sems,
):
    copies = start_copies([(wq_far, wq), (wo_far, wo), (wc_far, wc)], sems)
    att = wq.shape[1]
    boxes, out = feature.shape
    classes = cotangent.shape[1]
    span = window.shape[0]
    rows = w0.shape[0]
    for k, w in enumerate((w0, w1, w2, w3, w4)):
        window[k * rows : (k + 1) * rows, :] = w[...]
    scale = att ** (-0.5)
    norm_gain, norm_shift = mid_vectors[4:5, :], mid_vectors[5:6, :]

    row_seconds = lax.broadcasted_iota(jnp.int32, (boxes, span), 1) // PER_SEC + (place[0] - REACH) * SEC_DEV
    line = lax.broadcasted_iota(jnp.int32, (boxes, 128), 0)
    box_seconds = jnp.zeros((boxes, 128), jnp.int32)
    for k in range(boxes):
        box_seconds = jnp.where(line == k, seconds[k], box_seconds)
    box_seconds = box_seconds[:, 0:1]
    live = (row_seconds >= 0) & (row_seconds < all_seconds) & (jnp.abs(box_seconds - row_seconds) <= HALF)
    end = 0
    for k in range(lengths.shape[0]):
        end = end + lengths[k]
        live = live & ((end <= row_seconds) == (end <= box_seconds))

    copies[0].wait()
    feature_low = feature[...].astype(BF16)
    pack[:, :out] = feature_low
    queries = plain(feature_low, wq[...]).astype(BF16)
    keys, values = window[:, :att], window[:, att:]
    scores = over_columns(queries, keys) * scale
    top = jnp.max(jnp.where(live, scores, -1e30), axis=1, keepdims=True)
    exps = jnp.where(live, jnp.exp(jnp.where(live, scores - top, 0.0)), 0.0)
    probs = exps / jnp.sum(exps, axis=1, keepdims=True)
    probs_low = probs.astype(BF16)
    pre = plain(probs_low, values) + queries.astype(F32)
    centred = pre - jnp.mean(pre, axis=1, keepdims=True)
    inv = lax.rsqrt(jnp.mean(centred * centred, axis=1, keepdims=True) + EPSILON)
    x = centred * inv
    h = 0.5 * (x * norm_gain + norm_shift)
    activated = (h + h * jnp.tanh(h)).astype(BF16)
    copies[1].wait()
    combined_low = (feature[...] + plain(activated, wo[...]) + vectors[4:5, :]).astype(BF16)
    pack[:, out : 2 * out] = combined_low
    copies[2].wait()
    logits[...] = over_columns(feature_low, wc[:, :out]) + over_columns(combined_low, wc[:, out:]) + class_bias[...]
    g = cotangent[...].astype(BF16)
    class_sums[...] = jnp.sum(g.astype(F32), axis=0, keepdims=True)
    first = plain(g, wc[:, :out])
    second = plain(g, wc[:, out:])
    gb = second.astype(BF16)
    pack[:, 2 * out : 3 * out] = gb
    bias_sums[...] = jnp.sum(gb.astype(F32), axis=0, keepdims=True)
    u = over_columns(gb, wo[...]) * (0.5 * doubled_slope(h))
    norm_sums[0:1, :] = jnp.sum(u * x, axis=0, keepdims=True)
    norm_sums[1:2, :] = jnp.sum(u, axis=0, keepdims=True)
    e = u * norm_gain
    dpre = inv * (e - jnp.mean(e, axis=1, keepdims=True) - x * jnp.mean(e * x, axis=1, keepdims=True))
    da = dpre.astype(BF16)
    dprobs = over_columns(da, values)
    delta = jnp.sum(probs * dprobs, axis=1, keepdims=True)
    ds = (probs * (dprobs - delta)).astype(BF16)
    dq = (plain(ds, keys) * scale + dpre).astype(BF16)
    at = 3 * out
    for value in (dq, activated, queries, da):
        pack[:, at : at + att] = value
        at += att
    pack[:, at : at + 128] = jnp.zeros((boxes, 128), BF16)
    pack[:, at : at + classes] = g
    at += 128
    pack[:, at : at + span] = ds
    pack[:, at + span :] = probs_low
    dfeature[...] = first + second + over_columns(dq, wq[...])


def head(place, seconds, lengths, feature, windows, wq, wo, wc, mid_vectors, vectors, class_bias, cotangent, all_seconds):
    boxes, out = feature.shape
    att = wq.shape[1]
    classes = wc.shape[0]
    span = sum(w.shape[0] for w in windows)
    shapes = [
        ((boxes, classes), F32),
        ((boxes, out), F32),
        ((boxes, 3 * out + 4 * att + 128 + 2 * span), BF16),
        ((2, att), F32),
        ((1, out), F32),
        ((1, classes), F32),
    ]
    return pl.pallas_call(
        functools.partial(head_kernel, all_seconds),
        in_specs=[SCALARS] * 3 + [ON_CHIP] * 6 + [FAR] * 3 + [ON_CHIP] * 4,
        out_specs=[ON_CHIP] * len(shapes),
        out_shape=[jax.ShapeDtypeStruct(s, d) for s, d in shapes],
        scratch_shapes=[
            pltpu.VMEM((span, 2 * att), BF16),
            pltpu.VMEM(wq.shape, BF16),
            pltpu.VMEM(wo.shape, BF16),
            pltpu.VMEM(wc.shape, BF16),
            pltpu.SemaphoreType.DMA((3,)),
        ],
        compiler_params=params(16),
        cost_estimate=BRIEF,
        name="head",
    )(place, seconds, lengths, feature, *windows, *outside(wq, wo, wc), mid_vectors, vectors, class_bias, cotangent)


def halves(place, bit, value, sent, kept):
    size = sent.shape[0]
    mine = place[4 + bit]
    sent[...] = value[pl.ds(pl.multiple_of((1 - mine) * size, 16), size), :]
    kept[...] = value[pl.ds(pl.multiple_of(mine * size, 16), size), :]


def small_weights_kernel(
    grouped, place, pair, far_pair, pair_bank, far_bank, sent_a, kept_a, sent_b, kept_b,
    pack, banks, dbank, first, second,
):
    boxes = pair.shape[0] // 2
    for k, source in ((place[3], pair), (1 - place[3], far_pair)):
        for half in range(2):
            lines = pl.ds(pl.multiple_of((2 * half + k) * boxes, 16), boxes)
            pack[lines, :] = source[half * boxes : (half + 1) * boxes, :]
    rows = pair_bank.shape[0] // 4
    for k, source in ((place[3], pair_bank), (1 - place[3], far_bank)):
        for block in range(4):
            lines = pl.ds(pl.multiple_of((2 * block + k) * rows, 16), rows)
            banks[lines, :] = source[block * rows : (block + 1) * rows, :]
    width = first.shape[1]
    att, out, piece = width, banks.shape[1], width // 4
    span = (2 * REACH + 1) * rows
    q = place[1]
    columns = lambda base, size: pl.ds(pl.multiple_of(base + q * size, size), size)
    base = 3 * out
    at = base + 4 * att + 128
    dbank[...] = jnp.zeros(dbank.shape, F32)
    for k in range(grouped):
        lines, window = slice(k * boxes, (k + 1) * boxes), slice(k * rows, k * rows + span)
        ds, probs = pack[lines, at : at + span], pack[lines, at + span : at + 2 * span]
        dbank[window, :piece] += over_rows(ds, pack[lines, columns(base + 2 * att, piece)]) * att ** (-0.5)
        dbank[window, piece:] += over_rows(probs, pack[lines, columns(base + 3 * att, piece)])
    for left, right, target, row in (
        (pack[:, columns(base, piece)], pack[:, :out], first, 0),
        (dbank[:, :piece].astype(BF16), banks[...], first, att),
        (dbank[:, piece:].astype(BF16), banks[...], second, 0),
    ):
        product = over_rows(left, right).astype(BF16)
        for k in range(out // width):
            target[row + k * piece : row + (k + 1) * piece, :] = product[:, k * width : (k + 1) * width]
    second[att : 2 * att, :] = over_rows(
        pack[:, base + att : base + 2 * att], pack[:, columns(2 * out, out // 4)]
    ).astype(BF16)
    at = base + 4 * att
    product = over_rows(pack[:, at : at + 128], pack[:, columns(0, out // 2)]).astype(BF16)
    first[2 * att :, :] = product[:, :width]
    second[2 * att :, :] = product[:, width:]
    halves(place, 0, first, sent_a, kept_a)
    halves(place, 0, second, sent_b, kept_b)


def small_weights(place, pair, far_pair, pair_bank, far_bank, att, grouped):
    rows, out = 2 * att + 128, pair_bank.shape[1]
    reach = 2 * pair_bank.shape[0]
    return pl.pallas_call(
        functools.partial(small_weights_kernel, grouped),
        in_specs=[SCALARS] + [ON_CHIP] * 4,
        out_specs=[ON_CHIP] * 4,
        out_shape=[jax.ShapeDtypeStruct((rows // 2, att), BF16)] * 4,
        scratch_shapes=[
            pltpu.VMEM((2 * pair.shape[0], pair.shape[1]), BF16),
            pltpu.VMEM((reach, out), BF16),
            pltpu.VMEM((reach, att // 2), F32),
            pltpu.VMEM((rows, att), BF16),
            pltpu.VMEM((rows, att), BF16),
        ],
        compiler_params=params(20),
        cost_estimate=BRIEF,
        name="small_weights",
    )(place, pair, far_pair, pair_bank, far_bank)


class View:
    def __init__(self, array, at=0, rows=None):
        self.array, self.at = array, at
        self.rows = array.shape[0] if rows is None else rows

    @property
    def shape(self):
        return (self.rows, *self.array.shape[1:])

    def of(self, array):
        return View(array, self.at, self.rows)


def view(value):
    return value if isinstance(value, View) else View(value)


class Task:
    def __init__(self, run, inputs, outputs, scratch=()):
        self.run, self.scratch = run, list(scratch)
        self.inputs = [view(v) for v in inputs]
        self.outputs = [out if isinstance(out[0], tuple) else (out, None) for out in outputs]


def distinct(views):
    arrays, places = [], []
    for v in views:
        found = [k for k, array in enumerate(arrays) if array is v.array]
        places.append(found[0] if found else len(arrays))
        if not found:
            arrays.append(v.array)
    return arrays, places


def rows_of(ref, v):
    return ref if v.rows == v.array.shape[0] else ref.at[v.at : v.at + v.rows]


def step(place, tasks):
    arrays, places = distinct([v for t in tasks for v in t.inputs])
    shapes, boxes, outputs = [], {}, []
    for task in tasks:
        for shape, way in task.outputs:
            if way is None:
                shapes.append(list(shape))
                outputs.append((len(shapes) - 1, 0, shape[0]))
            else:
                if way not in boxes:
                    boxes[way] = len(shapes)
                    shapes.append([0, shape[1]])
                box = shapes[boxes[way]]
                outputs.append((boxes[way], box[0], shape[0]))
                box[0] += shape[0]

    def kernel(place_ref, *refs):
        ins, outs, scratch = refs[: len(arrays)], refs[len(arrays) : len(arrays) + len(shapes)], refs[len(arrays) + len(shapes) :]
        where, made = list(places), list(outputs)
        for task in tasks:
            sources = [rows_of(ins[where.pop(0)], v) for v in task.inputs]
            targets = []
            for _ in task.outputs:
                k, at, rows = made.pop(0)
                targets.append(outs[k] if rows == shapes[k][0] else outs[k].at[at : at + rows])
            task.run(place_ref, *sources, *targets, *scratch[: len(task.scratch)])
            scratch = scratch[len(task.scratch) :]

    results = pl.pallas_call(
        kernel,
        in_specs=[SCALARS] + [ON_CHIP] * len(arrays),
        out_specs=[ON_CHIP] * len(shapes),
        out_shape=[jax.ShapeDtypeStruct(tuple(shape), BF16) for shape in shapes],
        scratch_shapes=[pltpu.VMEM(shape, BF16) for t in tasks for shape in t.scratch],
        compiler_params=params(16),
        cost_estimate=BRIEF,
        name="step",
    )(place, *arrays)
    made = [View(results[k], at, rows) for k, at, rows in outputs]
    grouped = []
    for task in tasks:
        grouped.append(made[: len(task.outputs)])
        made = made[len(task.outputs) :]
    return grouped


def add_task(a, b, way=None):
    def run(place, x, y, total):
        total[...] = x[...] + y[...]

    return Task(run, (a, b), [(view(a).shape, way)])


HALVES, WHOLE, GATHER = range(3)
FIVE = [(0, HALVES), (1, HALVES), (2, WHOLE), (1, GATHER), (0, GATHER)]
FOUR = [(0, HALVES), (1, WHOLE), (2, WHOLE), (0, GATHER)]
THREE = [(0, WHOLE), (1, WHOLE), (2, WHOLE)]


class BankTotal:
    def __init__(self, sent, kept, plan):
        self.sent, self.kept, self.plan, self.stage = view(sent), view(kept), plan, 0

    @property
    def done(self):
        return self.stage == len(self.plan)

    def way(self, stage):
        return ("bank", 1 << self.plan[stage][0])

    def arrival(self, other):
        (bit, kind), (size, width) = self.plan[self.stage], self.kept.shape
        last = self.stage + 1 == len(self.plan)
        if last and kind == GATHER:
            return None
        way = None if last else self.way(self.stage + 1)
        if kind == GATHER:

            def gather(place, mine, other, joined):
                join(place, bit, mine, other, joined)

            return Task(gather, (self.kept, other), [((2 * size, width), way)])
        if last or self.plan[self.stage + 1][1] != HALVES:
            return add_task(self.kept, other, way)
        next_bit = self.plan[self.stage + 1][0]

        def add(place, kept, other, sent, left, total):
            total[...] = kept[...] + other[...]
            halves(place, next_bit, total, sent, left)

        half = (size // 2, width)
        return Task(add, (self.kept, other), [(half, way), half], [(size, width)])

    def land(self, other, results):
        if results is None:
            self.other = other
        else:
            self.sent, self.kept = results[0], results[-1]
            if self.plan[self.stage] == (2, WHOLE):
                self.sent = self.kept = beyond(self.kept)
        self.stage += 1


def beyond(value):
    size = lax.axis_size("bank")
    if size == 8:
        return value
    own = lax.slice_in_dim(value.array, value.at, value.at + value.rows)
    return View(lax.psum(own, "bank", axis_index_groups=[list(range(k, size, 8)) for k in range(8)]))


def join(place, bit, mine, other, joined):
    size = mine.shape[0]
    at = place[4 + bit]
    joined[pl.ds(pl.multiple_of(at * size, 16), size), :] = mine[...]
    joined[pl.ds(pl.multiple_of((1 - at) * size, 16), size), :] = other[...]


def emit(place, run, inputs, outputs, scratch, name):
    arrays, places = distinct(inputs)

    def kernel(place_ref, *refs):
        sources = [rows_of(refs[k], v) for k, v in zip(places, inputs)]
        run(place_ref, *sources, *refs[len(arrays) :])

    return pl.pallas_call(
        kernel,
        in_specs=[SCALARS] + [ON_CHIP] * len(arrays),
        out_specs=[ON_CHIP] * len(outputs),
        out_shape=[jax.ShapeDtypeStruct(shape, F32) for shape in outputs],
        scratch_shapes=[pltpu.VMEM(shape, BF16) for shape in scratch],
        compiler_params=params(20),
        cost_estimate=BRIEF,
        name=name,
    )(place, *arrays)


def emit_small(place, flow_a, flow_b, out, att, classes):
    piece = att // 4
    rows = 2 * att + 128

    def run(place, a, other_a, b, other_b, dquery, dkey, dvalue, doutput, dclass, first, second):
        join(place, 0, a, other_a, first)
        join(place, 0, b, other_b, second)
        for source, row, target in ((first, 0, dquery), (first, att, dkey), (second, 0, dvalue)):
            for k in range(out // att):
                block = source[row + k * piece : row + (k + 1) * piece, :].astype(F32)
                target[k * att : (k + 1) * att, :] = block.T
        doutput[...] = second[att : 2 * att, :].astype(F32)
        dclass[:, :att] = first[2 * att :, :].astype(F32)[:classes]
        dclass[:, att:] = second[2 * att :, :].astype(F32)[:classes]

    return emit(
        place,
        run,
        (flow_a.kept, flow_a.other, flow_b.kept, flow_b.other),
        [(out, piece)] * 3 + [(att, att), (classes, 2 * att)],
        [(rows, att)] * 2,
        "emit_small",
    )


def emit_wide(place, flow_a, flow_b, width_in, mid, tile):
    half = (width_in + mid) // 2

    def run(place, a, other_a, b, other_b, shortcut, expand, joined):
        join(place, 0, a, other_a, joined.at[:half])
        join(place, 0, b, other_b, joined.at[half:])
        shortcut[...] = joined[:width_in, :].astype(F32)
        expand[...] = joined[width_in:, :].astype(F32)

    inputs = (flow_a.kept, flow_a.other, flow_b.kept, flow_b.other)
    shapes = [(width_in, tile), (mid, tile)]
    return emit(place, run, inputs, shapes, [(width_in + mid, tile)], "emit_wide")


def emit_spatial(place, flow_a, flow_b, mid):
    quarter = mid // 4
    rows_a, rows_b = 2 * flow_a.kept.rows, 2 * flow_b.kept.rows

    def run(place, a, other_a, b, other_b, spatial, joined):
        join(place, 0, a, other_a, joined.at[:rows_a])
        join(place, 0, b, other_b, joined.at[rows_a:])
        for tap in range(9):
            for k in range(4):
                spatial[tap, k * quarter : (k + 1) * quarter, :] = joined[
                    tap * quarter : (tap + 1) * quarter, k * quarter : (k + 1) * quarter
                ].astype(F32)

    inputs = (flow_a.kept, flow_a.other, flow_b.kept, flow_b.other)
    return emit(place, run, inputs, [(9, mid, quarter)], [(rows_a + rows_b, mid)], "emit_spatial")[0]


def emit_last(place, flow, width_in, mid, tile, classes):
    quarter = mid // 4

    def run(place, joined, reduce, *targets):
        for k in range(2):
            reduce[k * mid : (k + 1) * mid, :] = joined[k * quarter : (k + 1) * quarter, :].astype(F32).T
        tail = joined[2 * quarter : 2 * quarter + 16, :].astype(F32)
        for k in range(4):
            targets[k][...] = tail[0:1, k * quarter : (k + 1) * quarter]
        for k in range(2):
            targets[4 + k][...] = tail[1:2, k * quarter : (k + 1) * quarter]
        targets[6][...] = tail[1:2, 2 * quarter : 2 * quarter + classes]
        for k in range(4):
            targets[7 + k][...] = tail[2 + k : 3 + k, :]

    shapes = [(width_in, quarter)] + [(1, quarter)] * 6 + [(1, classes)] + [(1, tile)] * 4
    return emit(place, run, (flow.kept,), shapes, [], "emit_last")


def move(value, how):
    kind, by = how
    if kind == "along":
        axis = ("bank", "box")
        size = lax.axis_size(axis)
        return lax.ppermute(value, axis, [(i, i + by) for i in range(size) if 0 <= i + by < size])
    return lax.ppermute(value, kind, [(i, i ^ by) for i in range(lax.axis_size(kind))])


def launch(moves):
    found, received = [], []
    for value, how in moves:
        same = [r for v, h, r in found if v is value.array and h == how]
        if not same:
            same = [move(value.array, how)]
            found.append((value.array, how, same[0]))
        received.append(value.of(same[0]))
    return received


def slot(place, kernel, inputs, moves=(), flows=(), tasks=None):
    flows = [flow for flow in flows if not flow.done]
    moves = [(view(value), how) for value, how in moves] + [(flow.sent, flow.way(flow.stage)) for flow in flows]
    arrays, places = distinct([value for value, _ in moves])
    inputs, arrays = lax.optimization_barrier((inputs, arrays))
    received = launch([(value.of(arrays[k]), how) for k, (value, how) in zip(places, moves)])
    results = kernel(*inputs) if kernel else ()
    arrays, places = distinct(received)
    results, arrays = lax.optimization_barrier((results, arrays))
    received = [v.of(arrays[k]) for v, k in zip(received, places)]
    count = len(moves) - len(flows)
    arrivals, landed = received[:count], received[count:]
    own = tasks(results, arrivals) if tasks else []
    pending = [flow.arrival(other) for flow, other in zip(flows, landed)]
    needed = own + [task for task in pending if task]
    outputs = step(place, needed) if needed else []
    made, outputs = outputs[: len(own)], outputs[len(own) :]
    for flow, task, other in zip(flows, pending, landed):
        flow.land(other, outputs.pop(0) if task else None)
    return results, arrivals, made


def local(
    roi_features,
    box_seconds,
    video_lengths,
    bank_features,
    reduce_weight,
    reduce_gain,
    reduce_shift,
    spatial_weight,
    spatial_gain,
    spatial_shift,
    expand_weight,
    expand_gain,
    expand_shift,
    shortcut_weight,
    shortcut_gain,
    shortcut_shift,
    query_weight,
    key_weight,
    value_weight,
    norm_gain,
    norm_shift,
    output_weight,
    output_bias,
    class_weight,
    class_bias,
    logit_cotangent,
):
    boxes, grid_side = roi_features.shape[:2]
    in_width = roi_features.shape[3]
    rows = boxes * grid_side * grid_side
    mid = reduce_weight.shape[1]
    out = expand_weight.shape[1]
    att = query_weight.shape[1]
    classes = class_weight.shape[1]
    tile, quarter = out // 4, mid // 4
    all_seconds = lax.axis_size(("bank", "box")) * SEC_DEV
    my_index = lax.axis_index(("bank", "box"))
    bank_index, box_index = lax.axis_index("bank"), lax.axis_index("box")
    core, side = box_index % 2, box_index // 2
    place = jnp.stack([my_index, box_index, side, core] + [(bank_index >> k) & 1 for k in range(3)])
    order = jnp.stack([(1 - side) * 2 + 1 - core, (1 - side) * 2 + core, side * 2 + 1 - core, side * 2 + core])
    shape = dict(grid_side=grid_side, boxes=boxes)
    on = functools.partial(slot, place)

    roi = roi_features.transpose(1, 2, 0, 3).reshape(rows, in_width)
    w9 = spatial_weight.reshape(9, mid, mid)
    place, order, roi = lax.optimization_barrier((place, order, roi))
    def bank_sides(results, arrivals):
        def run(place, own, far, first, last):
            lower = place[2] == 0
            first[...] = jnp.where(lower, own[...], far[...])
            last[...] = jnp.where(lower, far[...], own[...])

        return [Task(run, (bank_features, arrivals[-1]), [bank_features.shape] * 2)]

    results, _, ((bank_first, bank_last),) = on(
        functools.partial(trunk, **shape),
        (
            roi, reduce_weight, w9, bank_features, key_weight, value_weight,
            reduce_gain, reduce_shift, spatial_gain, spatial_shift, norm_gain, norm_shift,
            expand_gain, expand_shift, shortcut_gain, shortcut_shift, output_bias, class_bias,
        ),
        [(bank_features, ("box", 2))],
        tasks=bank_sides,
    )
    roi, x1, hidden, x2, middle, inv_mid, own_window, mid_vectors, vectors, class_bias = results
    around = [by for by in range(-REACH, REACH + 1) if by != 0]
    box_devices = lax.axis_size("box")

    def bundle(results, arrivals):
        def run(place, before, first, last, after, blocks):
            size = first.shape[0]
            for k, block in enumerate((before, first, last, after)):
                blocks[k * size : (k + 1) * size, :] = block[...]

        size, width = bank_first.shape
        return [Task(run, (arrivals[-2], bank_first, bank_last, arrivals[-1]), [(4 * size, width)])]

    (*xs, inv_out, feature), (*windows, _, _), ((pair_bank,),) = on(
        functools.partial(widen, **shape),
        (order, roi, middle, shortcut_weight, expand_weight, vectors),
        [(own_window, ("along", -by)) for by in around]
        + [(bank_last, ("along", box_devices)), (bank_first, ("along", -box_devices))],
        tasks=bundle,
    )
    windows = [w.array for w in windows]
    windows.insert(REACH, own_window)
    (logits, dfeature, pack, norm_sums, bias_sums, class_sums), (far_bank,), _ = on(
        functools.partial(head, all_seconds=all_seconds),
        (
            place, box_seconds, video_lengths, feature, windows, query_weight, output_weight, class_weight.T,
            mid_vectors, vectors, class_bias, logit_cotangent,
        ),
        [(pair_bank, ("box", 1))],
    )

    def narrow_slot(ks, before, *rest, **more):
        operands = (order, roi, middle, inv_out, vectors, dfeature, expand_weight)
        operands += tuple(xs[2 * ks[0] : 2 * ks[-1] + 2]) + before
        return on(functools.partial(narrow, ks=ks, **shape), operands, *rest, **more)

    def pack_pair(results, arrivals):
        def run(place, pack, far_pack, both):
            size = pack.shape[0]
            both[pl.ds(pl.multiple_of(place[2] * size, 16), size), :] = pack[...]
            both[pl.ds(pl.multiple_of((1 - place[2]) * size, 16), size), :] = far_pack[...]

        size, width = pack.shape
        return [Task(run, (pack, arrivals[0]), [(2 * size, width)])]

    (dmiddle, away_far, d0, sums0, keep_far, d1, sums1), _, ((pair_pack,),) = narrow_slot(
        (0, 1), (), [(pack, ("box", 2))], tasks=pack_pair
    )
    half = away_far.shape[0] // 2

    def wide_parts(results, arrivals):
        def run(place, keep, away, first, second):
            first[...] = keep[:half, :] + away[:half, :]
            second[...] = keep[half:, :] + away[half:, :]

        return [Task(run, (keep_far, arrivals[1]), [(half, tile)] * 2)]

    (dmiddle, away_near, d2, sums2), (far_pair, _), ((wide_first, wide_last),) = narrow_slot(
        (2,), (dmiddle,), [(pair_pack, ("box", 1)), (away_far, ("box", 1))], tasks=wide_parts
    )
    gathered = [v.array for v in (pair_pack, far_pair, pair_bank, far_bank)]
    sent_a, kept_a, sent_b, kept_b = small_weights(place, *gathered, att, box_devices)
    small_a, small_b = BankTotal(sent_a, kept_a, FIVE), BankTotal(sent_b, kept_b, FIVE)
    small = [small_a, small_b]
    (keep_near, d3, sums3, away_taps, keep_far_taps, dconv, dflat, spatial_sums), (near, far_first), _ = on(
        functools.partial(spatial_far, **shape),
        (
            order, place, roi, middle, inv_out, vectors, dfeature, expand_weight, xs[6], xs[7], dmiddle,
            x2, hidden, inv_mid, mid_vectors,
        ),
        [(away_near, ("box", 1)), (wide_first, ("box", 2))],
        [small_a],
    )

    def summed_halves(keep, away, far, at):
        rows = far.shape[0]

        def run(place, keep, away, far, sent, kept, total):
            total[...] = keep[at : at + rows, :] + away[at : at + rows, :] + far[...]
            halves(place, 0, total, sent, kept)

        size = (rows // 2, mid)
        return Task(run, (keep, away, far), [(size, ("bank", 1)), size], [(rows, mid)])

    cut = 5 * quarter

    def tap_parts(results, arrivals):
        def run(place, keep, away, first, second):
            first[...] = keep[:cut, :] + away[:cut, :]
            second[...] = keep[cut:, :] + away[cut:, :]

        size, way = keep_far_taps.shape[0], ("box", 2)
        return [
            summed_halves(keep_near, near, far_first, 0),
            summed_halves(keep_near, near, arrivals[1], half),
            Task(run, (keep_far_taps, arrivals[0]), [((cut, mid), way), (size - cut, mid)]),
        ]

    (away_taps, keep_taps), _, (wide_a, wide_b, (taps_first, taps_last)) = on(
        functools.partial(spatial_near, grid_side=grid_side),
        (place, hidden, dflat),
        [(away_taps, ("box", 1)), (wide_last, ("box", 2))],
        small,
        tasks=tap_parts,
    )
    wide = [BankTotal(*wide_a, FIVE), BankTotal(*wide_b, FIVE)]
    (dreduced, last_away, last_keep), (near_taps, _), (spatial_a,) = on(
        functools.partial(reduce_back, **shape),
        (
            order, dconv, x1, roi, w9, inv_mid, mid_vectors, spatial_sums, norm_sums, bias_sums, class_sums,
            sums0, sums1, sums2, sums3,
        ),
        [(away_taps, ("box", 1)), (taps_first, ("box", 2))],
        small + wide,
        tasks=lambda results, arrivals: [summed_halves(keep_taps, *arrivals, 0)],
    )
    spatial = [BankTotal(*spatial_a, FIVE)]
    dprojected = (d0, d1, d2, d3)

    def last_sides(results, arrivals):
        def run(place, keep, away, far, near):
            size = far.shape[0]
            far[...] = keep[:size, :] + away[:size, :]
            near[...] = keep[size:, :] + away[size:, :]

        return [
            summed_halves(keep_taps, near_taps, arrivals[0], cut),
            Task(run, (last_keep, arrivals[1]), [(last_keep.shape[0] // 2, mid)] * 2),
        ]

    roi_gradient, _, (spatial_b, (last_out, last_near)) = on(
        functools.partial(roi_back, half=0),
        (order, dreduced, dprojected, reduce_weight, shortcut_weight),
        [(taps_last, ("box", 2)), (last_away, ("box", 1))],
        small + wide + spatial,
        tasks=last_sides,
    )
    spatial.append(BankTotal(*spatial_b, FOUR))
    roi_gradient, _, ((last_total,),) = on(
        functools.partial(roi_back, half=1),
        (order, dreduced, dprojected, reduce_weight, shortcut_weight, roi_gradient),
        [(last_out, ("box", 2))],
        small + wide + spatial,
        tasks=lambda results, arrivals: [add_task(last_near, arrivals[0], ("bank", 1))],
    )
    last = BankTotal(last_total, last_total, THREE)
    flows = small + wide + spatial + [last]
    on(None, (), (), flows)
    on(None, (), (), flows)
    while any(not flow.done for flow in flows):
        on(None, (), (), flows)

    query_g, key_g, value_g, output_g, class_g = emit_small(place, *small, out, att, classes)
    shortcut_g, expand_g = emit_wide(place, *wide, in_width, mid, tile)
    spatial_g = emit_spatial(place, *spatial, mid)
    reduce_g, *sums = emit_last(place, last, in_width, mid, tile, classes)
    (
        reduce_gain_g, reduce_shift_g, spatial_gain_g, spatial_shift_g, norm_gain_g, norm_shift_g, class_bias_g,
        expand_gain_g, expand_shift_g, shortcut_gain_g, bias_g,
    ) = [v.reshape(v.shape[1]) for v in sums]
    return (
        logits,
        roi_gradient.reshape(grid_side, grid_side, boxes, in_width).transpose(2, 0, 1, 3),
        reduce_g,
        reduce_gain_g,
        reduce_shift_g,
        spatial_g.reshape(3, 3, mid, quarter),
        spatial_gain_g,
        spatial_shift_g,
        expand_g,
        expand_gain_g,
        expand_shift_g,
        shortcut_g,
        shortcut_gain_g,
        expand_shift_g,
        query_g,
        key_g,
        value_g,
        norm_gain_g,
        norm_shift_g,
        output_g,
        bias_g,
        class_g.T,
        class_bias_g,
    )


def solution(mesh):
    split = ("bank", "box")
    in_specs = (P(split), P(split), P(), P(split)) + (P(),) * 21 + (P(split),)
    column, vector = P(None, "box"), P("box")
    out_specs = (
        P(split),
        P(split),
        column,
        vector,
        vector,
        P(None, None, None, "box"),
        vector,
        vector,
        column,
        vector,
        vector,
        column,
        vector,
        vector,
        column,
        column,
        column,
        vector,
        vector,
        column,
        vector,
        P("box", None),
        P(),
    )
    return jax.shard_map(local, mesh=mesh, in_specs=in_specs, out_specs=out_specs, check_vma=False)
```

```python
import functools
import jax
import jax.numpy as jnp
from jax import lax
from jax.experimental import pallas as pl
from jax.experimental.pallas import tpu as pltpu
from jax.sharding import PartitionSpec as P

HALF = 30
PER_SEC = 8
SEC_DEV = 16
REACH = 2
EPSILON = 1e-05
MIB = 2**20
F32, BF16 = jnp.float32, jnp.bfloat16
BRIEF = pl.CostEstimate(flops=1, bytes_accessed=1, transcendentals=0)
ON_CHIP = pl.BlockSpec(memory_space=pltpu.VMEM)
SCALARS = pl.BlockSpec(memory_space=pltpu.SMEM)
FAR = pl.BlockSpec(memory_space=pl.ANY)
OVER_ROWS = (((0,), (0,)), ((), ()))
OVER_COLUMNS = (((1,), (1,)), ((), ()))


def plain(a, b):
    return jnp.dot(a, b, preferred_element_type=F32)


def over_rows(a, b):
    return lax.dot_general(a, b, OVER_ROWS, preferred_element_type=F32)


def over_columns(a, b):
    return lax.dot_general(a, b, OVER_COLUMNS, preferred_element_type=F32)


def params(mebibytes):
    return pltpu.CompilerParams(vmem_limit_bytes=mebibytes * MIB)


def kept(*arrays):
    return [pltpu.with_memory_space_constraint(v, pltpu.VMEM) for v in arrays]


def outside(*arrays):
    return [pltpu.with_memory_space_constraint(v, pltpu.HBM) for v in arrays]


def start_copies(pairs, sems):
    copies = [pltpu.make_async_copy(source, target, sems.at[k]) for k, (source, target) in enumerate(pairs)]
    for copy in copies:
        copy.start()
    return copies


def fold(values):
    values = values.astype(F32)
    return jnp.sum(values.reshape(values.shape[0] // 8, 8, values.shape[1]), axis=0)


def total_rows(values):
    return jnp.sum(values, axis=0, keepdims=True)


def centre(acc, centred, grid_side, boxes):
    rows, width = acc.shape
    step = grid_side * boxes
    first = acc[0:step, :]
    shift = total_rows(jnp.sum(first.reshape(step // 8, 8, width), axis=0)) / step

    def line(k, carry):
        total, square = carry
        sums = squares = None
        for w in range(grid_side):
            at = pl.ds((k * grid_side + w) * boxes, boxes)
            value = (acc[at, :] - shift).astype(BF16)
            centred[at, :] = value
            sums = value if sums is None else sums + value
            squares = value * value if squares is None else squares + value * value
        return total + fold(sums), square + fold(squares)

    zero = jnp.zeros((8, width), F32)
    total, square = lax.fori_loop(0, grid_side, line, (zero, zero), unroll=True)
    offset = total_rows(total) / rows
    var = total_rows(square) / rows - offset * offset
    return lax.rsqrt(jnp.maximum(var, 0.0) + EPSILON), offset, shift


def scaled(inv, offset, gain, shift):
    factor = 0.5 * gain * inv
    return factor, 0.5 * shift - factor * offset


def input_gradient(inv, offset, gain, total, total_c, rows):
    gain_gradient = inv * (total_c - offset * total)
    of_upstream = inv * gain
    of_centred = -of_upstream * inv * gain_gradient / rows
    term = -of_upstream * total / rows - of_centred * offset
    return of_upstream, of_centred, term, gain_gradient


def clear_border(padded):
    side, _, boxes, width = padded.shape
    zeros = jnp.zeros((boxes, width), BF16)
    for k in range(side):
        padded[0, k] = zeros
        padded[side - 1, k] = zeros
        padded[k, 0] = zeros
        padded[k, side - 1] = zeros


def by_cells(grid_side, boxes, body, carry):
    def line(k, carry):
        for w in range(grid_side):
            carry = body(k, w, pl.ds((k * grid_side + w) * boxes, boxes), carry)
        return carry

    return lax.fori_loop(0, grid_side, line, carry)


def trunk_kernel(
    grid_side, boxes, roi_far, wr_far, w9_far, bank_far, kw_far, vw_far, *rest
):
    far_vectors, rest = rest[:12], rest[12:]
    roi, x1, hidden, x2, middle, inv, window, vectors, wide_vectors, class_bias = rest[:10]
    wr, w9, bank, kw, vw, acc, sems = rest[10:17]
    near_vectors = rest[17:]
    copies = start_copies(
        [(roi_far, roi), (wr_far, wr), (w9_far, w9), (bank_far, bank), (kw_far, kw), (vw_far, vw)]
        + list(zip(far_vectors, near_vectors)),
        sems,
    )
    clear_border(hidden)
    for k, copy in enumerate(copies[6:]):
        copy.wait()
        value = near_vectors[k][...].astype(F32)
        value = value.reshape(1, value.shape[0])
        if k < 6:
            vectors[k : k + 1, :] = value
        elif k < 11:
            wide_vectors[k - 6 : k - 5, :] = value
        else:
            class_bias[...] = value
    copies[0].wait()
    copies[1].wait()
    acc[...] = plain(roi[...], wr[...])
    inv1, offset1, base = centre(acc, x1, grid_side, boxes)
    inv[0:1, :], inv[1:2, :] = inv1, offset1
    factor, term = scaled(inv1, base + offset1, vectors[0:1, :], vectors[1:2, :])

    def first(k, w, rows, carry):
        h = acc[rows, :] * factor + term
        hidden[k + 1, w + 1] = (h + h * jnp.tanh(h)).astype(BF16)
        return carry

    by_cells(grid_side, boxes, first, 0)
    copies[2].wait()
    for p in range(3):
        for q in range(3):
            taps = hidden[p : p + grid_side, q : q + grid_side].reshape(acc.shape)
            product = plain(taps, w9[p * 3 + q])
            if p + q == 0:
                acc[...] = product
            else:
                acc[...] += product
    inv2, offset2, base2 = centre(acc, x2, grid_side, boxes)
    inv[2:3, :], inv[3:4, :] = inv2, offset2
    factor2, term2 = scaled(inv2, base2 + offset2, vectors[2:3, :], vectors[3:4, :])

    def second(k, w, rows, carry):
        h = acc[rows, :] * factor2 + term2
        middle[rows, :] = (h + h * jnp.tanh(h)).astype(BF16)
        return carry

    by_cells(grid_side, boxes, second, 0)
    for copy in copies[3:6]:
        copy.wait()
    att = kw.shape[1]
    window[:, :att] = plain(bank[...], kw[...]).astype(BF16)
    window[:, att:] = plain(bank[...], vw[...]).astype(BF16)


def trunk(roi, wr, w9, bank, kw, vw, *vectors, grid_side, boxes):
    rows, mid = roi.shape[0], wr.shape[1]
    side = grid_side + 2
    return pl.pallas_call(
        functools.partial(trunk_kernel, grid_side, boxes),
        in_specs=[FAR] * 18,
        out_specs=[ON_CHIP] * 10,
        out_shape=[
            pltpu.VMEM(roi.shape, BF16),
            pltpu.VMEM((rows, mid), BF16),
            pltpu.VMEM((side, side, boxes, mid), BF16),
            pltpu.VMEM((rows, mid), BF16),
            pltpu.VMEM((rows, mid), BF16),
            jax.ShapeDtypeStruct((4, mid), F32),
            jax.ShapeDtypeStruct((bank.shape[0], 2 * kw.shape[1]), BF16),
            jax.ShapeDtypeStruct((6, mid), F32),
            jax.ShapeDtypeStruct((5, vectors[6].shape[0]), F32),
            jax.ShapeDtypeStruct((1, vectors[11].shape[0]), F32),
        ],
        scratch_shapes=[pltpu.VMEM(v.shape, BF16) for v in (wr, w9, bank, kw, vw)]
        + [pltpu.VMEM((rows, mid), F32), pltpu.SemaphoreType.DMA((18,))]
        + [pltpu.VMEM(v.shape, BF16) for v in vectors],
        compiler_params=params(18),
        cost_estimate=BRIEF,
        name="trunk",
    )(*outside(roi, wr, w9, bank, kw, vw, *vectors))


def widen_kernel(grid_side, boxes, order, roi, middle, ws_far, we_far, vectors, *rest):
    xs, (inv, feature, ws, we, acc_e, acc_p, sems) = rest[:8], rest[8:]
    width = acc_e.shape[1]
    at = [pl.ds(pl.multiple_of(order[k] * width, width), width) for k in range(4)]
    copies = start_copies(
        [pair for k in range(4) for pair in ((ws_far.at[:, at[k]], ws.at[k]), (we_far.at[:, at[k]], we.at[k]))],
        sems,
    )
    for k in range(4):
        xe, xp = xs[2 * k], xs[2 * k + 1]
        copies[2 * k].wait()
        acc_p[...] = plain(roi[...], ws[k])
        copies[2 * k + 1].wait()
        acc_e[...] = plain(middle[...], we[k])
        inv_p, offset_p, base_p = centre(acc_p, xp, grid_side, boxes)
        inv_e, offset_e, base_e = centre(acc_e, xe, grid_side, boxes)
        for row, value in enumerate((inv_e, inv_p, offset_e, offset_p)):
            inv[k, row : row + 1, :] = value
        factor_e, term_e = scaled(inv_e, base_e + offset_e, vectors[0:1, at[k]], vectors[1:2, at[k]])
        factor_p, term_p = scaled(inv_p, base_p + offset_p, vectors[2:3, at[k]], vectors[3:4, at[k]])
        term = term_e + term_p

        def line(row, total):
            for w in range(grid_side):
                rows = pl.ds((row * grid_side + w) * boxes, boxes)
                h = acc_e[rows, :] * factor_e + acc_p[rows, :] * factor_p + term
                total = total + (h + h * jnp.tanh(h))
            return total

        total = lax.fori_loop(0, grid_side, line, jnp.zeros((boxes, width), F32))
        feature[:, at[k]] = total / (grid_side * grid_side)


def widen(order, roi, middle, ws, we, vectors, grid_side, boxes):
    rows, width_in = roi.shape
    mid, out = we.shape
    tile = out // 4
    return pl.pallas_call(
        functools.partial(widen_kernel, grid_side, boxes),
        in_specs=[SCALARS, ON_CHIP, ON_CHIP, FAR, FAR, ON_CHIP],
        out_specs=[ON_CHIP] * 10,
        out_shape=[pltpu.VMEM((rows, tile), BF16)] * 8
        + [jax.ShapeDtypeStruct((4, 4, tile), F32), jax.ShapeDtypeStruct((boxes, out), F32)],
        scratch_shapes=[
            pltpu.VMEM((4, width_in, tile), BF16),
            pltpu.VMEM((4, mid, tile), BF16),
            pltpu.VMEM((rows, tile), F32),
            pltpu.VMEM((rows, tile), F32),
            pltpu.SemaphoreType.DMA((8,)),
        ],
        compiler_params=params(18),
        cost_estimate=BRIEF,
        name="widen",
    )(order, *kept(roi, middle), *outside(ws, we), vectors)


def doubled_slope(h):
    t = jnp.tanh(h)
    return (1.0 + t) * (1.0 + h * (1.0 - t))


def narrow_part(
    grid_side, boxes, k, order, roi, middle, xe, xp, we, inv, vectors, dfeature, part, dprojected, sums,
    upstream, dexpanded,
):
    rows, width = upstream.shape
    columns = pl.ds(pl.multiple_of(order[k] * width, width), width)
    gain_e, gain_p = vectors[0:1, columns], vectors[2:3, columns]
    inv_e, inv_p, offset_e, offset_p = [inv[k, row : row + 1, :] for row in range(4)]
    factor_e, term_e = scaled(inv_e, offset_e, gain_e, vectors[1:2, columns])
    factor_p, term_p = scaled(inv_p, offset_p, gain_p, vectors[3:4, columns])
    term = term_e + term_p
    slope_scale = dfeature[:, columns] * (0.5 / (grid_side * grid_side))

    def line(row, carry):
        sums = None
        for w in range(grid_side):
            at = pl.ds((row * grid_side + w) * boxes, boxes)
            e, p = xe[at, :].astype(F32), xp[at, :].astype(F32)
            u = doubled_slope(e * factor_e + p * factor_p + term) * slope_scale
            upstream[at, :] = u
            new = (u, u * e, u * p)
            sums = new if sums is None else [a + b for a, b in zip(sums, new)]
        return [a + fold(b) for a, b in zip(carry, sums)]

    zero = jnp.zeros((8, width), F32)
    total, total_e, total_p = [total_rows(v) for v in lax.fori_loop(0, grid_side, line, [zero] * 3)]
    ue, ce, te, gain_gradient_e = input_gradient(inv_e, offset_e, gain_e, total, total_e, rows)
    up, cp, tp, gain_gradient_p = input_gradient(inv_p, offset_p, gain_p, total, total_p, rows)
    sums[0:1, :] = gain_gradient_e
    sums[1:2, :] = total
    sums[2:3, :] = gain_gradient_p

    def second(row, w, at, carry):
        u = upstream[at, :]
        dexpanded[at, :] = (u * ue + xe[at, :].astype(F32) * ce + te).astype(BF16)
        dprojected[at, :] = (u * up + xp[at, :].astype(F32) * cp + tp).astype(BF16)
        return carry

    by_cells(grid_side, boxes, second, 0)
    split = roi.shape[1]
    part[0:split, :] = over_rows(roi[...], dprojected[...]).astype(BF16)
    part[split:, :] = over_rows(middle[...], dexpanded[...]).astype(BF16)
    return over_columns(dexpanded[...], we[...])


def expand_columns(order, ks, we_far, we, sems):
    width = we.shape[2]
    columns = [pl.ds(pl.multiple_of(order[k] * width, width), width) for k in ks]
    return start_copies([(we_far.at[:, at], we.at[n]) for n, at in enumerate(columns)], sems)


def narrow_kernel(grid_side, boxes, ks, order, roi, middle, inv, vectors, dfeature, we_far, *rest):
    count = len(ks)
    xs, rest = rest[: 2 * count], rest[2 * count :]
    *before, dmiddle = rest[: -4 - 3 * count]
    outs, (we, upstream, dexpanded, sems) = rest[-4 - 3 * count : -4], rest[-4:]
    copies = expand_columns(order, ks, we_far, we, sems)
    for n, k in enumerate(ks):
        copies[n].wait()
        back = narrow_part(
            grid_side, boxes, k, order, roi, middle, xs[2 * n], xs[2 * n + 1], we.at[n], inv, vectors, dfeature,
            *outs[3 * n : 3 * n + 3], upstream, dexpanded,
        )
        if n == 0:
            dmiddle[...] = before[0][...] + back if before else back
        else:
            dmiddle[...] += back


def narrow(order, roi, middle, inv, vectors, dfeature, we, *rest, ks, grid_side, boxes):
    rows, width_in = roi.shape
    mid, out = we.shape
    tile = out // 4
    xs, before = rest[: 2 * len(ks)], rest[2 * len(ks) :]
    return pl.pallas_call(
        functools.partial(narrow_kernel, grid_side, boxes, ks),
        in_specs=[SCALARS] + [ON_CHIP] * 5 + [FAR] + [ON_CHIP] * len(rest),
        out_specs=[ON_CHIP] * (1 + 3 * len(ks)),
        out_shape=[pltpu.VMEM((rows, mid), F32)]
        + [
            jax.ShapeDtypeStruct((width_in + mid, tile), BF16),
            pltpu.VMEM((rows, tile), BF16),
            jax.ShapeDtypeStruct((3, tile), F32),
        ]
        * len(ks),
        input_output_aliases={7 + 2 * len(ks): 0} if before else {},
        scratch_shapes=[
            pltpu.VMEM((len(ks), mid, tile), BF16),
            pltpu.VMEM((rows, tile), F32),
            pltpu.VMEM((rows, tile), BF16),
            pltpu.SemaphoreType.DMA((len(ks),)),
        ],
        compiler_params=params(16),
        cost_estimate=BRIEF,
        name="narrow",
    )(order, *kept(roi, middle), inv, vectors, dfeature, *outside(we), *kept(*xs, *before))


def norm_back(grid_side, boxes, upstream, centred, inv, offset, gain, shift, low, sums, store):
    rows, width = upstream.shape
    factor, term = scaled(inv, offset, gain, shift)

    def line(row, carry):
        sums = None
        for w in range(grid_side):
            at = pl.ds((row * grid_side + w) * boxes, boxes)
            c = centred[at, :].astype(F32)
            u = doubled_slope(c * factor + term) * (0.5 * upstream[at, :])
            low[at, :] = u
            new = (u, u * c)
            sums = new if sums is None else [a + b for a, b in zip(sums, new)]
        return [a + fold(b) for a, b in zip(carry, sums)]

    zero = jnp.zeros((8, width), F32)
    total, total_c = [total_rows(v) for v in lax.fori_loop(0, grid_side, line, [zero] * 2)]
    of_upstream, of_centred, term, gain_gradient = input_gradient(inv, offset, gain, total, total_c, rows)
    sums[0:1, :] = gain_gradient
    sums[1:2, :] = total

    def second(row, w, at, carry):
        value = low[at, :] * of_upstream + centred[at, :].astype(F32) * of_centred + term
        store(row, w, at, value.astype(BF16))
        return carry

    by_cells(grid_side, boxes, second, 0)


def spatial_taps(grid_side, side, core, hidden, dflat, part, away, keep):
    rows, width = dflat.shape
    half, quarter = width // 2, width // 4
    mine = pl.ds(pl.multiple_of(core * quarter, quarter), quarter)
    other = pl.ds(pl.multiple_of((1 - core) * quarter, quarter), quarter)
    columns = dflat[:, pl.ds(pl.multiple_of(side * half, half), half)]
    for p in range(3):
        for q in range(3):
            taps = hidden[p : p + grid_side, q : q + grid_side].reshape(rows, width)
            part[...] = over_rows(taps, columns).astype(BF16)
            lines = slice((p * 3 + q) * quarter, (p * 3 + q + 1) * quarter)
            for k in range(4):
                lanes = slice(k * quarter, (k + 1) * quarter)
                keep[lines, lanes] = part[lanes, mine]
                away[lines, lanes] = part[lanes, other]


def spatial_far_kernel(
    grid_side, boxes, order, place, roi, middle, inv_out, wide_vectors, dfeature, we_far, xe, xp, before,
    x2, hidden, inv, vectors, part, dprojected, wide_sums, away, keep, dconv, dflat, sums,
    we, upstream, dexpanded, taps, sems,
):
    copies = expand_columns(order, (3,), we_far, we, sems)
    clear_border(dconv)
    copies[0].wait()
    back = narrow_part(
        grid_side, boxes, 3, order, roi, middle, xe, xp, we.at[0], inv_out, wide_vectors, dfeature,
        part, dprojected, wide_sums, upstream, dexpanded,
    )
    upstream[...] = before[...] + back

    def store(row, w, at, value):
        dconv[row + 1, w + 1] = value
        dflat[at, :] = value

    norm_back(
        grid_side, boxes, upstream, x2, inv[2:3, :], inv[3:4, :], vectors[2:3, :], vectors[3:4, :], upstream, sums, store
    )
    spatial_taps(grid_side, 1 - place[2], place[3], hidden, dflat, taps, away, keep)


def spatial_far(
    order, place, roi, middle, inv_out, wide_vectors, dfeature, we, xe, xp, before, x2, hidden, inv, vectors,
    grid_side, boxes,
):
    rows, width_in = roi.shape
    mid, out = we.shape
    tile, side = out // 4, grid_side + 2
    taps = jax.ShapeDtypeStruct((9 * (mid // 4), mid), BF16)
    return pl.pallas_call(
        functools.partial(spatial_far_kernel, grid_side, boxes),
        in_specs=[SCALARS] * 2 + [ON_CHIP] * 5 + [FAR] + [ON_CHIP] * 7,
        out_specs=[ON_CHIP] * 8,
        out_shape=[
            jax.ShapeDtypeStruct((width_in + mid, tile), BF16),
            pltpu.VMEM((rows, tile), BF16),
            jax.ShapeDtypeStruct((3, tile), F32),
            taps,
            taps,
            pltpu.VMEM((side, side, boxes, mid), BF16),
            pltpu.VMEM((rows, mid), BF16),
            jax.ShapeDtypeStruct((2, mid), F32),
        ],
        scratch_shapes=[
            pltpu.VMEM((1, mid, tile), BF16),
            pltpu.VMEM((rows, tile), F32),
            pltpu.VMEM((rows, tile), BF16),
            pltpu.VMEM((mid, mid // 2), BF16),
            pltpu.SemaphoreType.DMA((1,)),
        ],
        compiler_params=params(18),
        cost_estimate=BRIEF,
        name="spatial_far",
    )(
        order, place, *kept(roi, middle), inv_out, wide_vectors, dfeature, *outside(we), *kept(xe, xp, before, x2, hidden),
        inv, vectors,
    )


def spatial_near_kernel(grid_side, place, hidden, dflat, dconv, w9_far, away, keep, dhidden, part, w9, sems):
    copies = start_copies([(w9_far.at[k], w9.at[k]) for k in range(9)], sems)
    rows, width = dflat.shape
    for p in range(3):
        for q in range(3):
            copies[p * 3 + q].wait()
            taps = dconv[2 - p : 2 - p + grid_side, 2 - q : 2 - q + grid_side].reshape(rows, width)
            product = over_columns(taps, w9[p * 3 + q])
            if p + q == 0:
                dhidden[...] = product
            else:
                dhidden[...] += product
    spatial_taps(grid_side, place[2], place[3], hidden, dflat, part, away, keep)


def spatial_near(place, hidden, dflat, dconv, w9, grid_side):
    rows, mid = dflat.shape
    taps = jax.ShapeDtypeStruct((9 * (mid // 4), mid), BF16)
    return pl.pallas_call(
        functools.partial(spatial_near_kernel, grid_side),
        in_specs=[SCALARS] + [ON_CHIP] * 3 + [FAR],
        out_specs=[ON_CHIP] * 3,
        out_shape=[taps, taps, pltpu.VMEM((rows, mid), F32)],
        scratch_shapes=[
            pltpu.VMEM((mid, mid // 2), BF16),
            pltpu.VMEM(w9.shape, BF16),
            pltpu.SemaphoreType.DMA((9,)),
        ],
        compiler_params=params(16),
        cost_estimate=BRIEF,
        name="spatial_near",
    )(place, *kept(hidden, dflat, dconv), *outside(w9))


def reduce_back_kernel(
    grid_side, boxes, order, dhidden, x1, roi, inv, vectors, spatial_sums, norm_sums, bias_sums, class_sums,
    s0, s1, s2, s3, dreduced, away, keep, upstream, weight, sums,
):
    rows, width = upstream.shape

    def store(row, w, at, value):
        dreduced[at, :] = value

    norm_back(
        grid_side, boxes, dhidden, x1, inv[0:1, :], inv[1:2, :], vectors[0:1, :], vectors[1:2, :], upstream, sums, store
    )
    weight[...] = over_rows(dreduced[...], roi[...]).astype(BF16)
    quarter, classes = width // 4, class_sums.shape[1]
    size = away.shape[0] // 2
    for k, (target, wide_sums) in enumerate(((away, s0), (keep, s1), (away, s2), (keep, s3))):
        base = (k // 2) * size
        lines = pl.ds(pl.multiple_of(order[k] * quarter, quarter), quarter)
        wide = pl.ds(pl.multiple_of(order[k] * width, width), width)
        target[base : base + quarter, :] = weight[lines, :width]
        target[base + quarter : base + 2 * quarter, :] = weight[lines, width:]
        line0 = [v[r : r + 1, lines] for v in (sums, spatial_sums) for r in range(2)]
        line1 = [norm_sums[r : r + 1, lines] for r in range(2)]
        line1 += [class_sums[...], jnp.zeros((1, width - 2 * quarter - classes), F32)]
        tail = jnp.concatenate(
            [
                jnp.concatenate(line0, axis=1),
                jnp.concatenate(line1, axis=1),
                wide_sums[...],
                bias_sums[:, wide],
                jnp.zeros((10, width), F32),
            ]
        )
        target[base + 2 * quarter : base + size, :] = tail.astype(BF16)


def reduce_back(order, dhidden, x1, roi, inv, vectors, *sums, grid_side, boxes):
    rows, width_in = roi.shape
    mid = dhidden.shape[1]
    part = jax.ShapeDtypeStruct((2 * (mid // 2 + 16), mid), BF16)
    return pl.pallas_call(
        functools.partial(reduce_back_kernel, grid_side, boxes),
        in_specs=[SCALARS] + [ON_CHIP] * 13,
        out_specs=[ON_CHIP] * 3,
        out_shape=[pltpu.VMEM((rows, mid), BF16), part, part],
        scratch_shapes=[
            pltpu.VMEM((rows, mid), F32),
            pltpu.VMEM((mid, width_in), BF16),
            pltpu.VMEM((2, mid), F32),
        ],
        compiler_params=params(14),
        cost_estimate=BRIEF,
        name="reduce_back",
    )(order, *kept(dhidden, x1, roi), inv, vectors, *sums)


def roi_back_kernel(half, order, dreduced, d0, d1, d2, d3, wr_far, ws_far, *rest):
    out, wr, ws, acc, low, sems = rest[-6:]
    tile = d0.shape[1]
    size = acc.shape[1]
    lines = pl.ds(half * size, size)
    columns = [pl.ds(pl.multiple_of(order[k] * tile, tile), tile) for k in range(4)]
    copies = start_copies(
        [(wr_far.at[lines, :], wr)] + [(ws_far.at[lines, columns[k]], ws.at[k]) for k in range(4)], sems
    )
    copies[0].wait()
    acc[...] = over_columns(dreduced[...], wr[...])
    for k, d in enumerate((d0, d1, d2, d3)):
        copies[k + 1].wait()
        acc[...] += over_columns(d[...], ws[k])
    low[...] = acc[...].astype(BF16)
    pltpu.sync_copy(low, out.at[:, lines])


def roi_back(order, dreduced, dprojected, wr, ws, *done, half):
    rows, mid = dreduced.shape
    width_in, out = ws.shape
    size = width_in // 2
    return pl.pallas_call(
        functools.partial(roi_back_kernel, half),
        in_specs=[SCALARS] + [ON_CHIP] * 5 + [FAR] * (2 + len(done)),
        out_specs=FAR,
        out_shape=pltpu.HBM((rows, width_in), BF16),
        input_output_aliases={8: 0} if done else {},
        scratch_shapes=[
            pltpu.VMEM((size, mid), BF16),
            pltpu.VMEM((4, size, out // 4), BF16),
            pltpu.VMEM((rows, size), F32),
            pltpu.VMEM((rows, size), BF16),
            pltpu.SemaphoreType.DMA((5,)),
        ],
        compiler_params=params(18),
        cost_estimate=BRIEF,
        name="roi_back",
    )(order, *kept(dreduced, *dprojected), *outside(wr, ws, *done))


def head_kernel(
    all_seconds, place, seconds, lengths, feature, w0, w1, w2, w3, w4, wq_far, wo_far, wc_far,
    mid_vectors, vectors, class_bias, cotangent,
    logits, dfeature, pack, norm_sums, bias_sums, class_sums, window, wq, wo, wc, sems,
):
    copies = start_copies([(wq_far, wq), (wo_far, wo), (wc_far, wc)], sems)
    att = wq.shape[1]
    boxes, out = feature.shape
    classes = cotangent.shape[1]
    span = window.shape[0]
    rows = w0.shape[0]
    for k, w in enumerate((w0, w1, w2, w3, w4)):
        window[k * rows : (k + 1) * rows, :] = w[...]
    scale = att ** (-0.5)
    norm_gain, norm_shift = mid_vectors[4:5, :], mid_vectors[5:6, :]

    row_seconds = lax.broadcasted_iota(jnp.int32, (boxes, span), 1) // PER_SEC + (place[0] - REACH) * SEC_DEV
    line = lax.broadcasted_iota(jnp.int32, (boxes, 128), 0)
    box_seconds = jnp.zeros((boxes, 128), jnp.int32)
    for k in range(boxes):
        box_seconds = jnp.where(line == k, seconds[k], box_seconds)
    box_seconds = box_seconds[:, 0:1]
    live = (row_seconds >= 0) & (row_seconds < all_seconds) & (jnp.abs(box_seconds - row_seconds) <= HALF)
    end = 0
    for k in range(lengths.shape[0]):
        end = end + lengths[k]
        live = live & ((end <= row_seconds) == (end <= box_seconds))

    copies[0].wait()
    feature_low = feature[...].astype(BF16)
    pack[:, :out] = feature_low
    queries = plain(feature_low, wq[...]).astype(BF16)
    keys, values = window[:, :att], window[:, att:]
    scores = over_columns(queries, keys) * scale
    top = jnp.max(jnp.where(live, scores, -1e30), axis=1, keepdims=True)
    exps = jnp.where(live, jnp.exp(jnp.where(live, scores - top, 0.0)), 0.0)
    probs = exps / jnp.sum(exps, axis=1, keepdims=True)
    probs_low = probs.astype(BF16)
    pre = plain(probs_low, values) + queries.astype(F32)
    centred = pre - jnp.mean(pre, axis=1, keepdims=True)
    inv = lax.rsqrt(jnp.mean(centred * centred, axis=1, keepdims=True) + EPSILON)
    x = centred * inv
    h = 0.5 * (x * norm_gain + norm_shift)
    activated = (h + h * jnp.tanh(h)).astype(BF16)
    copies[1].wait()
    combined_low = (feature[...] + plain(activated, wo[...]) + vectors[4:5, :]).astype(BF16)
    pack[:, out : 2 * out] = combined_low
    copies[2].wait()
    logits[...] = over_columns(feature_low, wc[:, :out]) + over_columns(combined_low, wc[:, out:]) + class_bias[...]
    g = cotangent[...].astype(BF16)
    class_sums[...] = jnp.sum(g.astype(F32), axis=0, keepdims=True)
    first = plain(g, wc[:, :out])
    second = plain(g, wc[:, out:])
    gb = second.astype(BF16)
    pack[:, 2 * out : 3 * out] = gb
    bias_sums[...] = jnp.sum(gb.astype(F32), axis=0, keepdims=True)
    u = over_columns(gb, wo[...]) * (0.5 * doubled_slope(h))
    norm_sums[0:1, :] = jnp.sum(u * x, axis=0, keepdims=True)
    norm_sums[1:2, :] = jnp.sum(u, axis=0, keepdims=True)
    e = u * norm_gain
    dpre = inv * (e - jnp.mean(e, axis=1, keepdims=True) - x * jnp.mean(e * x, axis=1, keepdims=True))
    da = dpre.astype(BF16)
    dprobs = over_columns(da, values)
    delta = jnp.sum(probs * dprobs, axis=1, keepdims=True)
    ds = (probs * (dprobs - delta)).astype(BF16)
    dq = (plain(ds, keys) * scale + dpre).astype(BF16)
    at = 3 * out
    for value in (dq, activated, queries, da):
        pack[:, at : at + att] = value
        at += att
    pack[:, at : at + 128] = jnp.zeros((boxes, 128), BF16)
    pack[:, at : at + classes] = g
    at += 128
    pack[:, at : at + span] = ds
    pack[:, at + span :] = probs_low
    dfeature[...] = first + second + over_columns(dq, wq[...])


def head(place, seconds, lengths, feature, windows, wq, wo, wc, mid_vectors, vectors, class_bias, cotangent, all_seconds):
    boxes, out = feature.shape
    att = wq.shape[1]
    classes = wc.shape[0]
    span = sum(w.shape[0] for w in windows)
    shapes = [
        ((boxes, classes), F32),
        ((boxes, out), F32),
        ((boxes, 3 * out + 4 * att + 128 + 2 * span), BF16),
        ((2, att), F32),
        ((1, out), F32),
        ((1, classes), F32),
    ]
    return pl.pallas_call(
        functools.partial(head_kernel, all_seconds),
        in_specs=[SCALARS] * 3 + [ON_CHIP] * 6 + [FAR] * 3 + [ON_CHIP] * 4,
        out_specs=[ON_CHIP] * len(shapes),
        out_shape=[jax.ShapeDtypeStruct(s, d) for s, d in shapes],
        scratch_shapes=[
            pltpu.VMEM((span, 2 * att), BF16),
            pltpu.VMEM(wq.shape, BF16),
            pltpu.VMEM(wo.shape, BF16),
            pltpu.VMEM(wc.shape, BF16),
            pltpu.SemaphoreType.DMA((3,)),
        ],
        compiler_params=params(16),
        cost_estimate=BRIEF,
        name="head",
    )(place, seconds, lengths, feature, *windows, *outside(wq, wo, wc), mid_vectors, vectors, class_bias, cotangent)


def halves(place, bit, value, sent, kept):
    size = sent.shape[0]
    mine = place[4 + bit]
    sent[...] = value[pl.ds(pl.multiple_of((1 - mine) * size, 16), size), :]
    kept[...] = value[pl.ds(pl.multiple_of(mine * size, 16), size), :]


def small_weights_kernel(
    grouped, place, pair, far_pair, pair_bank, far_bank, sent_a, kept_a, sent_b, kept_b,
    pack, banks, dbank, first, second,
):
    boxes = pair.shape[0] // 2
    for k, source in ((place[3], pair), (1 - place[3], far_pair)):
        for half in range(2):
            lines = pl.ds(pl.multiple_of((2 * half + k) * boxes, 16), boxes)
            pack[lines, :] = source[half * boxes : (half + 1) * boxes, :]
    rows = pair_bank.shape[0] // 4
    for k, source in ((place[3], pair_bank), (1 - place[3], far_bank)):
        for block in range(4):
            lines = pl.ds(pl.multiple_of((2 * block + k) * rows, 16), rows)
            banks[lines, :] = source[block * rows : (block + 1) * rows, :]
    width = first.shape[1]
    att, out, piece = width, banks.shape[1], width // 4
    span = (2 * REACH + 1) * rows
    q = place[1]
    columns = lambda base, size: pl.ds(pl.multiple_of(base + q * size, size), size)
    base = 3 * out
    at = base + 4 * att + 128
    dbank[...] = jnp.zeros(dbank.shape, F32)
    for k in range(grouped):
        lines, window = slice(k * boxes, (k + 1) * boxes), slice(k * rows, k * rows + span)
        ds, probs = pack[lines, at : at + span], pack[lines, at + span : at + 2 * span]
        dbank[window, :piece] += over_rows(ds, pack[lines, columns(base + 2 * att, piece)]) * att ** (-0.5)
        dbank[window, piece:] += over_rows(probs, pack[lines, columns(base + 3 * att, piece)])
    for left, right, target, row in (
        (pack[:, columns(base, piece)], pack[:, :out], first, 0),
        (dbank[:, :piece].astype(BF16), banks[...], first, att),
        (dbank[:, piece:].astype(BF16), banks[...], second, 0),
    ):
        product = over_rows(left, right).astype(BF16)
        for k in range(out // width):
            target[row + k * piece : row + (k + 1) * piece, :] = product[:, k * width : (k + 1) * width]
    second[att : 2 * att, :] = over_rows(
        pack[:, base + att : base + 2 * att], pack[:, columns(2 * out, out // 4)]
    ).astype(BF16)
    at = base + 4 * att
    product = over_rows(pack[:, at : at + 128], pack[:, columns(0, out // 2)]).astype(BF16)
    first[2 * att :, :] = product[:, :width]
    second[2 * att :, :] = product[:, width:]
    halves(place, 0, first, sent_a, kept_a)
    halves(place, 0, second, sent_b, kept_b)


def small_weights(place, pair, far_pair, pair_bank, far_bank, att, grouped):
    rows, out = 2 * att + 128, pair_bank.shape[1]
    reach = 2 * pair_bank.shape[0]
    return pl.pallas_call(
        functools.partial(small_weights_kernel, grouped),
        in_specs=[SCALARS] + [ON_CHIP] * 4,
        out_specs=[ON_CHIP] * 4,
        out_shape=[jax.ShapeDtypeStruct((rows // 2, att), BF16)] * 4,
        scratch_shapes=[
            pltpu.VMEM((2 * pair.shape[0], pair.shape[1]), BF16),
            pltpu.VMEM((reach, out), BF16),
            pltpu.VMEM((reach, att // 2), F32),
            pltpu.VMEM((rows, att), BF16),
            pltpu.VMEM((rows, att), BF16),
        ],
        compiler_params=params(20),
        cost_estimate=BRIEF,
        name="small_weights",
    )(place, pair, far_pair, pair_bank, far_bank)


class View:
    def __init__(self, array, at=0, rows=None):
        self.array, self.at = array, at
        self.rows = array.shape[0] if rows is None else rows

    @property
    def shape(self):
        return (self.rows, *self.array.shape[1:])

    def of(self, array):
        return View(array, self.at, self.rows)


def view(value):
    return value if isinstance(value, View) else View(value)


class Task:
    def __init__(self, run, inputs, outputs, scratch=()):
        self.run, self.scratch = run, list(scratch)
        self.inputs = [view(v) for v in inputs]
        self.outputs = [out if isinstance(out[0], tuple) else (out, None) for out in outputs]


def distinct(views):
    arrays, places = [], []
    for v in views:
        found = [k for k, array in enumerate(arrays) if array is v.array]
        places.append(found[0] if found else len(arrays))
        if not found:
            arrays.append(v.array)
    return arrays, places


def rows_of(ref, v):
    return ref if v.rows == v.array.shape[0] else ref.at[v.at : v.at + v.rows]


def step(place, tasks):
    arrays, places = distinct([v for t in tasks for v in t.inputs])
    shapes, boxes, outputs = [], {}, []
    for task in tasks:
        for shape, way in task.outputs:
            if way is None:
                shapes.append(list(shape))
                outputs.append((len(shapes) - 1, 0, shape[0]))
            else:
                if way not in boxes:
                    boxes[way] = len(shapes)
                    shapes.append([0, shape[1]])
                box = shapes[boxes[way]]
                outputs.append((boxes[way], box[0], shape[0]))
                box[0] += shape[0]

    def kernel(place_ref, *refs):
        ins, outs, scratch = refs[: len(arrays)], refs[len(arrays) : len(arrays) + len(shapes)], refs[len(arrays) + len(shapes) :]
        where, made = list(places), list(outputs)
        for task in tasks:
            sources = [rows_of(ins[where.pop(0)], v) for v in task.inputs]
            targets = []
            for _ in task.outputs:
                k, at, rows = made.pop(0)
                targets.append(outs[k] if rows == shapes[k][0] else outs[k].at[at : at + rows])
            task.run(place_ref, *sources, *targets, *scratch[: len(task.scratch)])
            scratch = scratch[len(task.scratch) :]

    results = pl.pallas_call(
        kernel,
        in_specs=[SCALARS] + [ON_CHIP] * len(arrays),
        out_specs=[ON_CHIP] * len(shapes),
        out_shape=[jax.ShapeDtypeStruct(tuple(shape), BF16) for shape in shapes],
        scratch_shapes=[pltpu.VMEM(shape, BF16) for t in tasks for shape in t.scratch],
        compiler_params=params(16),
        cost_estimate=BRIEF,
        name="step",
    )(place, *arrays)
    made = [View(results[k], at, rows) for k, at, rows in outputs]
    grouped = []
    for task in tasks:
        grouped.append(made[: len(task.outputs)])
        made = made[len(task.outputs) :]
    return grouped


def add_task(a, b, way=None):
    def run(place, x, y, total):
        total[...] = x[...] + y[...]

    return Task(run, (a, b), [(view(a).shape, way)])


HALVES, WHOLE, GATHER = range(3)
FIVE = [(0, HALVES), (1, HALVES), (2, WHOLE), (1, GATHER), (0, GATHER)]
FOUR = [(0, HALVES), (1, WHOLE), (2, WHOLE), (0, GATHER)]
THREE = [(0, WHOLE), (1, WHOLE), (2, WHOLE)]


class BankTotal:
    def __init__(self, sent, kept, plan):
        self.sent, self.kept, self.plan, self.stage = view(sent), view(kept), plan, 0

    @property
    def done(self):
        return self.stage == len(self.plan)

    def way(self, stage):
        return ("bank", 1 << self.plan[stage][0])

    def arrival(self, other):
        (bit, kind), (size, width) = self.plan[self.stage], self.kept.shape
        last = self.stage + 1 == len(self.plan)
        if last and kind == GATHER:
            return None
        way = None if last else self.way(self.stage + 1)
        if kind == GATHER:

            def gather(place, mine, other, joined):
                join(place, bit, mine, other, joined)

            return Task(gather, (self.kept, other), [((2 * size, width), way)])
        if last or self.plan[self.stage + 1][1] != HALVES:
            return add_task(self.kept, other, way)
        next_bit = self.plan[self.stage + 1][0]

        def add(place, kept, other, sent, left, total):
            total[...] = kept[...] + other[...]
            halves(place, next_bit, total, sent, left)

        half = (size // 2, width)
        return Task(add, (self.kept, other), [(half, way), half], [(size, width)])

    def land(self, other, results):
        if results is None:
            self.other = other
        else:
            self.sent, self.kept = results[0], results[-1]
            if self.plan[self.stage] == (2, WHOLE):
                self.sent = self.kept = beyond(self.kept)
        self.stage += 1


def beyond(value):
    size = lax.axis_size("bank")
    if size == 8:
        return value
    own = lax.slice_in_dim(value.array, value.at, value.at + value.rows)
    return View(lax.psum(own, "bank", axis_index_groups=[list(range(k, size, 8)) for k in range(8)]))


def join(place, bit, mine, other, joined):
    size = mine.shape[0]
    at = place[4 + bit]
    joined[pl.ds(pl.multiple_of(at * size, 16), size), :] = mine[...]
    joined[pl.ds(pl.multiple_of((1 - at) * size, 16), size), :] = other[...]


def emit(place, run, inputs, outputs, scratch, name):
    arrays, places = distinct(inputs)

    def kernel(place_ref, *refs):
        sources = [rows_of(refs[k], v) for k, v in zip(places, inputs)]
        run(place_ref, *sources, *refs[len(arrays) :])

    return pl.pallas_call(
        kernel,
        in_specs=[SCALARS] + [ON_CHIP] * len(arrays),
        out_specs=[ON_CHIP] * len(outputs),
        out_shape=[jax.ShapeDtypeStruct(shape, F32) for shape in outputs],
        scratch_shapes=[pltpu.VMEM(shape, BF16) for shape in scratch],
        compiler_params=params(20),
        cost_estimate=BRIEF,
        name=name,
    )(place, *arrays)


def emit_small(place, a, other_a, b, other_b, out, att, classes):
    piece = att // 4
    rows = 2 * att + 128

    def run(place, a, other_a, b, other_b, dquery, dkey, dvalue, doutput, dclass, first, second):
        join(place, 0, a, other_a, first)
        join(place, 0, b, other_b, second)
        for source, row, target in ((first, 0, dquery), (first, att, dkey), (second, 0, dvalue)):
            for k in range(out // att):
                block = source[row + k * piece : row + (k + 1) * piece, :].astype(F32)
                target[k * att : (k + 1) * att, :] = block.T
        doutput[...] = second[att : 2 * att, :].astype(F32)
        dclass[:, :att] = first[2 * att :, :].astype(F32)[:classes]
        dclass[:, att:] = second[2 * att :, :].astype(F32)[:classes]

    return emit(
        place,
        run,
        (a, other_a, b, other_b),
        [(out, piece)] * 3 + [(att, att), (classes, 2 * att)],
        [(rows, att)] * 2,
        "emit_small",
    )


def emit_wide(place, a, other_a, b, other_b, width_in, mid, tile):
    half = 2 * a.rows

    def run(place, a, other_a, b, other_b, shortcut, expand, joined):
        join(place, 0, a, other_a, joined.at[:half])
        join(place, 0, b, other_b, joined.at[half:])
        shortcut[...] = joined[:width_in, :].astype(F32)
        expand[...] = joined[width_in:, :].astype(F32)

    inputs = (a, other_a, b, other_b)
    shapes = [(width_in, tile), (mid, tile)]
    return emit(place, run, inputs, shapes, [(width_in + mid, tile)], "emit_wide")


def emit_last(place, flow_a, flow_b, last, width_in, mid, tile, classes):
    quarter = mid // 4
    rows_a, rows_b = 2 * flow_a.kept.rows, 2 * flow_b.kept.rows

    def run(place, a, other_a, b, other_b, rest, spatial, reduce, *targets):
        targets, taps = targets[:-1], targets[-1]
        join(place, 0, a, other_a, taps.at[:rows_a])
        join(place, 0, b, other_b, taps.at[rows_a:])
        for tap in range(9):
            for k in range(4):
                spatial[tap, k * quarter : (k + 1) * quarter, :] = taps[
                    tap * quarter : (tap + 1) * quarter, k * quarter : (k + 1) * quarter
                ].astype(F32)
        for k in range(2):
            reduce[k * mid : (k + 1) * mid, :] = rest[k * quarter : (k + 1) * quarter, :].astype(F32).T
        tail = rest[2 * quarter : 2 * quarter + 16, :].astype(F32)
        for k in range(4):
            targets[k][...] = tail[0:1, k * quarter : (k + 1) * quarter]
        for k in range(2):
            targets[4 + k][...] = tail[1:2, k * quarter : (k + 1) * quarter]
        targets[6][...] = tail[1:2, 2 * quarter : 2 * quarter + classes]
        for k in range(4):
            targets[7 + k][...] = tail[2 + k : 3 + k, :]
        targets[11][...] = tail[3:4, :]

    inputs = (flow_a.kept, flow_a.other, flow_b.kept, flow_b.other, last.kept)
    shapes = [(9, mid, quarter), (width_in, quarter)] + [(1, quarter)] * 6 + [(1, classes)] + [(1, tile)] * 5
    return emit(place, run, inputs, shapes, [(rows_a + rows_b, mid)], "emit_last")


def move(value, how):
    kind, by = how
    if kind == "edge":
        axis = ("bank", "box")
        size = lax.axis_size(axis)
        targets = [(i, i + by if i % by >= by // 2 else i - by) for i in range(size)]
        return lax.ppermute(value, axis, [(i, j) for i, j in targets if 0 <= j < size])
    if kind == "along":
        axis = ("bank", "box")
        size = lax.axis_size(axis)
        return lax.ppermute(value, axis, [(i, i + by) for i in range(size) if 0 <= i + by < size])
    return lax.ppermute(value, kind, [(i, i ^ by) for i in range(lax.axis_size(kind))])


def launch(moves):
    found, received = [], []
    for value, how in moves:
        same = [r for v, h, r in found if v is value.array and h == how]
        if not same:
            same = [move(value.array, how)]
            found.append((value.array, how, same[0]))
        received.append(value.of(same[0]))
    return received


def slot(place, kernel, inputs, moves=(), flows=(), tasks=None, late=()):
    flows = [flow for flow in flows if not flow.done]
    waits = [len(m) == 2 for m in moves] + [True] * len(flows)
    moves = [(view(m[0]), m[1]) for m in moves] + [(flow.sent, flow.way(flow.stage)) for flow in flows]
    arrays, places = distinct([value for value, _ in moves])
    inputs, arrays = lax.optimization_barrier((inputs, arrays))
    received = launch([(value.of(arrays[k]), how) for k, (value, how) in zip(places, moves)])
    results = kernel(*inputs) if kernel else ()
    waited = [v for v, wait in zip(received, waits) if wait] + list(late)
    arrays, places = distinct(waited)
    results, arrays = lax.optimization_barrier((results, arrays))
    waited = [v.of(arrays[k]) for v, k in zip(waited, places)]
    late = waited[len(waited) - len(late) :]
    received = [waited.pop(0) if wait else v for v, wait in zip(received, waits)]
    count = len(moves) - len(flows)
    arrivals, landed = received[:count] + late, received[count:]
    own = tasks(results, arrivals) if tasks else []
    pending = [flow.arrival(other) for flow, other in zip(flows, landed)]
    needed = own + [task for task in pending if task]
    outputs = step(place, needed) if needed else []
    made, outputs = outputs[: len(own)], outputs[len(own) :]
    for flow, task, other in zip(flows, pending, landed):
        flow.land(other, outputs.pop(0) if task else None)
    return results, arrivals, made


def local(
    roi_features,
    box_seconds,
    video_lengths,
    bank_features,
    reduce_weight,
    reduce_gain,
    reduce_shift,
    spatial_weight,
    spatial_gain,
    spatial_shift,
    expand_weight,
    expand_gain,
    expand_shift,
    shortcut_weight,
    shortcut_gain,
    shortcut_shift,
    query_weight,
    key_weight,
    value_weight,
    norm_gain,
    norm_shift,
    output_weight,
    output_bias,
    class_weight,
    class_bias,
    logit_cotangent,
):
    boxes, grid_side = roi_features.shape[:2]
    in_width = roi_features.shape[3]
    rows = boxes * grid_side * grid_side
    mid = reduce_weight.shape[1]
    out = expand_weight.shape[1]
    att = query_weight.shape[1]
    classes = class_weight.shape[1]
    tile, quarter = out // 4, mid // 4
    all_seconds = lax.axis_size(("bank", "box")) * SEC_DEV
    my_index = lax.axis_index(("bank", "box"))
    bank_index, box_index = lax.axis_index("bank"), lax.axis_index("box")
    core, side = box_index % 2, box_index // 2
    place = jnp.stack([my_index, box_index, side, core] + [(bank_index >> k) & 1 for k in range(3)])
    order = jnp.stack([(1 - side) * 2 + 1 - core, (1 - side) * 2 + core, side * 2 + 1 - core, side * 2 + core])
    shape = dict(grid_side=grid_side, boxes=boxes)
    on = functools.partial(slot, place)

    roi = roi_features.transpose(1, 2, 0, 3).reshape(rows, in_width)
    w9 = spatial_weight.reshape(9, mid, mid)
    place, order, roi = lax.optimization_barrier((place, order, roi))
    box_devices = lax.axis_size("box")
    results, (far_bank, edge), _ = on(
        functools.partial(trunk, **shape),
        (
            roi, reduce_weight, w9, bank_features, key_weight, value_weight,
            reduce_gain, reduce_shift, spatial_gain, spatial_shift, norm_gain, norm_shift,
            expand_gain, expand_shift, shortcut_gain, shortcut_shift, output_bias, class_bias,
        ),
        [(bank_features, ("box", 2)), (bank_features, ("edge", box_devices))],
    )
    roi, x1, hidden, x2, middle, inv_mid, own_window, mid_vectors, vectors, class_bias = results
    around = [by for by in range(-REACH, REACH + 1) if by != 0]

    def bundle(results, arrivals):
        def run(place, own, far, edge, far_edge, blocks):
            size = own.shape[0]
            upper = place[2] == 1
            pairs = ((edge, far_edge), (far, own), (own, far), (far_edge, edge))
            for k, (a, b) in enumerate(pairs):
                blocks[k * size : (k + 1) * size, :] = jnp.where(upper, a[...], b[...])

        size, width = bank_features.shape
        return [Task(run, (bank_features, far_bank, edge, arrivals[-1]), [(4 * size, width)])]

    (*xs, inv_out, feature), (*windows, _), ((pair_bank,),) = on(
        functools.partial(widen, **shape),
        (order, roi, middle, shortcut_weight, expand_weight, vectors),
        [(own_window, ("along", -by)) for by in around] + [(edge, ("box", 2))],
        tasks=bundle,
    )
    windows = [w.array for w in windows]
    windows.insert(REACH, own_window)
    (logits, dfeature, pack, norm_sums, bias_sums, class_sums), (far_bank,), _ = on(
        functools.partial(head, all_seconds=all_seconds),
        (
            place, box_seconds, video_lengths, feature, windows, query_weight, output_weight, class_weight.T,
            mid_vectors, vectors, class_bias, logit_cotangent,
        ),
        [(pair_bank, ("box", 1))],
    )

    def narrow_slot(ks, before, *rest, **more):
        operands = (order, roi, middle, inv_out, vectors, dfeature, expand_weight)
        operands += tuple(xs[2 * ks[0] : 2 * ks[-1] + 2]) + before
        return on(functools.partial(narrow, ks=ks, **shape), operands, *rest, **more)

    def pack_pair(results, arrivals):
        def run(place, pack, far_pack, both):
            size = pack.shape[0]
            both[pl.ds(pl.multiple_of(place[2] * size, 16), size), :] = pack[...]
            both[pl.ds(pl.multiple_of((1 - place[2]) * size, 16), size), :] = far_pack[...]

        size, width = pack.shape
        return [Task(run, (pack, arrivals[0]), [(2 * size, width)])]

    (dmiddle, away_far, d0, sums0, keep_far, d1, sums1), _, ((pair_pack,),) = narrow_slot(
        (0, 1), (), [(pack, ("box", 2))], tasks=pack_pair
    )
    half = away_far.shape[0] // 2

    def wide_parts(results, arrivals):
        def run(place, keep, away, first, second):
            first[...] = keep[:half, :] + away[:half, :]
            second[...] = keep[half:, :] + away[half:, :]

        return [Task(run, (keep_far, arrivals[1]), [(half, tile)] * 2)]

    (dmiddle, away_near, d2, sums2), (far_pair, _), ((wide_first, wide_last),) = narrow_slot(
        (2,),
        (dmiddle,),
        [(pair_pack, ("box", 1)), (away_far, ("box", 1))],
        tasks=wide_parts,
    )
    gathered = [v.array for v in (pair_pack, far_pair, pair_bank, far_bank)]
    sent_a, kept_a, sent_b, kept_b = small_weights(place, *gathered, att, box_devices)
    small_a, small_b = BankTotal(sent_a, kept_a, FIVE), BankTotal(sent_b, kept_b, FIVE)
    small = [small_a, small_b]
    (keep_near, d3, sums3, away_taps, keep_far_taps, dconv, dflat, spatial_sums), (near, far_first), _ = on(
        functools.partial(spatial_far, **shape),
        (
            order, place, roi, middle, inv_out, vectors, dfeature, expand_weight, xs[6], xs[7], dmiddle,
            x2, hidden, inv_mid, mid_vectors,
        ),
        [(away_near, ("box", 1)), (wide_first, ("box", 2))],
        [small_a],
    )

    def summed_halves(keep, away, far, at):
        rows = far.shape[0]

        def run(place, keep, away, far, sent, kept, total):
            total[...] = keep[at : at + rows, :] + away[at : at + rows, :] + far[...]
            halves(place, 0, total, sent, kept)

        size = (rows // 2, mid)
        return Task(run, (keep, away, far), [(size, ("bank", 1)), size], [(rows, mid)])

    cut = 5 * quarter

    def tap_parts(results, arrivals):
        def run(place, keep, away, first, second):
            first[...] = keep[:cut, :] + away[:cut, :]
            second[...] = keep[cut:, :] + away[cut:, :]

        size, way = keep_far_taps.shape[0], ("box", 2)
        return [
            summed_halves(keep_near, near, far_first, 0),
            summed_halves(keep_near, near, arrivals[1], half),
            Task(run, (keep_far_taps, arrivals[0]), [((cut, mid), way), (size - cut, mid)]),
        ]

    (away_taps, keep_taps, dhidden), _, (wide_a, wide_b, (taps_first, taps_last)) = on(
        functools.partial(spatial_near, grid_side=grid_side),
        (place, hidden, dflat, dconv, w9),
        [(away_taps, ("box", 1)), (wide_last, ("box", 2))],
        small,
        tasks=tap_parts,
    )
    wide = [BankTotal(*wide_a, FIVE), BankTotal(*wide_b, FIVE)]
    (dreduced, last_away, last_keep), (near_taps, _), (spatial_a,) = on(
        functools.partial(reduce_back, **shape),
        (
            order, dhidden, x1, roi, inv_mid, mid_vectors, spatial_sums, norm_sums, bias_sums, class_sums,
            sums0, sums1, sums2, sums3,
        ),
        [(away_taps, ("box", 1)), (taps_first, ("box", 2))],
        small + wide,
        tasks=lambda results, arrivals: [summed_halves(keep_taps, *arrivals, 0)],
    )
    spatial = [BankTotal(*spatial_a, FIVE)]
    dprojected = (d0, d1, d2, d3)

    def last_sides(results, arrivals):
        def run(place, keep, away, far, near):
            size = far.shape[0]
            far[...] = keep[:size, :] + away[:size, :]
            near[...] = keep[size:, :] + away[size:, :]

        return [
            summed_halves(keep_taps, near_taps, arrivals[0], cut),
            Task(run, (last_keep, arrivals[1]), [(last_keep.shape[0] // 2, mid)] * 2),
        ]

    roi_gradient, _, (spatial_b, (last_out, last_near)) = on(
        functools.partial(roi_back, half=0),
        (order, dreduced, dprojected, reduce_weight, shortcut_weight),
        [(taps_last, ("box", 2)), (last_away, ("box", 1))],
        small + wide + spatial,
        tasks=last_sides,
    )
    spatial.append(BankTotal(*spatial_b, FOUR))
    roi_gradient, _, ((last_total,),) = on(
        functools.partial(roi_back, half=1),
        (order, dreduced, dprojected, reduce_weight, shortcut_weight, roi_gradient),
        [(last_out, ("box", 2))],
        small + wide + spatial,
        tasks=lambda results, arrivals: [add_task(last_near, arrivals[0], ("bank", 1))],
    )
    last = BankTotal(last_total, last_total, THREE)
    flows = small + wide + spatial + [last]
    emitted = {}
    makers = {
        "small": (small, lambda *arrays: emit_small(place, *arrays, out, att, classes)),
        "wide": (wide, lambda *arrays: emit_wide(place, *arrays, in_width, mid, tile)),
    }
    while any(not flow.done for flow in flows):
        ready = [k for k, (group, _) in makers.items() if k not in emitted and all(flow.done for flow in group)]
        views = [v for k in ready for flow in makers[k][0] for v in (flow.kept, flow.other)]
        arrays, places = distinct(views)

        def outputs(*arrays):
            found = [v.of(arrays[k]) for v, k in zip(views, places)]
            return [makers[k][1](*found[4 * n : 4 * n + 4]) for n, k in enumerate(ready)]

        results, _, _ = on(outputs, tuple(arrays), (), flows)
        emitted.update(zip(ready, results))
    for k, (group, make) in makers.items():
        if k not in emitted:
            emitted[k] = make(*[v for flow in group for v in (flow.kept, flow.other)])
    query_g, key_g, value_g, output_g, class_g = emitted["small"]
    shortcut_g, expand_g = emitted["wide"]
    spatial_g, reduce_g, *sums = emit_last(place, *spatial, last, in_width, mid, tile, classes)
    (
        reduce_gain_g, reduce_shift_g, spatial_gain_g, spatial_shift_g, norm_gain_g, norm_shift_g, class_bias_g,
        expand_gain_g, expand_shift_g, shortcut_gain_g, bias_g, shortcut_shift_g,
    ) = [v.reshape(v.shape[1]) for v in sums]
    return (
        logits,
        roi_gradient.reshape(grid_side, grid_side, boxes, in_width).transpose(2, 0, 1, 3),
        reduce_g,
        reduce_gain_g,
        reduce_shift_g,
        spatial_g.reshape(3, 3, mid, quarter),
        spatial_gain_g,
        spatial_shift_g,
        expand_g,
        expand_gain_g,
        expand_shift_g,
        shortcut_g,
        shortcut_gain_g,
        shortcut_shift_g,
        query_g,
        key_g,
        value_g,
        norm_gain_g,
        norm_shift_g,
        output_g,
        bias_g,
        class_g.T,
        class_bias_g,
    )


def solution(mesh):
    split = ("bank", "box")
    in_specs = (P(split), P(split), P(), P(split)) + (P(),) * 21 + (P(split),)
    column, vector = P(None, "box"), P("box")
    out_specs = (
        P(split),
        P(split),
        column,
        vector,
        vector,
        P(None, None, None, "box"),
        vector,
        vector,
        column,
        vector,
        vector,
        column,
        vector,
        vector,
        column,
        column,
        column,
        vector,
        vector,
        column,
        vector,
        P("box", None),
        P(),
    )
    return jax.shard_map(local, mesh=mesh, in_specs=in_specs, out_specs=out_specs, check_vma=False)
```

```python
import functools
import jax
import jax.numpy as jnp
from jax import lax
from jax.experimental import pallas as pl
from jax.experimental.pallas import tpu as pltpu
from jax.sharding import PartitionSpec as P

HALF = 30
PER_SEC = 8
SEC_DEV = 16
REACH = 2
EPSILON = 1e-05
MIB = 2**20
F32, BF16 = jnp.float32, jnp.bfloat16
BRIEF = pl.CostEstimate(flops=1, bytes_accessed=1, transcendentals=0)
ON_CHIP = pl.BlockSpec(memory_space=pltpu.VMEM)
SCALARS = pl.BlockSpec(memory_space=pltpu.SMEM)
FAR = pl.BlockSpec(memory_space=pl.ANY)
OVER_ROWS = (((0,), (0,)), ((), ()))
OVER_COLUMNS = (((1,), (1,)), ((), ()))


def plain(a, b):
    return jnp.dot(a, b, preferred_element_type=F32)


def over_rows(a, b):
    return lax.dot_general(a, b, OVER_ROWS, preferred_element_type=F32)


def over_columns(a, b):
    return lax.dot_general(a, b, OVER_COLUMNS, preferred_element_type=F32)


def params(mebibytes):
    return pltpu.CompilerParams(vmem_limit_bytes=mebibytes * MIB)


def kept(*arrays):
    return [pltpu.with_memory_space_constraint(v, pltpu.VMEM) for v in arrays]


def outside(*arrays):
    return [pltpu.with_memory_space_constraint(v, pltpu.HBM) for v in arrays]


def start_copies(pairs, sems):
    copies = [pltpu.make_async_copy(source, target, sems.at[k]) for k, (source, target) in enumerate(pairs)]
    for copy in copies:
        copy.start()
    return copies


def fold(values):
    values = values.astype(F32)
    return jnp.sum(values.reshape(values.shape[0] // 8, 8, values.shape[1]), axis=0)


def total_rows(values):
    return jnp.sum(values, axis=0, keepdims=True)


def centre(acc, centred, grid_side, boxes):
    rows, width = acc.shape
    step = grid_side * boxes
    first = acc[0:step, :]
    shift = total_rows(jnp.sum(first.reshape(step // 8, 8, width), axis=0)) / step

    def line(k, carry):
        total, square = carry
        sums = squares = None
        for w in range(grid_side):
            at = pl.ds((k * grid_side + w) * boxes, boxes)
            value = (acc[at, :] - shift).astype(BF16)
            centred[at, :] = value
            sums = value if sums is None else sums + value
            squares = value * value if squares is None else squares + value * value
        return total + fold(sums), square + fold(squares)

    zero = jnp.zeros((8, width), F32)
    total, square = lax.fori_loop(0, grid_side, line, (zero, zero), unroll=True)
    offset = total_rows(total) / rows
    var = total_rows(square) / rows - offset * offset
    return lax.rsqrt(jnp.maximum(var, 0.0) + EPSILON), offset, shift


def scaled(inv, offset, gain, shift):
    factor = 0.5 * gain * inv
    return factor, 0.5 * shift - factor * offset


def input_gradient(inv, offset, gain, total, total_c, rows):
    gain_gradient = inv * (total_c - offset * total)
    of_upstream = inv * gain
    of_centred = -of_upstream * inv * gain_gradient / rows
    term = -of_upstream * total / rows - of_centred * offset
    return of_upstream, of_centred, term, gain_gradient


def clear_border(padded):
    side, _, boxes, width = padded.shape
    zeros = jnp.zeros((boxes, width), BF16)
    for k in range(side):
        padded[0, k] = zeros
        padded[side - 1, k] = zeros
        padded[k, 0] = zeros
        padded[k, side - 1] = zeros


def by_cells(grid_side, boxes, body, carry):
    def line(k, carry):
        for w in range(grid_side):
            carry = body(k, w, pl.ds((k * grid_side + w) * boxes, boxes), carry)
        return carry

    return lax.fori_loop(0, grid_side, line, carry)


def trunk_kernel(
    grid_side, boxes, roi_far, wr_far, w9_far, bank_far, kw_far, vw_far, *rest
):
    far_vectors, rest = rest[:12], rest[12:]
    roi, x1, hidden, x2, middle, inv, window, vectors, wide_vectors, class_bias = rest[:10]
    wr, w9, bank, kw, vw, acc, sems = rest[10:17]
    near_vectors = rest[17:]
    copies = start_copies(
        [(roi_far, roi), (wr_far, wr), (w9_far, w9), (bank_far, bank), (kw_far, kw), (vw_far, vw)]
        + list(zip(far_vectors, near_vectors)),
        sems,
    )
    clear_border(hidden)
    for k, copy in enumerate(copies[6:]):
        copy.wait()
        value = near_vectors[k][...].astype(F32)
        value = value.reshape(1, value.shape[0])
        if k < 6:
            vectors[k : k + 1, :] = value
        elif k < 11:
            wide_vectors[k - 6 : k - 5, :] = value
        else:
            class_bias[...] = value
    copies[0].wait()
    copies[1].wait()
    acc[...] = plain(roi[...], wr[...])
    inv1, offset1, base = centre(acc, x1, grid_side, boxes)
    inv[0:1, :], inv[1:2, :] = inv1, offset1
    factor, term = scaled(inv1, base + offset1, vectors[0:1, :], vectors[1:2, :])

    def first(k, w, rows, carry):
        h = acc[rows, :] * factor + term
        hidden[k + 1, w + 1] = (h + h * jnp.tanh(h)).astype(BF16)
        return carry

    by_cells(grid_side, boxes, first, 0)
    copies[2].wait()
    for p in range(3):
        for q in range(3):
            taps = hidden[p : p + grid_side, q : q + grid_side].reshape(acc.shape)
            product = plain(taps, w9[p * 3 + q])
            if p + q == 0:
                acc[...] = product
            else:
                acc[...] += product
    inv2, offset2, base2 = centre(acc, x2, grid_side, boxes)
    inv[2:3, :], inv[3:4, :] = inv2, offset2
    factor2, term2 = scaled(inv2, base2 + offset2, vectors[2:3, :], vectors[3:4, :])

    def second(k, w, rows, carry):
        h = acc[rows, :] * factor2 + term2
        middle[rows, :] = (h + h * jnp.tanh(h)).astype(BF16)
        return carry

    by_cells(grid_side, boxes, second, 0)
    for copy in copies[3:6]:
        copy.wait()
    att = kw.shape[1]
    window[:, :att] = plain(bank[...], kw[...]).astype(BF16)
    window[:, att:] = plain(bank[...], vw[...]).astype(BF16)


def trunk(roi, wr, w9, bank, kw, vw, *vectors, grid_side, boxes):
    rows, mid = roi.shape[0], wr.shape[1]
    side = grid_side + 2
    return pl.pallas_call(
        functools.partial(trunk_kernel, grid_side, boxes),
        in_specs=[FAR] * 18,
        out_specs=[ON_CHIP] * 10,
        out_shape=[
            pltpu.VMEM(roi.shape, BF16),
            pltpu.VMEM((rows, mid), BF16),
            pltpu.VMEM((side, side, boxes, mid), BF16),
            pltpu.VMEM((rows, mid), BF16),
            pltpu.VMEM((rows, mid), BF16),
            jax.ShapeDtypeStruct((4, mid), F32),
            jax.ShapeDtypeStruct((bank.shape[0], 2 * kw.shape[1]), BF16),
            jax.ShapeDtypeStruct((6, mid), F32),
            jax.ShapeDtypeStruct((5, vectors[6].shape[0]), F32),
            jax.ShapeDtypeStruct((1, vectors[11].shape[0]), F32),
        ],
        scratch_shapes=[pltpu.VMEM(v.shape, BF16) for v in (wr, w9, bank, kw, vw)]
        + [pltpu.VMEM((rows, mid), F32), pltpu.SemaphoreType.DMA((18,))]
        + [pltpu.VMEM(v.shape, BF16) for v in vectors],
        compiler_params=params(18),
        cost_estimate=BRIEF,
        name="trunk",
    )(*outside(roi, wr, w9, bank, kw, vw, *vectors))


def widen_kernel(grid_side, boxes, order, roi, middle, ws_far, we_far, vectors, *rest):
    xs, (inv, feature, ws, we, acc_e, acc_p, sems) = rest[:8], rest[8:]
    width = acc_e.shape[1]
    at = [pl.ds(pl.multiple_of(order[k] * width, width), width) for k in range(4)]
    copies = start_copies(
        [pair for k in range(4) for pair in ((ws_far.at[:, at[k]], ws.at[k]), (we_far.at[:, at[k]], we.at[k]))],
        sems,
    )
    for k in range(4):
        xe, xp = xs[2 * k], xs[2 * k + 1]
        copies[2 * k].wait()
        acc_p[...] = plain(roi[...], ws[k])
        copies[2 * k + 1].wait()
        acc_e[...] = plain(middle[...], we[k])
        inv_p, offset_p, base_p = centre(acc_p, xp, grid_side, boxes)
        inv_e, offset_e, base_e = centre(acc_e, xe, grid_side, boxes)
        for row, value in enumerate((inv_e, inv_p, offset_e, offset_p)):
            inv[k, row : row + 1, :] = value
        factor_e, term_e = scaled(inv_e, base_e + offset_e, vectors[0:1, at[k]], vectors[1:2, at[k]])
        factor_p, term_p = scaled(inv_p, base_p + offset_p, vectors[2:3, at[k]], vectors[3:4, at[k]])
        term = term_e + term_p

        def line(row, total):
            for w in range(grid_side):
                rows = pl.ds((row * grid_side + w) * boxes, boxes)
                h = acc_e[rows, :] * factor_e + acc_p[rows, :] * factor_p + term
                total = total + (h + h * jnp.tanh(h))
            return total

        total = lax.fori_loop(0, grid_side, line, jnp.zeros((boxes, width), F32))
        feature[:, at[k]] = total / (grid_side * grid_side)


def widen(order, roi, middle, ws, we, vectors, grid_side, boxes):
    rows, width_in = roi.shape
    mid, out = we.shape
    tile = out // 4
    return pl.pallas_call(
        functools.partial(widen_kernel, grid_side, boxes),
        in_specs=[SCALARS, ON_CHIP, ON_CHIP, FAR, FAR, ON_CHIP],
        out_specs=[ON_CHIP] * 10,
        out_shape=[pltpu.VMEM((rows, tile), BF16)] * 8
        + [jax.ShapeDtypeStruct((4, 4, tile), F32), jax.ShapeDtypeStruct((boxes, out), F32)],
        scratch_shapes=[
            pltpu.VMEM((4, width_in, tile), BF16),
            pltpu.VMEM((4, mid, tile), BF16),
            pltpu.VMEM((rows, tile), F32),
            pltpu.VMEM((rows, tile), F32),
            pltpu.SemaphoreType.DMA((8,)),
        ],
        compiler_params=params(18),
        cost_estimate=BRIEF,
        name="widen",
    )(order, *kept(roi, middle), *outside(ws, we), vectors)


def doubled_slope(h):
    t = jnp.tanh(h)
    return (1.0 + t) * (1.0 + h * (1.0 - t))


def narrow_part(
    grid_side, boxes, k, order, roi, middle, xe, xp, we, inv, vectors, dfeature, part, dprojected, sums,
    upstream, dexpanded,
):
    rows, width = upstream.shape
    columns = pl.ds(pl.multiple_of(order[k] * width, width), width)
    gain_e, gain_p = vectors[0:1, columns], vectors[2:3, columns]
    inv_e, inv_p, offset_e, offset_p = [inv[k, row : row + 1, :] for row in range(4)]
    factor_e, term_e = scaled(inv_e, offset_e, gain_e, vectors[1:2, columns])
    factor_p, term_p = scaled(inv_p, offset_p, gain_p, vectors[3:4, columns])
    term = term_e + term_p
    slope_scale = dfeature[:, columns] * (0.5 / (grid_side * grid_side))

    def line(row, carry):
        sums = None
        for w in range(grid_side):
            at = pl.ds((row * grid_side + w) * boxes, boxes)
            e, p = xe[at, :].astype(F32), xp[at, :].astype(F32)
            u = doubled_slope(e * factor_e + p * factor_p + term) * slope_scale
            upstream[at, :] = u
            new = (u, u * e, u * p)
            sums = new if sums is None else [a + b for a, b in zip(sums, new)]
        return [a + fold(b) for a, b in zip(carry, sums)]

    zero = jnp.zeros((8, width), F32)
    total, total_e, total_p = [total_rows(v) for v in lax.fori_loop(0, grid_side, line, [zero] * 3)]
    ue, ce, te, gain_gradient_e = input_gradient(inv_e, offset_e, gain_e, total, total_e, rows)
    up, cp, tp, gain_gradient_p = input_gradient(inv_p, offset_p, gain_p, total, total_p, rows)
    sums[0:1, :] = gain_gradient_e
    sums[1:2, :] = total
    sums[2:3, :] = gain_gradient_p

    def second(row, w, at, carry):
        u = upstream[at, :]
        dexpanded[at, :] = (u * ue + xe[at, :].astype(F32) * ce + te).astype(BF16)
        dprojected[at, :] = (u * up + xp[at, :].astype(F32) * cp + tp).astype(BF16)
        return carry

    for row in range(grid_side):
        for w in range(grid_side):
            second(row, w, pl.ds((row * grid_side + w) * boxes, boxes), 0)
    split = roi.shape[1]
    part[0:split, :] = over_rows(roi[...], dprojected[...]).astype(BF16)
    part[split:, :] = over_rows(middle[...], dexpanded[...]).astype(BF16)
    return over_columns(dexpanded[...], we[...])


def expand_columns(order, ks, we_far, we, sems):
    width = we.shape[2]
    columns = [pl.ds(pl.multiple_of(order[k] * width, width), width) for k in ks]
    return start_copies([(we_far.at[:, at], we.at[n]) for n, at in enumerate(columns)], sems)


def narrow_kernel(grid_side, boxes, ks, order, roi, middle, inv, vectors, dfeature, we_far, *rest):
    count = len(ks)
    xs, rest = rest[: 2 * count], rest[2 * count :]
    *before, dmiddle = rest[: -4 - 3 * count]
    outs, (we, upstream, dexpanded, sems) = rest[-4 - 3 * count : -4], rest[-4:]
    copies = expand_columns(order, ks, we_far, we, sems)
    for n, k in enumerate(ks):
        copies[n].wait()
        back = narrow_part(
            grid_side, boxes, k, order, roi, middle, xs[2 * n], xs[2 * n + 1], we.at[n], inv, vectors, dfeature,
            *outs[3 * n : 3 * n + 3], upstream, dexpanded,
        )
        if n == 0:
            dmiddle[...] = before[0][...] + back if before else back
        else:
            dmiddle[...] += back


def narrow(order, roi, middle, inv, vectors, dfeature, we, *rest, ks, grid_side, boxes):
    rows, width_in = roi.shape
    mid, out = we.shape
    tile = out // 4
    xs, before = rest[: 2 * len(ks)], rest[2 * len(ks) :]
    return pl.pallas_call(
        functools.partial(narrow_kernel, grid_side, boxes, ks),
        in_specs=[SCALARS] + [ON_CHIP] * 5 + [FAR] + [ON_CHIP] * len(rest),
        out_specs=[ON_CHIP] * (1 + 3 * len(ks)),
        out_shape=[pltpu.VMEM((rows, mid), F32)]
        + [
            jax.ShapeDtypeStruct((width_in + mid, tile), BF16),
            pltpu.VMEM((rows, tile), BF16),
            jax.ShapeDtypeStruct((3, tile), F32),
        ]
        * len(ks),
        input_output_aliases={7 + 2 * len(ks): 0} if before else {},
        scratch_shapes=[
            pltpu.VMEM((len(ks), mid, tile), BF16),
            pltpu.VMEM((rows, tile), F32),
            pltpu.VMEM((rows, tile), BF16),
            pltpu.SemaphoreType.DMA((len(ks),)),
        ],
        compiler_params=params(16),
        cost_estimate=BRIEF,
        name="narrow",
    )(order, *kept(roi, middle), inv, vectors, dfeature, *outside(we), *kept(*xs, *before))


def norm_back(grid_side, boxes, upstream, centred, inv, offset, gain, shift, low, sums, store):
    rows, width = upstream.shape
    factor, term = scaled(inv, offset, gain, shift)

    def line(row, carry):
        sums = None
        for w in range(grid_side):
            at = pl.ds((row * grid_side + w) * boxes, boxes)
            c = centred[at, :].astype(F32)
            u = doubled_slope(c * factor + term) * (0.5 * upstream[at, :])
            low[at, :] = u
            new = (u, u * c)
            sums = new if sums is None else [a + b for a, b in zip(sums, new)]
        return [a + fold(b) for a, b in zip(carry, sums)]

    zero = jnp.zeros((8, width), F32)
    total, total_c = [total_rows(v) for v in lax.fori_loop(0, grid_side, line, [zero] * 2)]
    of_upstream, of_centred, term, gain_gradient = input_gradient(inv, offset, gain, total, total_c, rows)
    sums[0:1, :] = gain_gradient
    sums[1:2, :] = total

    def second(row, w, at, carry):
        value = low[at, :] * of_upstream + centred[at, :].astype(F32) * of_centred + term
        store(row, w, at, value.astype(BF16))
        return carry

    by_cells(grid_side, boxes, second, 0)


def spatial_taps(grid_side, side, core, hidden, dflat, part, away, keep):
    rows, width = dflat.shape
    half, quarter = width // 2, width // 4
    mine = pl.ds(pl.multiple_of(core * quarter, quarter), quarter)
    other = pl.ds(pl.multiple_of((1 - core) * quarter, quarter), quarter)
    columns = dflat[:, pl.ds(pl.multiple_of(side * half, half), half)]
    for p in range(3):
        for q in range(3):
            taps = hidden[p : p + grid_side, q : q + grid_side].reshape(rows, width)
            part[...] = over_rows(taps, columns).astype(BF16)
            lines = slice((p * 3 + q) * quarter, (p * 3 + q + 1) * quarter)
            for k in range(4):
                lanes = slice(k * quarter, (k + 1) * quarter)
                keep[lines, lanes] = part[lanes, mine]
                away[lines, lanes] = part[lanes, other]


def spatial_far_kernel(
    grid_side, boxes, order, place, roi, middle, inv_out, wide_vectors, dfeature, we_far, xe, xp, before,
    x2, hidden, inv, vectors, part, dprojected, wide_sums, away, keep, dconv, dflat, sums,
    we, upstream, dexpanded, taps, sems,
):
    copies = expand_columns(order, (3,), we_far, we, sems)
    clear_border(dconv)
    copies[0].wait()
    back = narrow_part(
        grid_side, boxes, 3, order, roi, middle, xe, xp, we.at[0], inv_out, wide_vectors, dfeature,
        part, dprojected, wide_sums, upstream, dexpanded,
    )
    upstream[...] = before[...] + back

    def store(row, w, at, value):
        dconv[row + 1, w + 1] = value
        dflat[at, :] = value

    norm_back(
        grid_side, boxes, upstream, x2, inv[2:3, :], inv[3:4, :], vectors[2:3, :], vectors[3:4, :], upstream, sums, store
    )
    spatial_taps(grid_side, 1 - place[2], place[3], hidden, dflat, taps, away, keep)


def spatial_far(
    order, place, roi, middle, inv_out, wide_vectors, dfeature, we, xe, xp, before, x2, hidden, inv, vectors,
    grid_side, boxes,
):
    rows, width_in = roi.shape
    mid, out = we.shape
    tile, side = out // 4, grid_side + 2
    taps = jax.ShapeDtypeStruct((9 * (mid // 4), mid), BF16)
    return pl.pallas_call(
        functools.partial(spatial_far_kernel, grid_side, boxes),
        in_specs=[SCALARS] * 2 + [ON_CHIP] * 5 + [FAR] + [ON_CHIP] * 7,
        out_specs=[ON_CHIP] * 8,
        out_shape=[
            jax.ShapeDtypeStruct((width_in + mid, tile), BF16),
            pltpu.VMEM((rows, tile), BF16),
            jax.ShapeDtypeStruct((3, tile), F32),
            taps,
            taps,
            pltpu.VMEM((side, side, boxes, mid), BF16),
            pltpu.VMEM((rows, mid), BF16),
            jax.ShapeDtypeStruct((2, mid), F32),
        ],
        scratch_shapes=[
            pltpu.VMEM((1, mid, tile), BF16),
            pltpu.VMEM((rows, tile), F32),
            pltpu.VMEM((rows, tile), BF16),
            pltpu.VMEM((mid, mid // 2), BF16),
            pltpu.SemaphoreType.DMA((1,)),
        ],
        compiler_params=params(18),
        cost_estimate=BRIEF,
        name="spatial_far",
    )(
        order, place, *kept(roi, middle), inv_out, wide_vectors, dfeature, *outside(we), *kept(xe, xp, before, x2, hidden),
        inv, vectors,
    )


def spatial_near_kernel(grid_side, place, hidden, dflat, dconv, w9_far, away, keep, dhidden, part, w9, sems):
    copies = start_copies([(w9_far.at[k], w9.at[k]) for k in range(6)], sems)
    rows, width = dflat.shape
    for p in range(2):
        for q in range(3):
            copies[p * 3 + q].wait()
            taps = dconv[2 - p : 2 - p + grid_side, 2 - q : 2 - q + grid_side].reshape(rows, width)
            product = over_columns(taps, w9[p * 3 + q])
            if p + q == 0:
                dhidden[...] = product
            else:
                dhidden[...] += product
    spatial_taps(grid_side, place[2], place[3], hidden, dflat, part, away, keep)


def spatial_near(place, hidden, dflat, dconv, w9, grid_side):
    rows, mid = dflat.shape
    taps = jax.ShapeDtypeStruct((9 * (mid // 4), mid), BF16)
    return pl.pallas_call(
        functools.partial(spatial_near_kernel, grid_side),
        in_specs=[SCALARS] + [ON_CHIP] * 3 + [FAR],
        out_specs=[ON_CHIP] * 3,
        out_shape=[taps, taps, pltpu.VMEM((rows, mid), F32)],
        scratch_shapes=[
            pltpu.VMEM((mid, mid // 2), BF16),
            pltpu.VMEM((6, mid, mid), BF16),
            pltpu.SemaphoreType.DMA((6,)),
        ],
        compiler_params=params(16),
        cost_estimate=BRIEF,
        name="spatial_near",
    )(place, *kept(hidden, dflat, dconv), *outside(w9))


def reduce_back_kernel(
    grid_side, boxes, order, dhidden, dconv, x1, roi, w9_far, inv, vectors, spatial_sums, norm_sums, bias_sums, class_sums,
    s0, s1, s2, s3, dreduced, away, keep, upstream, w9, weight, sums, sems,
):
    rows, width = upstream.shape
    copies = start_copies([(w9_far.at[6 + q], w9.at[q]) for q in range(3)], sems)
    for q in range(3):
        copies[q].wait()
        taps = dconv[0:grid_side, 2 - q : 2 - q + grid_side].reshape(rows, width)
        product = over_columns(taps, w9[q])
        if q == 0:
            upstream[...] = dhidden[...] + product
        else:
            upstream[...] += product

    def store(row, w, at, value):
        dreduced[at, :] = value

    norm_back(
        grid_side, boxes, upstream, x1, inv[0:1, :], inv[1:2, :], vectors[0:1, :], vectors[1:2, :], upstream, sums, store
    )
    weight[...] = over_rows(dreduced[...], roi[...]).astype(BF16)
    quarter, classes = width // 4, class_sums.shape[1]
    size = away.shape[0] // 2
    for k, (target, wide_sums) in enumerate(((away, s0), (keep, s1), (away, s2), (keep, s3))):
        base = (k // 2) * size
        lines = pl.ds(pl.multiple_of(order[k] * quarter, quarter), quarter)
        wide = pl.ds(pl.multiple_of(order[k] * width, width), width)
        target[base : base + quarter, :] = weight[lines, :width]
        target[base + quarter : base + 2 * quarter, :] = weight[lines, width:]
        line0 = [v[r : r + 1, lines] for v in (sums, spatial_sums) for r in range(2)]
        line1 = [norm_sums[r : r + 1, lines] for r in range(2)]
        line1 += [class_sums[...], jnp.zeros((1, width - 2 * quarter - classes), F32)]
        tail = jnp.concatenate(
            [
                jnp.concatenate(line0, axis=1),
                jnp.concatenate(line1, axis=1),
                wide_sums[...],
                bias_sums[:, wide],
                jnp.zeros((10, width), F32),
            ]
        )
        target[base + 2 * quarter : base + size, :] = tail.astype(BF16)


def reduce_back(order, dhidden, dconv, x1, roi, w9, inv, vectors, *sums, grid_side, boxes):
    rows, width_in = roi.shape
    mid = dhidden.shape[1]
    part = jax.ShapeDtypeStruct((2 * (mid // 2 + 16), mid), BF16)
    return pl.pallas_call(
        functools.partial(reduce_back_kernel, grid_side, boxes),
        in_specs=[SCALARS] + [ON_CHIP] * 4 + [FAR] + [ON_CHIP] * 10,
        out_specs=[ON_CHIP] * 3,
        out_shape=[pltpu.VMEM((rows, mid), BF16), part, part],
        scratch_shapes=[
            pltpu.VMEM((rows, mid), F32),
            pltpu.VMEM((3, mid, mid), BF16),
            pltpu.VMEM((mid, width_in), BF16),
            pltpu.VMEM((2, mid), F32),
            pltpu.SemaphoreType.DMA((3,)),
        ],
        compiler_params=params(20),
        cost_estimate=BRIEF,
        name="reduce_back",
    )(order, *kept(dhidden, dconv, x1, roi), *outside(w9), inv, vectors, *sums)


def roi_back_kernel(half, order, dreduced, d0, d1, d2, d3, wr_far, ws_far, *rest):
    out, wr, ws, acc, low, sems = rest[-6:]
    tile = d0.shape[1]
    size = acc.shape[1]
    lines = pl.ds(half * size, size)
    columns = [pl.ds(pl.multiple_of(order[k] * tile, tile), tile) for k in range(4)]
    copies = start_copies(
        [(wr_far.at[lines, :], wr)] + [(ws_far.at[lines, columns[k]], ws.at[k]) for k in range(4)], sems
    )
    copies[0].wait()
    acc[...] = over_columns(dreduced[...], wr[...])
    for k, d in enumerate((d0, d1, d2, d3)):
        copies[k + 1].wait()
        acc[...] += over_columns(d[...], ws[k])
    low[...] = acc[...].astype(BF16)
    pltpu.sync_copy(low, out.at[:, lines])


def roi_back(order, dreduced, dprojected, wr, ws, *done, half):
    rows, mid = dreduced.shape
    width_in, out = ws.shape
    size = width_in // 2
    return pl.pallas_call(
        functools.partial(roi_back_kernel, half),
        in_specs=[SCALARS] + [ON_CHIP] * 5 + [FAR] * (2 + len(done)),
        out_specs=FAR,
        out_shape=pltpu.HBM((rows, width_in), BF16),
        input_output_aliases={8: 0} if done else {},
        scratch_shapes=[
            pltpu.VMEM((size, mid), BF16),
            pltpu.VMEM((4, size, out // 4), BF16),
            pltpu.VMEM((rows, size), F32),
            pltpu.VMEM((rows, size), BF16),
            pltpu.SemaphoreType.DMA((5,)),
        ],
        compiler_params=params(18),
        cost_estimate=BRIEF,
        name="roi_back",
    )(order, *kept(dreduced, *dprojected), *outside(wr, ws, *done))


def head_kernel(
    all_seconds, place, seconds, lengths, feature, w0, w1, w2, w3, w4, wq_far, wo_far, wc_far,
    mid_vectors, vectors, class_bias, cotangent,
    logits, dfeature, pack, norm_sums, bias_sums, class_sums, window, wq, wo, wc, sems,
):
    copies = start_copies([(wq_far, wq), (wo_far, wo), (wc_far, wc)], sems)
    att = wq.shape[1]
    boxes, out = feature.shape
    classes = cotangent.shape[1]
    span = window.shape[0]
    rows = w0.shape[0]
    for k, w in enumerate((w0, w1, w2, w3, w4)):
        window[k * rows : (k + 1) * rows, :] = w[...]
    scale = att ** (-0.5)
    norm_gain, norm_shift = mid_vectors[4:5, :], mid_vectors[5:6, :]

    row_seconds = lax.broadcasted_iota(jnp.int32, (boxes, span), 1) // PER_SEC + (place[0] - REACH) * SEC_DEV
    line = lax.broadcasted_iota(jnp.int32, (boxes, 128), 0)
    box_seconds = jnp.zeros((boxes, 128), jnp.int32)
    for k in range(boxes):
        box_seconds = jnp.where(line == k, seconds[k], box_seconds)
    box_seconds = box_seconds[:, 0:1]
    live = (row_seconds >= 0) & (row_seconds < all_seconds) & (jnp.abs(box_seconds - row_seconds) <= HALF)
    end = 0
    for k in range(lengths.shape[0]):
        end = end + lengths[k]
        live = live & ((end <= row_seconds) == (end <= box_seconds))

    copies[0].wait()
    feature_low = feature[...].astype(BF16)
    pack[:, :out] = feature_low
    queries = plain(feature_low, wq[...]).astype(BF16)
    keys, values = window[:, :att], window[:, att:]
    scores = over_columns(queries, keys) * scale
    top = jnp.max(jnp.where(live, scores, -1e30), axis=1, keepdims=True)
    exps = jnp.where(live, jnp.exp(jnp.where(live, scores - top, 0.0)), 0.0)
    probs = exps / jnp.sum(exps, axis=1, keepdims=True)
    probs_low = probs.astype(BF16)
    pre = plain(probs_low, values) + queries.astype(F32)
    centred = pre - jnp.mean(pre, axis=1, keepdims=True)
    inv = lax.rsqrt(jnp.mean(centred * centred, axis=1, keepdims=True) + EPSILON)
    x = centred * inv
    h = 0.5 * (x * norm_gain + norm_shift)
    activated = (h + h * jnp.tanh(h)).astype(BF16)
    copies[1].wait()
    combined_low = (feature[...] + plain(activated, wo[...]) + vectors[4:5, :]).astype(BF16)
    pack[:, out : 2 * out] = combined_low
    copies[2].wait()
    logits[...] = over_columns(feature_low, wc[:, :out]) + over_columns(combined_low, wc[:, out:]) + class_bias[...]
    g = cotangent[...].astype(BF16)
    class_sums[...] = jnp.sum(g.astype(F32), axis=0, keepdims=True)
    first = plain(g, wc[:, :out])
    second = plain(g, wc[:, out:])
    gb = second.astype(BF16)
    pack[:, 2 * out : 3 * out] = gb
    bias_sums[...] = jnp.sum(gb.astype(F32), axis=0, keepdims=True)
    u = over_columns(gb, wo[...]) * (0.5 * doubled_slope(h))
    norm_sums[0:1, :] = jnp.sum(u * x, axis=0, keepdims=True)
    norm_sums[1:2, :] = jnp.sum(u, axis=0, keepdims=True)
    e = u * norm_gain
    dpre = inv * (e - jnp.mean(e, axis=1, keepdims=True) - x * jnp.mean(e * x, axis=1, keepdims=True))
    da = dpre.astype(BF16)
    dprobs = over_columns(da, values)
    delta = jnp.sum(probs * dprobs, axis=1, keepdims=True)
    ds = (probs * (dprobs - delta)).astype(BF16)
    dq = (plain(ds, keys) * scale + dpre).astype(BF16)
    at = 3 * out
    for value in (dq, activated, queries, da):
        pack[:, at : at + att] = value
        at += att
    pack[:, at : at + 128] = jnp.zeros((boxes, 128), BF16)
    pack[:, at : at + classes] = g
    at += 128
    pack[:, at : at + span] = ds
    pack[:, at + span :] = probs_low
    dfeature[...] = first + second + over_columns(dq, wq[...])


def head(place, seconds, lengths, feature, windows, wq, wo, wc, mid_vectors, vectors, class_bias, cotangent, all_seconds):
    boxes, out = feature.shape
    att = wq.shape[1]
    classes = wc.shape[0]
    span = sum(w.shape[0] for w in windows)
    shapes = [
        ((boxes, classes), F32),
        ((boxes, out), F32),
        ((boxes, 3 * out + 4 * att + 128 + 2 * span), BF16),
        ((2, att), F32),
        ((1, out), F32),
        ((1, classes), F32),
    ]
    return pl.pallas_call(
        functools.partial(head_kernel, all_seconds),
        in_specs=[SCALARS] * 3 + [ON_CHIP] * 6 + [FAR] * 3 + [ON_CHIP] * 4,
        out_specs=[ON_CHIP] * len(shapes),
        out_shape=[jax.ShapeDtypeStruct(s, d) for s, d in shapes],
        scratch_shapes=[
            pltpu.VMEM((span, 2 * att), BF16),
            pltpu.VMEM(wq.shape, BF16),
            pltpu.VMEM(wo.shape, BF16),
            pltpu.VMEM(wc.shape, BF16),
            pltpu.SemaphoreType.DMA((3,)),
        ],
        compiler_params=params(16),
        cost_estimate=BRIEF,
        name="head",
    )(place, seconds, lengths, feature, *windows, *outside(wq, wo, wc), mid_vectors, vectors, class_bias, cotangent)


def halves(place, bit, value, sent, kept):
    size = sent.shape[0]
    mine = place[4 + bit]
    sent[...] = value[pl.ds(pl.multiple_of((1 - mine) * size, 16), size), :]
    kept[...] = value[pl.ds(pl.multiple_of(mine * size, 16), size), :]


def small_weights_kernel(
    grouped, place, pair, far_pair, pair_bank, far_bank, sent_a, kept_a, sent_b, kept_b,
    pack, banks, dbank, first, second,
):
    boxes = pair.shape[0] // 2
    for k, source in ((place[3], pair), (1 - place[3], far_pair)):
        for half in range(2):
            lines = pl.ds(pl.multiple_of((2 * half + k) * boxes, 16), boxes)
            pack[lines, :] = source[half * boxes : (half + 1) * boxes, :]
    rows = pair_bank.shape[0] // 4
    for k, source in ((place[3], pair_bank), (1 - place[3], far_bank)):
        for block in range(4):
            lines = pl.ds(pl.multiple_of((2 * block + k) * rows, 16), rows)
            banks[lines, :] = source[block * rows : (block + 1) * rows, :]
    width = first.shape[1]
    att, out, piece = width, banks.shape[1], width // 4
    span = (2 * REACH + 1) * rows
    q = place[1]
    columns = lambda base, size: pl.ds(pl.multiple_of(base + q * size, size), size)
    base = 3 * out
    at = base + 4 * att + 128
    dbank[...] = jnp.zeros(dbank.shape, F32)
    for k in range(grouped):
        lines, window = slice(k * boxes, (k + 1) * boxes), slice(k * rows, k * rows + span)
        ds, probs = pack[lines, at : at + span], pack[lines, at + span : at + 2 * span]
        dbank[window, :piece] += over_rows(ds, pack[lines, columns(base + 2 * att, piece)]) * att ** (-0.5)
        dbank[window, piece:] += over_rows(probs, pack[lines, columns(base + 3 * att, piece)])
    for left, right, target, row in (
        (pack[:, columns(base, piece)], pack[:, :out], first, 0),
        (dbank[:, :piece].astype(BF16), banks[...], first, att),
        (dbank[:, piece:].astype(BF16), banks[...], second, 0),
    ):
        product = over_rows(left, right).astype(BF16)
        for k in range(out // width):
            target[row + k * piece : row + (k + 1) * piece, :] = product[:, k * width : (k + 1) * width]
    second[att : 2 * att, :] = over_rows(
        pack[:, base + att : base + 2 * att], pack[:, columns(2 * out, out // 4)]
    ).astype(BF16)
    at = base + 4 * att
    product = over_rows(pack[:, at : at + 128], pack[:, columns(0, out // 2)]).astype(BF16)
    first[2 * att :, :] = product[:, :width]
    second[2 * att :, :] = product[:, width:]
    halves(place, 0, first, sent_a, kept_a)
    halves(place, 0, second, sent_b, kept_b)


def small_weights(place, pair, far_pair, pair_bank, far_bank, att, grouped):
    rows, out = 2 * att + 128, pair_bank.shape[1]
    reach = 2 * pair_bank.shape[0]
    return pl.pallas_call(
        functools.partial(small_weights_kernel, grouped),
        in_specs=[SCALARS] + [ON_CHIP] * 4,
        out_specs=[ON_CHIP] * 4,
        out_shape=[jax.ShapeDtypeStruct((rows // 2, att), BF16)] * 4,
        scratch_shapes=[
            pltpu.VMEM((2 * pair.shape[0], pair.shape[1]), BF16),
            pltpu.VMEM((reach, out), BF16),
            pltpu.VMEM((reach, att // 2), F32),
            pltpu.VMEM((rows, att), BF16),
            pltpu.VMEM((rows, att), BF16),
        ],
        compiler_params=params(20),
        cost_estimate=BRIEF,
        name="small_weights",
    )(place, pair, far_pair, pair_bank, far_bank)


class View:
    def __init__(self, array, at=0, rows=None):
        self.array, self.at = array, at
        self.rows = array.shape[0] if rows is None else rows

    @property
    def shape(self):
        return (self.rows, *self.array.shape[1:])

    def of(self, array):
        return View(array, self.at, self.rows)


def view(value):
    return value if isinstance(value, View) else View(value)


class Task:
    def __init__(self, run, inputs, outputs, scratch=()):
        self.run, self.scratch = run, list(scratch)
        self.inputs = [view(v) for v in inputs]
        self.outputs = [out if isinstance(out[0], tuple) else (out, None) for out in outputs]


def distinct(views):
    arrays, places = [], []
    for v in views:
        found = [k for k, array in enumerate(arrays) if array is v.array]
        places.append(found[0] if found else len(arrays))
        if not found:
            arrays.append(v.array)
    return arrays, places


def rows_of(ref, v):
    return ref if v.rows == v.array.shape[0] else ref.at[v.at : v.at + v.rows]


def step(place, tasks):
    arrays, places = distinct([v for t in tasks for v in t.inputs])
    shapes, boxes, outputs = [], {}, []
    for task in tasks:
        for shape, way in task.outputs:
            if way is None:
                shapes.append(list(shape))
                outputs.append((len(shapes) - 1, 0, shape[0]))
            else:
                if way not in boxes:
                    boxes[way] = len(shapes)
                    shapes.append([0, shape[1]])
                box = shapes[boxes[way]]
                outputs.append((boxes[way], box[0], shape[0]))
                box[0] += shape[0]

    def kernel(place_ref, *refs):
        ins, outs, scratch = refs[: len(arrays)], refs[len(arrays) : len(arrays) + len(shapes)], refs[len(arrays) + len(shapes) :]
        where, made = list(places), list(outputs)
        for task in tasks:
            sources = [rows_of(ins[where.pop(0)], v) for v in task.inputs]
            targets = []
            for _ in task.outputs:
                k, at, rows = made.pop(0)
                targets.append(outs[k] if rows == shapes[k][0] else outs[k].at[at : at + rows])
            task.run(place_ref, *sources, *targets, *scratch[: len(task.scratch)])
            scratch = scratch[len(task.scratch) :]

    results = pl.pallas_call(
        kernel,
        in_specs=[SCALARS] + [ON_CHIP] * len(arrays),
        out_specs=[ON_CHIP] * len(shapes),
        out_shape=[jax.ShapeDtypeStruct(tuple(shape), BF16) for shape in shapes],
        scratch_shapes=[pltpu.VMEM(shape, BF16) for t in tasks for shape in t.scratch],
        compiler_params=params(16),
        cost_estimate=BRIEF,
        name="step",
    )(place, *arrays)
    made = [View(results[k], at, rows) for k, at, rows in outputs]
    grouped = []
    for task in tasks:
        grouped.append(made[: len(task.outputs)])
        made = made[len(task.outputs) :]
    return grouped


def add_task(a, b, way=None):
    def run(place, x, y, total):
        total[...] = x[...] + y[...]

    return Task(run, (a, b), [(view(a).shape, way)])


HALVES, WHOLE, GATHER = range(3)
FIVE = [(0, HALVES), (1, HALVES), (2, WHOLE), (1, GATHER), (0, GATHER)]
FOUR = [(0, HALVES), (1, WHOLE), (2, WHOLE), (0, GATHER)]
THREE = [(0, WHOLE), (1, WHOLE), (2, WHOLE)]


class BankTotal:
    def __init__(self, sent, kept, plan):
        self.sent, self.kept, self.plan, self.stage = view(sent), view(kept), plan, 0

    @property
    def done(self):
        return self.stage == len(self.plan)

    def way(self, stage):
        return ("bank", 1 << self.plan[stage][0])

    def arrival(self, other):
        (bit, kind), (size, width) = self.plan[self.stage], self.kept.shape
        last = self.stage + 1 == len(self.plan)
        if last and kind == GATHER:
            return None
        way = None if last else self.way(self.stage + 1)
        if kind == GATHER:

            def gather(place, mine, other, joined):
                join(place, bit, mine, other, joined)

            return Task(gather, (self.kept, other), [((2 * size, width), way)])
        if last or self.plan[self.stage + 1][1] != HALVES:
            return add_task(self.kept, other, way)
        next_bit = self.plan[self.stage + 1][0]

        def add(place, kept, other, sent, left, total):
            total[...] = kept[...] + other[...]
            halves(place, next_bit, total, sent, left)

        half = (size // 2, width)
        return Task(add, (self.kept, other), [(half, way), half], [(size, width)])

    def land(self, other, results):
        if results is None:
            self.other = other
        else:
            self.sent, self.kept = results[0], results[-1]
            if self.plan[self.stage] == (2, WHOLE):
                self.sent = self.kept = beyond(self.kept)
        self.stage += 1


def beyond(value):
    size = lax.axis_size("bank")
    if size == 8:
        return value
    own = lax.slice_in_dim(value.array, value.at, value.at + value.rows)
    return View(lax.psum(own, "bank", axis_index_groups=[list(range(k, size, 8)) for k in range(8)]))


def join(place, bit, mine, other, joined):
    size = mine.shape[0]
    at = place[4 + bit]
    joined[pl.ds(pl.multiple_of(at * size, 16), size), :] = mine[...]
    joined[pl.ds(pl.multiple_of((1 - at) * size, 16), size), :] = other[...]


def emit(place, run, inputs, outputs, scratch, name):
    arrays, places = distinct(inputs)

    def kernel(place_ref, *refs):
        sources = [rows_of(refs[k], v) for k, v in zip(places, inputs)]
        run(place_ref, *sources, *refs[len(arrays) :])

    return pl.pallas_call(
        kernel,
        in_specs=[SCALARS] + [ON_CHIP] * len(arrays),
        out_specs=[ON_CHIP] * len(outputs),
        out_shape=[jax.ShapeDtypeStruct(shape, F32) for shape in outputs],
        scratch_shapes=[pltpu.VMEM(shape, BF16) for shape in scratch],
        compiler_params=params(20),
        cost_estimate=BRIEF,
        name=name,
    )(place, *arrays)


def emit_small(place, a, other_a, b, other_b, out, att, classes):
    piece = att // 4
    rows = 2 * att + 128

    def run(place, a, other_a, b, other_b, dquery, dkey, dvalue, doutput, dclass, first, second):
        join(place, 0, a, other_a, first)
        join(place, 0, b, other_b, second)
        for source, row, target in ((first, 0, dquery), (first, att, dkey), (second, 0, dvalue)):
            for k in range(out // att):
                block = source[row + k * piece : row + (k + 1) * piece, :].astype(F32)
                target[k * att : (k + 1) * att, :] = block.T
        doutput[...] = second[att : 2 * att, :].astype(F32)
        dclass[:, :att] = first[2 * att :, :].astype(F32)[:classes]
        dclass[:, att:] = second[2 * att :, :].astype(F32)[:classes]

    return emit(
        place,
        run,
        (a, other_a, b, other_b),
        [(out, piece)] * 3 + [(att, att), (classes, 2 * att)],
        [(rows, att)] * 2,
        "emit_small",
    )


def emit_wide(place, a, other_a, b, other_b, width_in, mid, tile):
    half = 2 * a.rows

    def run(place, a, other_a, b, other_b, shortcut, expand, joined):
        join(place, 0, a, other_a, joined.at[:half])
        join(place, 0, b, other_b, joined.at[half:])
        shortcut[...] = joined[:width_in, :].astype(F32)
        expand[...] = joined[width_in:, :].astype(F32)

    inputs = (a, other_a, b, other_b)
    shapes = [(width_in, tile), (mid, tile)]
    return emit(place, run, inputs, shapes, [(width_in + mid, tile)], "emit_wide")


def emit_last(place, flow_a, flow_b, last, width_in, mid, tile, classes):
    quarter = mid // 4
    rows_a, rows_b = 2 * flow_a.kept.rows, 2 * flow_b.kept.rows

    def run(place, a, other_a, b, other_b, rest, spatial, reduce, *targets):
        targets, taps = targets[:-1], targets[-1]
        join(place, 0, a, other_a, taps.at[:rows_a])
        join(place, 0, b, other_b, taps.at[rows_a:])
        for tap in range(9):
            for k in range(4):
                spatial[tap, k * quarter : (k + 1) * quarter, :] = taps[
                    tap * quarter : (tap + 1) * quarter, k * quarter : (k + 1) * quarter
                ].astype(F32)
        for k in range(2):
            reduce[k * mid : (k + 1) * mid, :] = rest[k * quarter : (k + 1) * quarter, :].astype(F32).T
        tail = rest[2 * quarter : 2 * quarter + 16, :].astype(F32)
        for k in range(4):
            targets[k][...] = tail[0:1, k * quarter : (k + 1) * quarter]
        for k in range(2):
            targets[4 + k][...] = tail[1:2, k * quarter : (k + 1) * quarter]
        targets[6][...] = tail[1:2, 2 * quarter : 2 * quarter + classes]
        for k in range(4):
            targets[7 + k][...] = tail[2 + k : 3 + k, :]
        targets[11][...] = tail[3:4, :]

    inputs = (flow_a.kept, flow_a.other, flow_b.kept, flow_b.other, last.kept)
    shapes = [(9, mid, quarter), (width_in, quarter)] + [(1, quarter)] * 6 + [(1, classes)] + [(1, tile)] * 5
    return emit(place, run, inputs, shapes, [(rows_a + rows_b, mid)], "emit_last")


def move(value, how):
    kind, by = how
    if kind == "edge":
        axis = ("bank", "box")
        size = lax.axis_size(axis)
        targets = [(i, i + by if i % by >= by // 2 else i - by) for i in range(size)]
        return lax.ppermute(value, axis, [(i, j) for i, j in targets if 0 <= j < size])
    if kind == "along":
        axis = ("bank", "box")
        size = lax.axis_size(axis)
        return lax.ppermute(value, axis, [(i, i + by) for i in range(size) if 0 <= i + by < size])
    return lax.ppermute(value, kind, [(i, i ^ by) for i in range(lax.axis_size(kind))])


def launch(moves):
    found, received = [], []
    for value, how in moves:
        same = [r for v, h, r in found if v is value.array and h == how]
        if not same:
            same = [move(value.array, how)]
            found.append((value.array, how, same[0]))
        received.append(value.of(same[0]))
    return received


def slot(place, kernel, inputs, moves=(), flows=(), tasks=None, late=()):
    flows = [flow for flow in flows if not flow.done]
    waits = [len(m) == 2 for m in moves] + [True] * len(flows)
    moves = [(view(m[0]), m[1]) for m in moves] + [(flow.sent, flow.way(flow.stage)) for flow in flows]
    arrays, places = distinct([value for value, _ in moves])
    inputs, arrays = lax.optimization_barrier((inputs, arrays))
    received = launch([(value.of(arrays[k]), how) for k, (value, how) in zip(places, moves)])
    results = kernel(*inputs) if kernel else ()
    waited = [v for v, wait in zip(received, waits) if wait] + list(late)
    arrays, places = distinct(waited)
    results, arrays = lax.optimization_barrier((results, arrays))
    waited = [v.of(arrays[k]) for v, k in zip(waited, places)]
    late = waited[len(waited) - len(late) :]
    received = [waited.pop(0) if wait else v for v, wait in zip(received, waits)]
    count = len(moves) - len(flows)
    arrivals, landed = received[:count] + late, received[count:]
    own = tasks(results, arrivals) if tasks else []
    pending = [flow.arrival(other) for flow, other in zip(flows, landed)]
    needed = own + [task for task in pending if task]
    outputs = step(place, needed) if needed else []
    made, outputs = outputs[: len(own)], outputs[len(own) :]
    for flow, task, other in zip(flows, pending, landed):
        flow.land(other, outputs.pop(0) if task else None)
    return results, arrivals, made


def local(
    roi_features,
    box_seconds,
    video_lengths,
    bank_features,
    reduce_weight,
    reduce_gain,
    reduce_shift,
    spatial_weight,
    spatial_gain,
    spatial_shift,
    expand_weight,
    expand_gain,
    expand_shift,
    shortcut_weight,
    shortcut_gain,
    shortcut_shift,
    query_weight,
    key_weight,
    value_weight,
    norm_gain,
    norm_shift,
    output_weight,
    output_bias,
    class_weight,
    class_bias,
    logit_cotangent,
):
    boxes, grid_side = roi_features.shape[:2]
    in_width = roi_features.shape[3]
    rows = boxes * grid_side * grid_side
    mid = reduce_weight.shape[1]
    out = expand_weight.shape[1]
    att = query_weight.shape[1]
    classes = class_weight.shape[1]
    tile, quarter = out // 4, mid // 4
    all_seconds = lax.axis_size(("bank", "box")) * SEC_DEV
    my_index = lax.axis_index(("bank", "box"))
    bank_index, box_index = lax.axis_index("bank"), lax.axis_index("box")
    core, side = box_index % 2, box_index // 2
    place = jnp.stack([my_index, box_index, side, core] + [(bank_index >> k) & 1 for k in range(3)])
    order = jnp.stack([(1 - side) * 2 + 1 - core, (1 - side) * 2 + core, side * 2 + 1 - core, side * 2 + core])
    shape = dict(grid_side=grid_side, boxes=boxes)
    on = functools.partial(slot, place)

    roi = roi_features.transpose(1, 2, 0, 3).reshape(rows, in_width)
    w9 = spatial_weight.reshape(9, mid, mid)
    place, order, roi = lax.optimization_barrier((place, order, roi))
    box_devices = lax.axis_size("box")
    results, (far_bank, edge), _ = on(
        functools.partial(trunk, **shape),
        (
            roi, reduce_weight, w9, bank_features, key_weight, value_weight,
            reduce_gain, reduce_shift, spatial_gain, spatial_shift, norm_gain, norm_shift,
            expand_gain, expand_shift, shortcut_gain, shortcut_shift, output_bias, class_bias,
        ),
        [(bank_features, ("box", 2)), (bank_features, ("edge", box_devices))],
    )
    roi, x1, hidden, x2, middle, inv_mid, own_window, mid_vectors, vectors, class_bias = results
    around = [by for by in range(-REACH, REACH + 1) if by != 0]

    (*xs, inv_out, feature), (*windows, far_edge), _ = on(
        functools.partial(widen, **shape),
        (order, roi, middle, shortcut_weight, expand_weight, vectors),
        [(own_window, ("along", -by)) for by in around] + [(edge, ("box", 2))],
    )
    windows = [w.array for w in windows]
    windows.insert(REACH, own_window)
    (logits, dfeature, pack, norm_sums, bias_sums, class_sums), _, _ = on(
        functools.partial(head, all_seconds=all_seconds),
        (
            place, box_seconds, video_lengths, feature, windows, query_weight, output_weight, class_weight.T,
            mid_vectors, vectors, class_bias, logit_cotangent,
        ),
    )

    def narrow_slot(ks, before, *rest, **more):
        operands = (order, roi, middle, inv_out, vectors, dfeature, expand_weight)
        operands += tuple(xs[2 * ks[0] : 2 * ks[-1] + 2]) + before
        return on(functools.partial(narrow, ks=ks, **shape), operands, *rest, **more)

    def pack_pair(results, arrivals):
        def run(place, pack, far_pack, both):
            size = pack.shape[0]
            both[pl.ds(pl.multiple_of(place[2] * size, 16), size), :] = pack[...]
            both[pl.ds(pl.multiple_of((1 - place[2]) * size, 16), size), :] = far_pack[...]

        def bundle(place, own, far, edge, far_edge, blocks):
            size = own.shape[0]
            upper = place[2] == 1
            pairs = ((edge, far_edge), (far, own), (own, far), (far_edge, edge))
            for k, (a, b) in enumerate(pairs):
                blocks[k * size : (k + 1) * size, :] = jnp.where(upper, a[...], b[...])

        size, width = pack.shape
        rows, features = bank_features.shape
        return [
            Task(run, (pack, arrivals[0]), [(2 * size, width)]),
            Task(bundle, (bank_features, far_bank, edge, far_edge), [(4 * rows, features)]),
        ]

    (dmiddle, away_far, d0, sums0, keep_far, d1, sums1), _, ((pair_pack,), (pair_bank,)) = narrow_slot(
        (0, 1), (), [(pack, ("box", 2))], tasks=pack_pair
    )
    half = 13 * (away_far.shape[0] // 24)

    def wide_parts(results, arrivals):
        def run(place, keep, away, first, second):
            first[...] = keep[:half, :] + away[:half, :]
            second[...] = keep[half:, :] + away[half:, :]

        return [Task(run, (keep_far, arrivals[1]), [(half, tile), (keep_far.shape[0] - half, tile)])]

    (dmiddle, away_near, d2, sums2), (far_pair, _, far_bundle), ((wide_first, wide_last),) = narrow_slot(
        (2,),
        (dmiddle,),
        [(pair_pack, ("box", 1)), (away_far, ("box", 1)), (pair_bank, ("box", 1))],
        tasks=wide_parts,
    )
    gathered = [v.array for v in (pair_pack, far_pair, pair_bank, far_bundle)]
    sent_a, kept_a, sent_b, kept_b = small_weights(place, *gathered, att, box_devices)
    small_a, small_b = BankTotal(sent_a, kept_a, FIVE), BankTotal(sent_b, kept_b, FIVE)
    small = [small_a, small_b]
    (keep_near, d3, sums3, away_taps, keep_far_taps, dconv, dflat, spatial_sums), (near, far_first), _ = on(
        functools.partial(spatial_far, **shape),
        (
            order, place, roi, middle, inv_out, vectors, dfeature, expand_weight, xs[6], xs[7], dmiddle,
            x2, hidden, inv_mid, mid_vectors,
        ),
        [(away_near, ("box", 1)), (wide_first, ("box", 2))],
        [small_a],
    )

    def summed_halves(keep, away, far, at):
        rows = far.shape[0]

        def run(place, keep, away, far, sent, kept, total):
            total[...] = keep[at : at + rows, :] + away[at : at + rows, :] + far[...]
            halves(place, 0, total, sent, kept)

        size = (rows // 2, mid)
        return Task(run, (keep, away, far), [(size, ("bank", 1)), size], [(rows, mid)])

    cut = 5 * quarter

    def tap_parts(results, arrivals):
        def run(place, keep, away, first, second):
            first[...] = keep[:cut, :] + away[:cut, :]
            second[...] = keep[cut:, :] + away[cut:, :]

        size, way = keep_far_taps.shape[0], ("box", 2)
        return [
            summed_halves(keep_near, near, far_first, 0),
            summed_halves(keep_near, near, arrivals[1], half),
            Task(run, (keep_far_taps, arrivals[0]), [((cut, mid), way), (size - cut, mid)]),
        ]

    (away_taps, keep_taps, dhidden), _, (wide_a, wide_b, (taps_first, taps_last)) = on(
        functools.partial(spatial_near, grid_side=grid_side),
        (place, hidden, dflat, dconv, w9),
        [(away_taps, ("box", 1)), (wide_last, ("box", 2))],
        small,
        tasks=tap_parts,
    )
    wide = [BankTotal(*wide_a, FIVE), BankTotal(*wide_b, FIVE)]
    (dreduced, last_away, last_keep), (near_taps, _), (spatial_a,) = on(
        functools.partial(reduce_back, **shape),
        (
            order, dhidden, dconv, x1, roi, w9, inv_mid, mid_vectors, spatial_sums, norm_sums, bias_sums, class_sums,
            sums0, sums1, sums2, sums3,
        ),
        [(away_taps, ("box", 1)), (taps_first, ("box", 2))],
        small + wide,
        tasks=lambda results, arrivals: [summed_halves(keep_taps, *arrivals, 0)],
    )
    spatial = [BankTotal(*spatial_a, FIVE)]
    dprojected = (d0, d1, d2, d3)

    def last_sides(results, arrivals):
        def run(place, keep, away, far, near):
            size = far.shape[0]
            far[...] = keep[:size, :] + away[:size, :]
            near[...] = keep[size:, :] + away[size:, :]

        return [
            summed_halves(keep_taps, near_taps, arrivals[0], cut),
            Task(run, (last_keep, arrivals[1]), [(last_keep.shape[0] // 2, mid)] * 2),
        ]

    roi_gradient, _, (spatial_b, (last_out, last_near)) = on(
        functools.partial(roi_back, half=0),
        (order, dreduced, dprojected, reduce_weight, shortcut_weight),
        [(taps_last, ("box", 2)), (last_away, ("box", 1))],
        small + wide + spatial,
        tasks=last_sides,
    )
    spatial.append(BankTotal(*spatial_b, FOUR))
    roi_gradient, _, ((last_total,),) = on(
        functools.partial(roi_back, half=1),
        (order, dreduced, dprojected, reduce_weight, shortcut_weight, roi_gradient),
        [(last_out, ("box", 2))],
        small + wide + spatial,
        tasks=lambda results, arrivals: [add_task(last_near, arrivals[0], ("bank", 1))],
    )
    last = BankTotal(last_total, last_total, THREE)
    flows = small + wide + spatial + [last]
    emitted = {}
    makers = {
        "small": (small, lambda *arrays: emit_small(place, *arrays, out, att, classes)),
        "wide": (wide, lambda *arrays: emit_wide(place, *arrays, in_width, mid, tile)),
    }
    while any(not flow.done for flow in flows):
        ready = [k for k, (group, _) in makers.items() if k not in emitted and all(flow.done for flow in group)]
        views = [v for k in ready for flow in makers[k][0] for v in (flow.kept, flow.other)]
        arrays, places = distinct(views)

        def outputs(*arrays):
            found = [v.of(arrays[k]) for v, k in zip(views, places)]
            return [makers[k][1](*found[4 * n : 4 * n + 4]) for n, k in enumerate(ready)]

        results, _, _ = on(outputs, tuple(arrays), (), flows)
        emitted.update(zip(ready, results))
    for k, (group, make) in makers.items():
        if k not in emitted:
            emitted[k] = make(*[v for flow in group for v in (flow.kept, flow.other)])
    query_g, key_g, value_g, output_g, class_g = emitted["small"]
    shortcut_g, expand_g = emitted["wide"]
    spatial_g, reduce_g, *sums = emit_last(place, *spatial, last, in_width, mid, tile, classes)
    (
        reduce_gain_g, reduce_shift_g, spatial_gain_g, spatial_shift_g, norm_gain_g, norm_shift_g, class_bias_g,
        expand_gain_g, expand_shift_g, shortcut_gain_g, bias_g, shortcut_shift_g,
    ) = [v.reshape(v.shape[1]) for v in sums]
    return (
        logits,
        roi_gradient.reshape(grid_side, grid_side, boxes, in_width).transpose(2, 0, 1, 3),
        reduce_g,
        reduce_gain_g,
        reduce_shift_g,
        spatial_g.reshape(3, 3, mid, quarter),
        spatial_gain_g,
        spatial_shift_g,
        expand_g,
        expand_gain_g,
        expand_shift_g,
        shortcut_g,
        shortcut_gain_g,
        shortcut_shift_g,
        query_g,
        key_g,
        value_g,
        norm_gain_g,
        norm_shift_g,
        output_g,
        bias_g,
        class_g.T,
        class_bias_g,
    )


def solution(mesh):
    split = ("bank", "box")
    in_specs = (P(split), P(split), P(), P(split)) + (P(),) * 21 + (P(split),)
    column, vector = P(None, "box"), P("box")
    out_specs = (
        P(split),
        P(split),
        column,
        vector,
        vector,
        P(None, None, None, "box"),
        vector,
        vector,
        column,
        vector,
        vector,
        column,
        vector,
        vector,
        column,
        column,
        column,
        vector,
        vector,
        column,
        vector,
        P("box", None),
        P(),
    )
    return jax.shard_map(local, mesh=mesh, in_specs=in_specs, out_specs=out_specs, check_vma=False)
```

```python
import functools
import jax
import jax.numpy as jnp
from jax import lax
from jax.experimental import pallas as pl
from jax.experimental.pallas import tpu as pltpu
from jax.sharding import PartitionSpec as P

HALF = 30
PER_SEC = 8
SEC_DEV = 16
REACH = 2
EPSILON = 1e-05
MIB = 2**20
F32, BF16 = jnp.float32, jnp.bfloat16
BRIEF = pl.CostEstimate(flops=1, bytes_accessed=1, transcendentals=0)
ON_CHIP = pl.BlockSpec(memory_space=pltpu.VMEM)
SCALARS = pl.BlockSpec(memory_space=pltpu.SMEM)
FAR = pl.BlockSpec(memory_space=pl.ANY)
OVER_ROWS = (((0,), (0,)), ((), ()))
OVER_COLUMNS = (((1,), (1,)), ((), ()))


def plain(a, b):
    return jnp.dot(a, b, preferred_element_type=F32)


def over_rows(a, b):
    return lax.dot_general(a, b, OVER_ROWS, preferred_element_type=F32)


def over_columns(a, b):
    return lax.dot_general(a, b, OVER_COLUMNS, preferred_element_type=F32)


def params(mebibytes):
    return pltpu.CompilerParams(vmem_limit_bytes=mebibytes * MIB)


def kept(*arrays):
    return [pltpu.with_memory_space_constraint(v, pltpu.VMEM) for v in arrays]


def outside(*arrays):
    return [pltpu.with_memory_space_constraint(v, pltpu.HBM) for v in arrays]


def start_copies(pairs, sems):
    copies = [pltpu.make_async_copy(source, target, sems.at[k]) for k, (source, target) in enumerate(pairs)]
    for copy in copies:
        copy.start()
    return copies


def fold(values):
    values = values.astype(F32)
    return jnp.sum(values.reshape(values.shape[0] // 8, 8, values.shape[1]), axis=0)


def total_rows(values):
    return jnp.sum(values, axis=0, keepdims=True)


def centre(acc, centred, grid_side, boxes):
    rows, width = acc.shape
    step = grid_side * boxes
    first = acc[0:step, :]
    shift = total_rows(jnp.sum(first.reshape(step // 8, 8, width), axis=0)) / step

    def line(k, carry):
        total, square = carry
        sums = squares = None
        for w in range(grid_side):
            at = pl.ds((k * grid_side + w) * boxes, boxes)
            value = (acc[at, :] - shift).astype(BF16)
            centred[at, :] = value
            sums = value if sums is None else sums + value
            squares = value * value if squares is None else squares + value * value
        return total + fold(sums), square + fold(squares)

    zero = jnp.zeros((8, width), F32)
    total, square = lax.fori_loop(0, grid_side, line, (zero, zero), unroll=True)
    offset = total_rows(total) / rows
    var = total_rows(square) / rows - offset * offset
    return lax.rsqrt(jnp.maximum(var, 0.0) + EPSILON), offset, shift


def scaled(inv, offset, gain, shift):
    factor = 0.5 * gain * inv
    return factor, 0.5 * shift - factor * offset


def input_gradient(inv, offset, gain, total, total_c, rows):
    gain_gradient = inv * (total_c - offset * total)
    of_upstream = inv * gain
    of_centred = -of_upstream * inv * gain_gradient / rows
    term = -of_upstream * total / rows - of_centred * offset
    return of_upstream, of_centred, term, gain_gradient


def clear_border(padded):
    side, _, boxes, width = padded.shape
    zeros = jnp.zeros((boxes, width), BF16)
    for k in range(side):
        padded[0, k] = zeros
        padded[side - 1, k] = zeros
        padded[k, 0] = zeros
        padded[k, side - 1] = zeros


def by_cells(grid_side, boxes, body, carry):
    for k in range(grid_side):
        for w in range(grid_side):
            carry = body(k, w, pl.ds((k * grid_side + w) * boxes, boxes), carry)
    return carry


def trunk_kernel(
    grid_side, boxes, roi_far, wr_far, w9_far, bank_far, kw_far, vw_far, *rest
):
    far_vectors, rest = rest[:12], rest[12:]
    roi, x1, hidden, x2, middle, inv, window, vectors, wide_vectors, class_bias = rest[:10]
    wr, w9, bank, kw, vw, acc, sems = rest[10:17]
    near_vectors = rest[17:]
    copies = start_copies(
        [(roi_far, roi), (wr_far, wr), (w9_far, w9), (bank_far, bank), (kw_far, kw), (vw_far, vw)]
        + list(zip(far_vectors, near_vectors)),
        sems,
    )
    clear_border(hidden)
    for k, copy in enumerate(copies[6:]):
        copy.wait()
        value = near_vectors[k][...].astype(F32)
        value = value.reshape(1, value.shape[0])
        if k < 6:
            vectors[k : k + 1, :] = value
        elif k < 11:
            wide_vectors[k - 6 : k - 5, :] = value
        else:
            class_bias[...] = value
    copies[0].wait()
    copies[1].wait()
    acc[...] = plain(roi[...], wr[...])
    inv1, offset1, base = centre(acc, x1, grid_side, boxes)
    inv[0:1, :], inv[1:2, :] = inv1, offset1
    factor, term = scaled(inv1, base + offset1, vectors[0:1, :], vectors[1:2, :])

    def first(k, w, rows, carry):
        h = acc[rows, :] * factor + term
        hidden[k + 1, w + 1] = (h + h * jnp.tanh(h)).astype(BF16)
        return carry

    by_cells(grid_side, boxes, first, 0)
    copies[2].wait()
    for p in range(3):
        for q in range(3):
            taps = hidden[p : p + grid_side, q : q + grid_side].reshape(acc.shape)
            product = plain(taps, w9[p * 3 + q])
            if p + q == 0:
                acc[...] = product
            else:
                acc[...] += product
    inv2, offset2, base2 = centre(acc, x2, grid_side, boxes)
    inv[2:3, :], inv[3:4, :] = inv2, offset2
    factor2, term2 = scaled(inv2, base2 + offset2, vectors[2:3, :], vectors[3:4, :])

    def second(k, w, rows, carry):
        h = acc[rows, :] * factor2 + term2
        middle[rows, :] = (h + h * jnp.tanh(h)).astype(BF16)
        return carry

    by_cells(grid_side, boxes, second, 0)
    for copy in copies[3:6]:
        copy.wait()
    att = kw.shape[1]
    window[:, :att] = plain(bank[...], kw[...]).astype(BF16)
    window[:, att:] = plain(bank[...], vw[...]).astype(BF16)


def trunk(roi, wr, w9, bank, kw, vw, *vectors, grid_side, boxes):
    rows, mid = roi.shape[0], wr.shape[1]
    side = grid_side + 2
    return pl.pallas_call(
        functools.partial(trunk_kernel, grid_side, boxes),
        in_specs=[FAR] * 18,
        out_specs=[ON_CHIP] * 10,
        out_shape=[
            pltpu.VMEM(roi.shape, BF16),
            pltpu.VMEM((rows, mid), BF16),
            pltpu.VMEM((side, side, boxes, mid), BF16),
            pltpu.VMEM((rows, mid), BF16),
            pltpu.VMEM((rows, mid), BF16),
            jax.ShapeDtypeStruct((4, mid), F32),
            jax.ShapeDtypeStruct((bank.shape[0], 2 * kw.shape[1]), BF16),
            jax.ShapeDtypeStruct((6, mid), F32),
            jax.ShapeDtypeStruct((5, vectors[6].shape[0]), F32),
            jax.ShapeDtypeStruct((1, vectors[11].shape[0]), F32),
        ],
        scratch_shapes=[pltpu.VMEM(v.shape, BF16) for v in (wr, w9, bank, kw, vw)]
        + [pltpu.VMEM((rows, mid), F32), pltpu.SemaphoreType.DMA((18,))]
        + [pltpu.VMEM(v.shape, BF16) for v in vectors],
        compiler_params=params(18),
        cost_estimate=BRIEF,
        name="trunk",
    )(*outside(roi, wr, w9, bank, kw, vw, *vectors))


def widen_kernel(grid_side, boxes, order, roi, middle, ws_far, we_far, vectors, *rest):
    xs, (inv, feature, ws, we, acc_e, acc_p, sems) = rest[:8], rest[8:]
    width = acc_e.shape[1]
    at = [pl.ds(pl.multiple_of(order[k] * width, width), width) for k in range(4)]
    copies = start_copies(
        [pair for k in range(4) for pair in ((ws_far.at[:, at[k]], ws.at[k]), (we_far.at[:, at[k]], we.at[k]))],
        sems,
    )
    for k in range(4):
        xe, xp = xs[2 * k], xs[2 * k + 1]
        copies[2 * k].wait()
        acc_p[...] = plain(roi[...], ws[k])
        copies[2 * k + 1].wait()
        acc_e[...] = plain(middle[...], we[k])
        inv_p, offset_p, base_p = centre(acc_p, xp, grid_side, boxes)
        inv_e, offset_e, base_e = centre(acc_e, xe, grid_side, boxes)
        for row, value in enumerate((inv_e, inv_p, offset_e, offset_p)):
            inv[k, row : row + 1, :] = value
        factor_e, term_e = scaled(inv_e, base_e + offset_e, vectors[0:1, at[k]], vectors[1:2, at[k]])
        factor_p, term_p = scaled(inv_p, base_p + offset_p, vectors[2:3, at[k]], vectors[3:4, at[k]])
        term = term_e + term_p

        def line(row, total):
            for w in range(grid_side):
                rows = pl.ds((row * grid_side + w) * boxes, boxes)
                h = acc_e[rows, :] * factor_e + acc_p[rows, :] * factor_p + term
                total = total + (h + h * jnp.tanh(h))
            return total

        total = lax.fori_loop(0, grid_side, line, jnp.zeros((boxes, width), F32))
        feature[:, at[k]] = total / (grid_side * grid_side)


def widen(order, roi, middle, ws, we, vectors, grid_side, boxes):
    rows, width_in = roi.shape
    mid, out = we.shape
    tile = out // 4
    return pl.pallas_call(
        functools.partial(widen_kernel, grid_side, boxes),
        in_specs=[SCALARS, ON_CHIP, ON_CHIP, FAR, FAR, ON_CHIP],
        out_specs=[ON_CHIP] * 10,
        out_shape=[pltpu.VMEM((rows, tile), BF16)] * 8
        + [jax.ShapeDtypeStruct((4, 4, tile), F32), jax.ShapeDtypeStruct((boxes, out), F32)],
        scratch_shapes=[
            pltpu.VMEM((4, width_in, tile), BF16),
            pltpu.VMEM((4, mid, tile), BF16),
            pltpu.VMEM((rows, tile), F32),
            pltpu.VMEM((rows, tile), F32),
            pltpu.SemaphoreType.DMA((8,)),
        ],
        compiler_params=params(18),
        cost_estimate=BRIEF,
        name="widen",
    )(order, *kept(roi, middle), *outside(ws, we), vectors)


def doubled_slope(h):
    t = jnp.tanh(h)
    return (1.0 + t) * (1.0 + h * (1.0 - t))


def narrow_part(
    grid_side, boxes, k, order, roi, middle, xe, xp, we, inv, vectors, dfeature, part, dprojected, sums,
    upstream, dexpanded,
):
    rows, width = upstream.shape
    columns = pl.ds(pl.multiple_of(order[k] * width, width), width)
    gain_e, gain_p = vectors[0:1, columns], vectors[2:3, columns]
    inv_e, inv_p, offset_e, offset_p = [inv[k, row : row + 1, :] for row in range(4)]
    factor_e, term_e = scaled(inv_e, offset_e, gain_e, vectors[1:2, columns])
    factor_p, term_p = scaled(inv_p, offset_p, gain_p, vectors[3:4, columns])
    term = term_e + term_p
    slope_scale = dfeature[:, columns] * (0.5 / (grid_side * grid_side))

    def line(row, carry):
        sums = None
        for w in range(grid_side):
            at = pl.ds((row * grid_side + w) * boxes, boxes)
            e, p = xe[at, :].astype(F32), xp[at, :].astype(F32)
            u = doubled_slope(e * factor_e + p * factor_p + term) * slope_scale
            upstream[at, :] = u
            new = (u, u * e, u * p)
            sums = new if sums is None else [a + b for a, b in zip(sums, new)]
        return [a + fold(b) for a, b in zip(carry, sums)]

    zero = jnp.zeros((8, width), F32)
    total, total_e, total_p = [total_rows(v) for v in lax.fori_loop(0, grid_side, line, [zero] * 3, unroll=True)]
    ue, ce, te, gain_gradient_e = input_gradient(inv_e, offset_e, gain_e, total, total_e, rows)
    up, cp, tp, gain_gradient_p = input_gradient(inv_p, offset_p, gain_p, total, total_p, rows)
    sums[0:1, :] = gain_gradient_e
    sums[1:2, :] = total
    sums[2:3, :] = gain_gradient_p

    def second(row, w, at, carry):
        u = upstream[at, :]
        dexpanded[at, :] = (u * ue + xe[at, :].astype(F32) * ce + te).astype(BF16)
        dprojected[at, :] = (u * up + xp[at, :].astype(F32) * cp + tp).astype(BF16)
        return carry

    for row in range(grid_side):
        for w in range(grid_side):
            second(row, w, pl.ds((row * grid_side + w) * boxes, boxes), 0)
    split = roi.shape[1]
    part[0:split, :] = over_rows(roi[...], dprojected[...]).astype(BF16)
    part[split:, :] = over_rows(middle[...], dexpanded[...]).astype(BF16)
    return over_columns(dexpanded[...], we[...])


def expand_columns(order, ks, we_far, we, sems):
    width = we.shape[2]
    columns = [pl.ds(pl.multiple_of(order[k] * width, width), width) for k in ks]
    return start_copies([(we_far.at[:, at], we.at[n]) for n, at in enumerate(columns)], sems)


def narrow_kernel(grid_side, boxes, ks, order, roi, middle, inv, vectors, dfeature, we_far, *rest):
    count = len(ks)
    xs, rest = rest[: 2 * count], rest[2 * count :]
    *before, dmiddle = rest[: -4 - 3 * count]
    outs, (we, upstream, dexpanded, sems) = rest[-4 - 3 * count : -4], rest[-4:]
    copies = expand_columns(order, ks, we_far, we, sems)
    for n, k in enumerate(ks):
        copies[n].wait()
        back = narrow_part(
            grid_side, boxes, k, order, roi, middle, xs[2 * n], xs[2 * n + 1], we.at[n], inv, vectors, dfeature,
            *outs[3 * n : 3 * n + 3], upstream, dexpanded,
        )
        if n == 0:
            dmiddle[...] = before[0][...] + back if before else back
        else:
            dmiddle[...] += back


def narrow(order, roi, middle, inv, vectors, dfeature, we, *rest, ks, grid_side, boxes):
    rows, width_in = roi.shape
    mid, out = we.shape
    tile = out // 4
    xs, before = rest[: 2 * len(ks)], rest[2 * len(ks) :]
    return pl.pallas_call(
        functools.partial(narrow_kernel, grid_side, boxes, ks),
        in_specs=[SCALARS] + [ON_CHIP] * 5 + [FAR] + [ON_CHIP] * len(rest),
        out_specs=[ON_CHIP] * (1 + 3 * len(ks)),
        out_shape=[pltpu.VMEM((rows, mid), F32)]
        + [
            jax.ShapeDtypeStruct((width_in + mid, tile), BF16),
            pltpu.VMEM((rows, tile), BF16),
            jax.ShapeDtypeStruct((3, tile), F32),
        ]
        * len(ks),
        input_output_aliases={7 + 2 * len(ks): 0} if before else {},
        scratch_shapes=[
            pltpu.VMEM((len(ks), mid, tile), BF16),
            pltpu.VMEM((rows, tile), F32),
            pltpu.VMEM((rows, tile), BF16),
            pltpu.SemaphoreType.DMA((len(ks),)),
        ],
        compiler_params=params(16),
        cost_estimate=BRIEF,
        name="narrow",
    )(order, *kept(roi, middle), inv, vectors, dfeature, *outside(we), *kept(*xs, *before))


def norm_back(grid_side, boxes, upstream, centred, inv, offset, gain, shift, low, sums, store):
    rows, width = upstream.shape
    factor, term = scaled(inv, offset, gain, shift)

    def line(row, carry):
        sums = None
        for w in range(grid_side):
            at = pl.ds((row * grid_side + w) * boxes, boxes)
            c = centred[at, :].astype(F32)
            u = doubled_slope(c * factor + term) * (0.5 * upstream[at, :])
            low[at, :] = u
            new = (u, u * c)
            sums = new if sums is None else [a + b for a, b in zip(sums, new)]
        return [a + fold(b) for a, b in zip(carry, sums)]

    zero = jnp.zeros((8, width), F32)
    total, total_c = [total_rows(v) for v in lax.fori_loop(0, grid_side, line, [zero] * 2)]
    of_upstream, of_centred, term, gain_gradient = input_gradient(inv, offset, gain, total, total_c, rows)
    sums[0:1, :] = gain_gradient
    sums[1:2, :] = total

    def second(row, w, at, carry):
        value = low[at, :] * of_upstream + centred[at, :].astype(F32) * of_centred + term
        store(row, w, at, value.astype(BF16))
        return carry

    by_cells(grid_side, boxes, second, 0)


def spatial_taps(grid_side, side, core, hidden, dflat, part, away, keep):
    rows, width = dflat.shape
    half, quarter = width // 2, width // 4
    mine = pl.ds(pl.multiple_of(core * quarter, quarter), quarter)
    other = pl.ds(pl.multiple_of((1 - core) * quarter, quarter), quarter)
    columns = dflat[:, pl.ds(pl.multiple_of(side * half, half), half)]
    for p in range(3):
        for q in range(3):
            taps = hidden[p : p + grid_side, q : q + grid_side].reshape(rows, width)
            part[...] = over_rows(taps, columns).astype(BF16)
            lines = slice((p * 3 + q) * quarter, (p * 3 + q + 1) * quarter)
            for k in range(4):
                lanes = slice(k * quarter, (k + 1) * quarter)
                keep[lines, lanes] = part[lanes, mine]
                away[lines, lanes] = part[lanes, other]


def spatial_far_kernel(
    grid_side, boxes, order, place, roi, middle, inv_out, wide_vectors, dfeature, we_far, xe, xp, before,
    x2, hidden, inv, vectors, part, dprojected, wide_sums, away, keep, dconv, dflat, sums,
    we, upstream, dexpanded, taps, sems,
):
    copies = expand_columns(order, (3,), we_far, we, sems)
    clear_border(dconv)
    copies[0].wait()
    back = narrow_part(
        grid_side, boxes, 3, order, roi, middle, xe, xp, we.at[0], inv_out, wide_vectors, dfeature,
        part, dprojected, wide_sums, upstream, dexpanded,
    )
    upstream[...] = before[...] + back

    def store(row, w, at, value):
        dconv[row + 1, w + 1] = value
        dflat[at, :] = value

    norm_back(
        grid_side, boxes, upstream, x2, inv[2:3, :], inv[3:4, :], vectors[2:3, :], vectors[3:4, :], upstream, sums, store
    )
    spatial_taps(grid_side, 1 - place[2], place[3], hidden, dflat, taps, away, keep)


def spatial_far(
    order, place, roi, middle, inv_out, wide_vectors, dfeature, we, xe, xp, before, x2, hidden, inv, vectors,
    grid_side, boxes,
):
    rows, width_in = roi.shape
    mid, out = we.shape
    tile, side = out // 4, grid_side + 2
    taps = jax.ShapeDtypeStruct((9 * (mid // 4), mid), BF16)
    return pl.pallas_call(
        functools.partial(spatial_far_kernel, grid_side, boxes),
        in_specs=[SCALARS] * 2 + [ON_CHIP] * 5 + [FAR] + [ON_CHIP] * 7,
        out_specs=[ON_CHIP] * 8,
        out_shape=[
            jax.ShapeDtypeStruct((width_in + mid, tile), BF16),
            pltpu.VMEM((rows, tile), BF16),
            jax.ShapeDtypeStruct((3, tile), F32),
            taps,
            taps,
            pltpu.VMEM((side, side, boxes, mid), BF16),
            pltpu.VMEM((rows, mid), BF16),
            jax.ShapeDtypeStruct((2, mid), F32),
        ],
        scratch_shapes=[
            pltpu.VMEM((1, mid, tile), BF16),
            pltpu.VMEM((rows, tile), F32),
            pltpu.VMEM((rows, tile), BF16),
            pltpu.VMEM((mid, mid // 2), BF16),
            pltpu.SemaphoreType.DMA((1,)),
        ],
        compiler_params=params(18),
        cost_estimate=BRIEF,
        name="spatial_far",
    )(
        order, place, *kept(roi, middle), inv_out, wide_vectors, dfeature, *outside(we), *kept(xe, xp, before, x2, hidden),
        inv, vectors,
    )


def spatial_near_kernel(grid_side, place, hidden, dflat, dconv, w9_far, away, keep, dhidden, part, w9, sems):
    copies = start_copies([(w9_far.at[k], w9.at[k]) for k in range(6)], sems)
    rows, width = dflat.shape
    for p in range(2):
        for q in range(3):
            copies[p * 3 + q].wait()
            taps = dconv[2 - p : 2 - p + grid_side, 2 - q : 2 - q + grid_side].reshape(rows, width)
            product = over_columns(taps, w9[p * 3 + q])
            if p + q == 0:
                dhidden[...] = product
            else:
                dhidden[...] += product
    spatial_taps(grid_side, place[2], place[3], hidden, dflat, part, away, keep)


def spatial_near(place, hidden, dflat, dconv, w9, grid_side):
    rows, mid = dflat.shape
    taps = jax.ShapeDtypeStruct((9 * (mid // 4), mid), BF16)
    return pl.pallas_call(
        functools.partial(spatial_near_kernel, grid_side),
        in_specs=[SCALARS] + [ON_CHIP] * 3 + [FAR],
        out_specs=[ON_CHIP] * 3,
        out_shape=[taps, taps, pltpu.VMEM((rows, mid), F32)],
        scratch_shapes=[
            pltpu.VMEM((mid, mid // 2), BF16),
            pltpu.VMEM((6, mid, mid), BF16),
            pltpu.SemaphoreType.DMA((6,)),
        ],
        compiler_params=params(16),
        cost_estimate=BRIEF,
        name="spatial_near",
    )(place, *kept(hidden, dflat, dconv), *outside(w9))


def reduce_back_kernel(
    grid_side, boxes, order, dhidden, dconv, x1, roi, w9_far, inv, vectors, spatial_sums, norm_sums, bias_sums, class_sums,
    s0, s1, s2, s3, dreduced, away, keep, upstream, w9, weight, sums, sems,
):
    rows, width = upstream.shape
    copies = start_copies([(w9_far.at[6 + q], w9.at[q]) for q in range(3)], sems)
    for q in range(3):
        copies[q].wait()
        taps = dconv[0:grid_side, 2 - q : 2 - q + grid_side].reshape(rows, width)
        product = over_columns(taps, w9[q])
        if q == 0:
            upstream[...] = dhidden[...] + product
        else:
            upstream[...] += product

    def store(row, w, at, value):
        dreduced[at, :] = value

    norm_back(
        grid_side, boxes, upstream, x1, inv[0:1, :], inv[1:2, :], vectors[0:1, :], vectors[1:2, :], upstream, sums, store
    )
    weight[...] = over_rows(dreduced[...], roi[...]).astype(BF16)
    quarter, classes = width // 4, class_sums.shape[1]
    size = away.shape[0] // 2
    for k, (target, wide_sums) in enumerate(((away, s0), (keep, s1), (away, s2), (keep, s3))):
        base = (k // 2) * size
        lines = pl.ds(pl.multiple_of(order[k] * quarter, quarter), quarter)
        wide = pl.ds(pl.multiple_of(order[k] * width, width), width)
        target[base : base + quarter, :] = weight[lines, :width]
        target[base + quarter : base + 2 * quarter, :] = weight[lines, width:]
        line0 = [v[r : r + 1, lines] for v in (sums, spatial_sums) for r in range(2)]
        line1 = [norm_sums[r : r + 1, lines] for r in range(2)]
        line1 += [class_sums[...], jnp.zeros((1, width - 2 * quarter - classes), F32)]
        tail = jnp.concatenate(
            [
                jnp.concatenate(line0, axis=1),
                jnp.concatenate(line1, axis=1),
                wide_sums[...],
                bias_sums[:, wide],
                jnp.zeros((10, width), F32),
            ]
        )
        target[base + 2 * quarter : base + size, :] = tail.astype(BF16)


def reduce_back(order, dhidden, dconv, x1, roi, w9, inv, vectors, *sums, grid_side, boxes):
    rows, width_in = roi.shape
    mid = dhidden.shape[1]
    part = jax.ShapeDtypeStruct((2 * (mid // 2 + 16), mid), BF16)
    return pl.pallas_call(
        functools.partial(reduce_back_kernel, grid_side, boxes),
        in_specs=[SCALARS] + [ON_CHIP] * 4 + [FAR] + [ON_CHIP] * 10,
        out_specs=[ON_CHIP] * 3,
        out_shape=[pltpu.VMEM((rows, mid), BF16), part, part],
        scratch_shapes=[
            pltpu.VMEM((rows, mid), F32),
            pltpu.VMEM((3, mid, mid), BF16),
            pltpu.VMEM((mid, width_in), BF16),
            pltpu.VMEM((2, mid), F32),
            pltpu.SemaphoreType.DMA((3,)),
        ],
        compiler_params=params(20),
        cost_estimate=BRIEF,
        name="reduce_back",
    )(order, *kept(dhidden, dconv, x1, roi), *outside(w9), inv, vectors, *sums)


def roi_back_kernel(half, order, dreduced, d0, d1, d2, d3, wr_far, ws_far, *rest):
    out, wr, ws, acc, low, sems = rest[-6:]
    tile = d0.shape[1]
    size = acc.shape[1]
    lines = pl.ds(half * size, size)
    columns = [pl.ds(pl.multiple_of(order[k] * tile, tile), tile) for k in range(4)]
    copies = start_copies(
        [(wr_far.at[lines, :], wr)] + [(ws_far.at[lines, columns[k]], ws.at[k]) for k in range(4)], sems
    )
    copies[0].wait()
    acc[...] = over_columns(dreduced[...], wr[...])
    for k, d in enumerate((d0, d1, d2, d3)):
        copies[k + 1].wait()
        acc[...] += over_columns(d[...], ws[k])
    low[...] = acc[...].astype(BF16)
    pltpu.sync_copy(low, out.at[:, lines])


def roi_back(order, dreduced, dprojected, wr, ws, *done, half):
    rows, mid = dreduced.shape
    width_in, out = ws.shape
    size = width_in // 2
    return pl.pallas_call(
        functools.partial(roi_back_kernel, half),
        in_specs=[SCALARS] + [ON_CHIP] * 5 + [FAR] * (2 + len(done)),
        out_specs=FAR,
        out_shape=pltpu.HBM((rows, width_in), BF16),
        input_output_aliases={8: 0} if done else {},
        scratch_shapes=[
            pltpu.VMEM((size, mid), BF16),
            pltpu.VMEM((4, size, out // 4), BF16),
            pltpu.VMEM((rows, size), F32),
            pltpu.VMEM((rows, size), BF16),
            pltpu.SemaphoreType.DMA((5,)),
        ],
        compiler_params=params(18),
        cost_estimate=BRIEF,
        name="roi_back",
    )(order, *kept(dreduced, *dprojected), *outside(wr, ws, *done))


def head_kernel(
    all_seconds, place, seconds, lengths, feature, w0, w1, w2, w3, w4, wq_far, wo_far, wc_far,
    mid_vectors, vectors, class_bias, cotangent,
    logits, dfeature, pack, norm_sums, bias_sums, class_sums, window, wq, wo, wc, sems,
):
    copies = start_copies([(wq_far, wq), (wo_far, wo), (wc_far, wc)], sems)
    att = wq.shape[1]
    boxes, out = feature.shape
    classes = cotangent.shape[1]
    span = window.shape[0]
    rows = w0.shape[0]
    for k, w in enumerate((w0, w1, w2, w3, w4)):
        window[k * rows : (k + 1) * rows, :] = w[...]
    scale = att ** (-0.5)
    norm_gain, norm_shift = mid_vectors[4:5, :], mid_vectors[5:6, :]

    row_seconds = lax.broadcasted_iota(jnp.int32, (boxes, span), 1) // PER_SEC + (place[0] - REACH) * SEC_DEV
    line = lax.broadcasted_iota(jnp.int32, (boxes, 128), 0)
    box_seconds = jnp.zeros((boxes, 128), jnp.int32)
    for k in range(boxes):
        box_seconds = jnp.where(line == k, seconds[k], box_seconds)
    box_seconds = box_seconds[:, 0:1]
    live = (row_seconds >= 0) & (row_seconds < all_seconds) & (jnp.abs(box_seconds - row_seconds) <= HALF)
    end = 0
    for k in range(lengths.shape[0]):
        end = end + lengths[k]
        live = live & ((end <= row_seconds) == (end <= box_seconds))

    copies[0].wait()
    feature_low = feature[...].astype(BF16)
    pack[:, :out] = feature_low
    queries = plain(feature_low, wq[...]).astype(BF16)
    keys, values = window[:, :att], window[:, att:]
    scores = over_columns(queries, keys) * scale
    top = jnp.max(jnp.where(live, scores, -1e30), axis=1, keepdims=True)
    exps = jnp.where(live, jnp.exp(jnp.where(live, scores - top, 0.0)), 0.0)
    probs = exps / jnp.sum(exps, axis=1, keepdims=True)
    probs_low = probs.astype(BF16)
    pre = plain(probs_low, values) + queries.astype(F32)
    centred = pre - jnp.mean(pre, axis=1, keepdims=True)
    inv = lax.rsqrt(jnp.mean(centred * centred, axis=1, keepdims=True) + EPSILON)
    x = centred * inv
    h = 0.5 * (x * norm_gain + norm_shift)
    activated = (h + h * jnp.tanh(h)).astype(BF16)
    copies[1].wait()
    combined_low = (feature[...] + plain(activated, wo[...]) + vectors[4:5, :]).astype(BF16)
    pack[:, out : 2 * out] = combined_low
    copies[2].wait()
    logits[...] = over_columns(feature_low, wc[:, :out]) + over_columns(combined_low, wc[:, out:]) + class_bias[...]
    g = cotangent[...].astype(BF16)
    class_sums[...] = jnp.sum(g.astype(F32), axis=0, keepdims=True)
    first = plain(g, wc[:, :out])
    second = plain(g, wc[:, out:])
    gb = second.astype(BF16)
    pack[:, 2 * out : 3 * out] = gb
    bias_sums[...] = jnp.sum(gb.astype(F32), axis=0, keepdims=True)
    u = over_columns(gb, wo[...]) * (0.5 * doubled_slope(h))
    norm_sums[0:1, :] = jnp.sum(u * x, axis=0, keepdims=True)
    norm_sums[1:2, :] = jnp.sum(u, axis=0, keepdims=True)
    e = u * norm_gain
    dpre = inv * (e - jnp.mean(e, axis=1, keepdims=True) - x * jnp.mean(e * x, axis=1, keepdims=True))
    da = dpre.astype(BF16)
    dprobs = over_columns(da, values)
    delta = jnp.sum(probs * dprobs, axis=1, keepdims=True)
    ds = (probs * (dprobs - delta)).astype(BF16)
    dq = (plain(ds, keys) * scale + dpre).astype(BF16)
    at = 3 * out
    for value in (dq, activated, queries, da):
        pack[:, at : at + att] = value
        at += att
    pack[:, at : at + 128] = jnp.zeros((boxes, 128), BF16)
    pack[:, at : at + classes] = g
    at += 128
    pack[:, at : at + span] = ds
    pack[:, at + span :] = probs_low
    dfeature[...] = first + second + over_columns(dq, wq[...])


def head(place, seconds, lengths, feature, windows, wq, wo, wc, mid_vectors, vectors, class_bias, cotangent, all_seconds):
    boxes, out = feature.shape
    att = wq.shape[1]
    classes = wc.shape[0]
    span = sum(w.shape[0] for w in windows)
    shapes = [
        ((boxes, classes), F32),
        ((boxes, out), F32),
        ((boxes, 3 * out + 4 * att + 128 + 2 * span), BF16),
        ((2, att), F32),
        ((1, out), F32),
        ((1, classes), F32),
    ]
    return pl.pallas_call(
        functools.partial(head_kernel, all_seconds),
        in_specs=[SCALARS] * 3 + [ON_CHIP] * 6 + [FAR] * 3 + [ON_CHIP] * 4,
        out_specs=[ON_CHIP] * len(shapes),
        out_shape=[jax.ShapeDtypeStruct(s, d) for s, d in shapes],
        scratch_shapes=[
            pltpu.VMEM((span, 2 * att), BF16),
            pltpu.VMEM(wq.shape, BF16),
            pltpu.VMEM(wo.shape, BF16),
            pltpu.VMEM(wc.shape, BF16),
            pltpu.SemaphoreType.DMA((3,)),
        ],
        compiler_params=params(16),
        cost_estimate=BRIEF,
        name="head",
    )(place, seconds, lengths, feature, *windows, *outside(wq, wo, wc), mid_vectors, vectors, class_bias, cotangent)


def halves(place, bit, value, sent, kept):
    size = sent.shape[0]
    mine = place[4 + bit]
    sent[...] = value[pl.ds(pl.multiple_of((1 - mine) * size, 16), size), :]
    kept[...] = value[pl.ds(pl.multiple_of(mine * size, 16), size), :]


def small_weights_kernel(
    grouped, place, pair, far_pair, pair_bank, far_bank, keep, away, sent_a, kept_a, sent_b, kept_b, wide_a, wide_b,
    pack, banks, dbank, first, second,
):
    cut = wide_a.shape[0]
    wide_a[...] = keep[:cut, :] + away[:cut, :]
    wide_b[...] = keep[cut:, :] + away[cut:, :]
    boxes = pair.shape[0] // 2
    for k, source in ((place[3], pair), (1 - place[3], far_pair)):
        for half in range(2):
            lines = pl.ds(pl.multiple_of((2 * half + k) * boxes, 16), boxes)
            pack[lines, :] = source[half * boxes : (half + 1) * boxes, :]
    rows = pair_bank.shape[0] // 4
    for k, source in ((place[3], pair_bank), (1 - place[3], far_bank)):
        for block in range(4):
            lines = pl.ds(pl.multiple_of((2 * block + k) * rows, 16), rows)
            banks[lines, :] = source[block * rows : (block + 1) * rows, :]
    width = first.shape[1]
    att, out, piece = width, banks.shape[1], width // 4
    span = (2 * REACH + 1) * rows
    q = place[1]
    columns = lambda base, size: pl.ds(pl.multiple_of(base + q * size, size), size)
    base = 3 * out
    at = base + 4 * att + 128
    dbank[...] = jnp.zeros(dbank.shape, F32)
    for k in range(grouped):
        lines, window = slice(k * boxes, (k + 1) * boxes), slice(k * rows, k * rows + span)
        ds, probs = pack[lines, at : at + span], pack[lines, at + span : at + 2 * span]
        dbank[window, :piece] += over_rows(ds, pack[lines, columns(base + 2 * att, piece)]) * att ** (-0.5)
        dbank[window, piece:] += over_rows(probs, pack[lines, columns(base + 3 * att, piece)])
    for left, right, target, row in (
        (pack[:, columns(base, piece)], pack[:, :out], first, 0),
        (dbank[:, :piece].astype(BF16), banks[...], first, att),
        (dbank[:, piece:].astype(BF16), banks[...], second, 0),
    ):
        product = over_rows(left, right).astype(BF16)
        for k in range(out // width):
            target[row + k * piece : row + (k + 1) * piece, :] = product[:, k * width : (k + 1) * width]
    second[att : 2 * att, :] = over_rows(
        pack[:, base + att : base + 2 * att], pack[:, columns(2 * out, out // 4)]
    ).astype(BF16)
    at = base + 4 * att
    product = over_rows(pack[:, at : at + 128], pack[:, columns(0, out // 2)]).astype(BF16)
    first[2 * att :, :] = product[:, :width]
    second[2 * att :, :] = product[:, width:]
    halves(place, 0, first, sent_a, kept_a)
    halves(place, 0, second, sent_b, kept_b)


def small_weights(place, pair, far_pair, pair_bank, far_bank, keep, away, cut, att, grouped):
    rows, out = 2 * att + 128, pair_bank.shape[1]
    reach = 2 * pair_bank.shape[0]
    return pl.pallas_call(
        functools.partial(small_weights_kernel, grouped),
        in_specs=[SCALARS] + [ON_CHIP] * 6,
        out_specs=[ON_CHIP] * 6,
        out_shape=[jax.ShapeDtypeStruct((rows // 2, att), BF16)] * 4
        + [jax.ShapeDtypeStruct((size, keep.shape[1]), BF16) for size in (cut, keep.shape[0] - cut)],
        scratch_shapes=[
            pltpu.VMEM((2 * pair.shape[0], pair.shape[1]), BF16),
            pltpu.VMEM((reach, out), BF16),
            pltpu.VMEM((reach, att // 2), F32),
            pltpu.VMEM((rows, att), BF16),
            pltpu.VMEM((rows, att), BF16),
        ],
        compiler_params=params(20),
        cost_estimate=BRIEF,
        name="small_weights",
    )(place, pair, far_pair, pair_bank, far_bank, *outside(keep, away))


class View:
    def __init__(self, array, at=0, rows=None):
        self.array, self.at = array, at
        self.rows = array.shape[0] if rows is None else rows

    @property
    def shape(self):
        return (self.rows, *self.array.shape[1:])

    def of(self, array):
        return View(array, self.at, self.rows)


def view(value):
    return value if isinstance(value, View) else View(value)


class Task:
    def __init__(self, run, inputs, outputs, scratch=()):
        self.run, self.scratch = run, list(scratch)
        self.inputs = [view(v) for v in inputs]
        self.outputs = [out if isinstance(out[0], tuple) else (out, None) for out in outputs]


def distinct(views):
    arrays, places = [], []
    for v in views:
        found = [k for k, array in enumerate(arrays) if array is v.array]
        places.append(found[0] if found else len(arrays))
        if not found:
            arrays.append(v.array)
    return arrays, places


def rows_of(ref, v):
    return ref if v.rows == v.array.shape[0] else ref.at[v.at : v.at + v.rows]


def step(place, tasks):
    arrays, places = distinct([v for t in tasks for v in t.inputs])
    shapes, boxes, outputs = [], {}, []
    for task in tasks:
        for shape, way in task.outputs:
            if way is None:
                shapes.append(list(shape))
                outputs.append((len(shapes) - 1, 0, shape[0]))
            else:
                if way not in boxes:
                    boxes[way] = len(shapes)
                    shapes.append([0, shape[1]])
                box = shapes[boxes[way]]
                outputs.append((boxes[way], box[0], shape[0]))
                box[0] += shape[0]

    def kernel(place_ref, *refs):
        ins, outs, scratch = refs[: len(arrays)], refs[len(arrays) : len(arrays) + len(shapes)], refs[len(arrays) + len(shapes) :]
        where, made = list(places), list(outputs)
        for task in tasks:
            sources = [rows_of(ins[where.pop(0)], v) for v in task.inputs]
            targets = []
            for _ in task.outputs:
                k, at, rows = made.pop(0)
                targets.append(outs[k] if rows == shapes[k][0] else outs[k].at[at : at + rows])
            task.run(place_ref, *sources, *targets, *scratch[: len(task.scratch)])
            scratch = scratch[len(task.scratch) :]

    results = pl.pallas_call(
        kernel,
        in_specs=[SCALARS] + [ON_CHIP] * len(arrays),
        out_specs=[ON_CHIP] * len(shapes),
        out_shape=[jax.ShapeDtypeStruct(tuple(shape), BF16) for shape in shapes],
        scratch_shapes=[pltpu.VMEM(shape, BF16) for t in tasks for shape in t.scratch],
        compiler_params=params(16),
        cost_estimate=BRIEF,
        name="step",
    )(place, *arrays)
    made = [View(results[k], at, rows) for k, at, rows in outputs]
    grouped = []
    for task in tasks:
        grouped.append(made[: len(task.outputs)])
        made = made[len(task.outputs) :]
    return grouped


def add_task(a, b, way=None):
    def run(place, x, y, total):
        total[...] = x[...] + y[...]

    return Task(run, (a, b), [(view(a).shape, way)])


HALVES, WHOLE, GATHER = range(3)
FIVE = [(0, HALVES), (1, HALVES), (2, WHOLE), (1, GATHER), (0, GATHER)]
FOUR = [(0, HALVES), (1, WHOLE), (2, WHOLE), (0, GATHER)]
THREE = [(0, WHOLE), (1, WHOLE), (2, WHOLE)]


class BankTotal:
    def __init__(self, sent, kept, plan):
        self.sent, self.kept, self.plan, self.stage = view(sent), view(kept), plan, 0

    @property
    def done(self):
        return self.stage == len(self.plan)

    def way(self, stage):
        return ("bank", 1 << self.plan[stage][0])

    def arrival(self, other):
        (bit, kind), (size, width) = self.plan[self.stage], self.kept.shape
        last = self.stage + 1 == len(self.plan)
        if last and kind == GATHER:
            return None
        way = None if last else self.way(self.stage + 1)
        if kind == GATHER:

            def gather(place, mine, other, joined):
                join(place, bit, mine, other, joined)

            return Task(gather, (self.kept, other), [((2 * size, width), way)])
        if last or self.plan[self.stage + 1][1] != HALVES:
            return add_task(self.kept, other, way)
        next_bit = self.plan[self.stage + 1][0]

        def add(place, kept, other, sent, left, total):
            total[...] = kept[...] + other[...]
            halves(place, next_bit, total, sent, left)

        half = (size // 2, width)
        return Task(add, (self.kept, other), [(half, way), half], [(size, width)])

    def land(self, other, results):
        if results is None:
            self.other = other
        else:
            self.sent, self.kept = results[0], results[-1]
            if self.plan[self.stage] == (2, WHOLE):
                self.sent = self.kept = beyond(self.kept)
        self.stage += 1


def beyond(value):
    size = lax.axis_size("bank")
    if size == 8:
        return value
    own = lax.slice_in_dim(value.array, value.at, value.at + value.rows)
    return View(lax.psum(own, "bank", axis_index_groups=[list(range(k, size, 8)) for k in range(8)]))


def join(place, bit, mine, other, joined):
    size = mine.shape[0]
    at = place[4 + bit]
    joined[pl.ds(pl.multiple_of(at * size, 16), size), :] = mine[...]
    joined[pl.ds(pl.multiple_of((1 - at) * size, 16), size), :] = other[...]


def emit(place, run, inputs, outputs, scratch, name):
    arrays, places = distinct(inputs)

    def kernel(place_ref, *refs):
        sources = [rows_of(refs[k], v) for k, v in zip(places, inputs)]
        run(place_ref, *sources, *refs[len(arrays) :])

    return pl.pallas_call(
        kernel,
        in_specs=[SCALARS] + [ON_CHIP] * len(arrays),
        out_specs=[ON_CHIP] * len(outputs),
        out_shape=[jax.ShapeDtypeStruct(shape, F32) for shape in outputs],
        scratch_shapes=[pltpu.VMEM(shape, BF16) for shape in scratch],
        compiler_params=params(20),
        cost_estimate=BRIEF,
        name=name,
    )(place, *arrays)


def emit_small(place, a, other_a, b, other_b, out, att, classes):
    piece = att // 4
    rows = 2 * att + 128

    def run(place, a, other_a, b, other_b, dquery, dkey, dvalue, doutput, dclass, first, second):
        join(place, 0, a, other_a, first)
        join(place, 0, b, other_b, second)
        for source, row, target in ((first, 0, dquery), (first, att, dkey), (second, 0, dvalue)):
            for k in range(out // att):
                block = source[row + k * piece : row + (k + 1) * piece, :].astype(F32)
                target[k * att : (k + 1) * att, :] = block.T
        doutput[...] = second[att : 2 * att, :].astype(F32)
        dclass[:, :att] = first[2 * att :, :].astype(F32)[:classes]
        dclass[:, att:] = second[2 * att :, :].astype(F32)[:classes]

    return emit(
        place,
        run,
        (a, other_a, b, other_b),
        [(out, piece)] * 3 + [(att, att), (classes, 2 * att)],
        [(rows, att)] * 2,
        "emit_small",
    )


def emit_wide(place, a, other_a, b, other_b, width_in, mid, tile):
    half = 2 * a.rows

    def run(place, a, other_a, b, other_b, shortcut, expand, joined):
        join(place, 0, a, other_a, joined.at[:half])
        join(place, 0, b, other_b, joined.at[half:])
        shortcut[...] = joined[:width_in, :].astype(F32)
        expand[...] = joined[width_in:, :].astype(F32)

    inputs = (a, other_a, b, other_b)
    shapes = [(width_in, tile), (mid, tile)]
    return emit(place, run, inputs, shapes, [(width_in + mid, tile)], "emit_wide")


def emit_last(place, flow_a, flow_b, last, width_in, mid, tile, classes):
    quarter = mid // 4
    rows_a, rows_b = 2 * flow_a.kept.rows, 2 * flow_b.kept.rows

    def run(place, a, other_a, b, other_b, rest, spatial, reduce, *targets):
        targets, taps = targets[:-1], targets[-1]
        join(place, 0, a, other_a, taps.at[:rows_a])
        join(place, 0, b, other_b, taps.at[rows_a:])
        for tap in range(9):
            for k in range(4):
                spatial[tap, k * quarter : (k + 1) * quarter, :] = taps[
                    tap * quarter : (tap + 1) * quarter, k * quarter : (k + 1) * quarter
                ].astype(F32)
        for k in range(2):
            reduce[k * mid : (k + 1) * mid, :] = rest[k * quarter : (k + 1) * quarter, :].astype(F32).T
        tail = rest[2 * quarter : 2 * quarter + 16, :].astype(F32)
        for k in range(4):
            targets[k][...] = tail[0:1, k * quarter : (k + 1) * quarter]
        for k in range(2):
            targets[4 + k][...] = tail[1:2, k * quarter : (k + 1) * quarter]
        targets[6][...] = tail[1:2, 2 * quarter : 2 * quarter + classes]
        for k in range(4):
            targets[7 + k][...] = tail[2 + k : 3 + k, :]
        targets[11][...] = tail[3:4, :]

    inputs = (flow_a.kept, flow_a.other, flow_b.kept, flow_b.other, last.kept)
    shapes = [(9, mid, quarter), (width_in, quarter)] + [(1, quarter)] * 6 + [(1, classes)] + [(1, tile)] * 5
    return emit(place, run, inputs, shapes, [(rows_a + rows_b, mid)], "emit_last")


def move(value, how):
    kind, by = how
    if kind == "edge":
        axis = ("bank", "box")
        size = lax.axis_size(axis)
        targets = [(i, i + by if i % by >= by // 2 else i - by) for i in range(size)]
        return lax.ppermute(value, axis, [(i, j) for i, j in targets if 0 <= j < size])
    if kind == "along":
        axis = ("bank", "box")
        size = lax.axis_size(axis)
        return lax.ppermute(value, axis, [(i, i + by) for i in range(size) if 0 <= i + by < size])
    return lax.ppermute(value, kind, [(i, i ^ by) for i in range(lax.axis_size(kind))])


def launch(moves):
    found, received = [], []
    for value, how in moves:
        same = [r for v, h, r in found if v is value.array and h == how]
        if not same:
            same = [move(value.array, how)]
            found.append((value.array, how, same[0]))
        received.append(value.of(same[0]))
    return received


def slot(place, kernel, inputs, moves=(), flows=(), tasks=None, late=()):
    flows = [flow for flow in flows if not flow.done]
    waits = [len(m) == 2 for m in moves] + [True] * len(flows)
    moves = [(view(m[0]), m[1]) for m in moves] + [(flow.sent, flow.way(flow.stage)) for flow in flows]
    arrays, places = distinct([value for value, _ in moves])
    inputs, arrays = lax.optimization_barrier((inputs, arrays))
    received = launch([(value.of(arrays[k]), how) for k, (value, how) in zip(places, moves)])
    results = kernel(*inputs) if kernel else ()
    waited = [v for v, wait in zip(received, waits) if wait] + list(late)
    arrays, places = distinct(waited)
    results, arrays = lax.optimization_barrier((results, arrays))
    waited = [v.of(arrays[k]) for v, k in zip(waited, places)]
    late = waited[len(waited) - len(late) :]
    received = [waited.pop(0) if wait else v for v, wait in zip(received, waits)]
    count = len(moves) - len(flows)
    arrivals, landed = received[:count] + late, received[count:]
    own = tasks(results, arrivals) if tasks else []
    pending = [flow.arrival(other) for flow, other in zip(flows, landed)]
    needed = own + [task for task in pending if task]
    outputs = step(place, needed) if needed else []
    made, outputs = outputs[: len(own)], outputs[len(own) :]
    for flow, task, other in zip(flows, pending, landed):
        flow.land(other, outputs.pop(0) if task else None)
    return results, arrivals, made


def local(
    roi_features,
    box_seconds,
    video_lengths,
    bank_features,
    reduce_weight,
    reduce_gain,
    reduce_shift,
    spatial_weight,
    spatial_gain,
    spatial_shift,
    expand_weight,
    expand_gain,
    expand_shift,
    shortcut_weight,
    shortcut_gain,
    shortcut_shift,
    query_weight,
    key_weight,
    value_weight,
    norm_gain,
    norm_shift,
    output_weight,
    output_bias,
    class_weight,
    class_bias,
    logit_cotangent,
):
    boxes, grid_side = roi_features.shape[:2]
    in_width = roi_features.shape[3]
    rows = boxes * grid_side * grid_side
    mid = reduce_weight.shape[1]
    out = expand_weight.shape[1]
    att = query_weight.shape[1]
    classes = class_weight.shape[1]
    tile, quarter = out // 4, mid // 4
    all_seconds = lax.axis_size(("bank", "box")) * SEC_DEV
    my_index = lax.axis_index(("bank", "box"))
    bank_index, box_index = lax.axis_index("bank"), lax.axis_index("box")
    core, side = box_index % 2, box_index // 2
    place = jnp.stack([my_index, box_index, side, core] + [(bank_index >> k) & 1 for k in range(3)])
    order = jnp.stack([(1 - side) * 2 + 1 - core, (1 - side) * 2 + core, side * 2 + 1 - core, side * 2 + core])
    shape = dict(grid_side=grid_side, boxes=boxes)
    on = functools.partial(slot, place)

    roi = roi_features.transpose(1, 2, 0, 3).reshape(rows, in_width)
    w9 = spatial_weight.reshape(9, mid, mid)
    place, order, roi = lax.optimization_barrier((place, order, roi))
    box_devices = lax.axis_size("box")
    results, (far_bank, edge), _ = on(
        functools.partial(trunk, **shape),
        (
            roi, reduce_weight, w9, bank_features, key_weight, value_weight,
            reduce_gain, reduce_shift, spatial_gain, spatial_shift, norm_gain, norm_shift,
            expand_gain, expand_shift, shortcut_gain, shortcut_shift, output_bias, class_bias,
        ),
        [(bank_features, ("box", 2)), (bank_features, ("edge", box_devices))],
    )
    roi, x1, hidden, x2, middle, inv_mid, own_window, mid_vectors, vectors, class_bias = results
    around = [by for by in range(-REACH, REACH + 1) if by != 0]

    (*xs, inv_out, feature), (*windows, far_edge), _ = on(
        functools.partial(widen, **shape),
        (order, roi, middle, shortcut_weight, expand_weight, vectors),
        [(own_window, ("along", -by)) for by in around] + [(edge, ("box", 2))],
    )
    windows = [w.array for w in windows]
    windows.insert(REACH, own_window)
    (logits, dfeature, pack, norm_sums, bias_sums, class_sums), _, _ = on(
        functools.partial(head, all_seconds=all_seconds),
        (
            place, box_seconds, video_lengths, feature, windows, query_weight, output_weight, class_weight.T,
            mid_vectors, vectors, class_bias, logit_cotangent,
        ),
    )

    def narrow_slot(ks, before, *rest, **more):
        operands = (order, roi, middle, inv_out, vectors, dfeature, expand_weight)
        operands += tuple(xs[2 * ks[0] : 2 * ks[-1] + 2]) + before
        return on(functools.partial(narrow, ks=ks, **shape), operands, *rest, **more)

    def pack_pair(results, arrivals):
        def run(place, pack, far_pack, both):
            size = pack.shape[0]
            both[pl.ds(pl.multiple_of(place[2] * size, 16), size), :] = pack[...]
            both[pl.ds(pl.multiple_of((1 - place[2]) * size, 16), size), :] = far_pack[...]

        def bundle(place, own, far, edge, far_edge, blocks):
            size = own.shape[0]
            upper = place[2] == 1
            pairs = ((edge, far_edge), (far, own), (own, far), (far_edge, edge))
            for k, (a, b) in enumerate(pairs):
                blocks[k * size : (k + 1) * size, :] = jnp.where(upper, a[...], b[...])

        size, width = pack.shape
        rows, features = bank_features.shape
        return [
            Task(run, (pack, arrivals[0]), [(2 * size, width)]),
            Task(bundle, (bank_features, far_bank, edge, far_edge), [(4 * rows, features)]),
        ]

    (dmiddle, away_far, d0, sums0, keep_far, d1, sums1), _, ((pair_pack,), (pair_bank,)) = narrow_slot(
        (0, 1), (), [(pack, ("box", 2))], tasks=pack_pair
    )
    half = 13 * (away_far.shape[0] // 24)

    (dmiddle, away_near, d2, sums2), (far_pair, wide_away, far_bundle), _ = narrow_slot(
        (2,),
        (dmiddle,),
        [(pair_pack, ("box", 1)), (away_far, ("box", 1)), (pair_bank, ("box", 1))],
    )
    gathered = [v.array for v in (pair_pack, far_pair, pair_bank, far_bundle)]
    sent_a, kept_a, sent_b, kept_b, wide_first, wide_last = small_weights(
        place, *gathered, keep_far, wide_away.array, half, att, box_devices
    )
    small_a, small_b = BankTotal(sent_a, kept_a, FIVE), BankTotal(sent_b, kept_b, FIVE)
    small = [small_a, small_b]
    (keep_near, d3, sums3, away_taps, keep_far_taps, dconv, dflat, spatial_sums), (near, far_first), _ = on(
        functools.partial(spatial_far, **shape),
        (
            order, place, roi, middle, inv_out, vectors, dfeature, expand_weight, xs[6], xs[7], dmiddle,
            x2, hidden, inv_mid, mid_vectors,
        ),
        [(away_near, ("box", 1)), (wide_first, ("box", 2))],
        [small_a],
    )

    def summed_halves(keep, away, far, at):
        rows = far.shape[0]

        def run(place, keep, away, far, sent, kept, total):
            total[...] = keep[at : at + rows, :] + away[at : at + rows, :] + far[...]
            halves(place, 0, total, sent, kept)

        size = (rows // 2, mid)
        return Task(run, (keep, away, far), [(size, ("bank", 1)), size], [(rows, mid)])

    cut = 5 * quarter

    def tap_parts(results, arrivals):
        def run(place, keep, away, first, second):
            first[...] = keep[:cut, :] + away[:cut, :]
            second[...] = keep[cut:, :] + away[cut:, :]

        size, way = keep_far_taps.shape[0], ("box", 2)
        return [
            summed_halves(keep_near, near, far_first, 0),
            summed_halves(keep_near, near, arrivals[1], half),
            Task(run, (keep_far_taps, arrivals[0]), [((cut, mid), way), (size - cut, mid)]),
        ]

    (away_taps, keep_taps, dhidden), _, (wide_a, wide_b, (taps_first, taps_last)) = on(
        functools.partial(spatial_near, grid_side=grid_side),
        (place, hidden, dflat, dconv, w9),
        [(away_taps, ("box", 1)), (wide_last, ("box", 2))],
        small,
        tasks=tap_parts,
    )
    wide = [BankTotal(*wide_a, FIVE), BankTotal(*wide_b, FIVE)]
    (dreduced, last_away, last_keep), (near_taps, _), (spatial_a,) = on(
        functools.partial(reduce_back, **shape),
        (
            order, dhidden, dconv, x1, roi, w9, inv_mid, mid_vectors, spatial_sums, norm_sums, bias_sums, class_sums,
            sums0, sums1, sums2, sums3,
        ),
        [(away_taps, ("box", 1)), (taps_first, ("box", 2))],
        small + wide,
        tasks=lambda results, arrivals: [summed_halves(keep_taps, *arrivals, 0)],
    )
    spatial = [BankTotal(*spatial_a, FIVE)]
    dprojected = (d0, d1, d2, d3)

    def last_sides(results, arrivals):
        def run(place, keep, away, far, near):
            size = far.shape[0]
            far[...] = keep[:size, :] + away[:size, :]
            near[...] = keep[size:, :] + away[size:, :]

        return [
            summed_halves(keep_taps, near_taps, arrivals[0], cut),
            Task(run, (last_keep, arrivals[1]), [(last_keep.shape[0] // 2, mid)] * 2),
        ]

    roi_gradient, _, (spatial_b, (last_out, last_near)) = on(
        functools.partial(roi_back, half=0),
        (order, dreduced, dprojected, reduce_weight, shortcut_weight),
        [(taps_last, ("box", 2)), (last_away, ("box", 1))],
        small + wide + spatial,
        tasks=last_sides,
    )
    spatial.append(BankTotal(*spatial_b, FOUR))
    roi_gradient, _, ((last_total,),) = on(
        functools.partial(roi_back, half=1),
        (order, dreduced, dprojected, reduce_weight, shortcut_weight, roi_gradient),
        [(last_out, ("box", 2))],
        small + wide + spatial,
        tasks=lambda results, arrivals: [add_task(last_near, arrivals[0], ("bank", 1))],
    )
    last = BankTotal(last_total, last_total, THREE)
    flows = small + wide + spatial + [last]
    emitted = {}
    makers = {
        "small": (small, lambda *arrays: emit_small(place, *arrays, out, att, classes)),
        "wide": (wide, lambda *arrays: emit_wide(place, *arrays, in_width, mid, tile)),
    }
    while any(not flow.done for flow in flows):
        ready = [k for k, (group, _) in makers.items() if k not in emitted and all(flow.done for flow in group)]
        views = [v for k in ready for flow in makers[k][0] for v in (flow.kept, flow.other)]
        arrays, places = distinct(views)

        def outputs(*arrays):
            found = [v.of(arrays[k]) for v, k in zip(views, places)]
            return [makers[k][1](*found[4 * n : 4 * n + 4]) for n, k in enumerate(ready)]

        results, _, _ = on(outputs, tuple(arrays), (), flows)
        emitted.update(zip(ready, results))
    for k, (group, make) in makers.items():
        if k not in emitted:
            emitted[k] = make(*[v for flow in group for v in (flow.kept, flow.other)])
    query_g, key_g, value_g, output_g, class_g = emitted["small"]
    shortcut_g, expand_g = emitted["wide"]
    spatial_g, reduce_g, *sums = emit_last(place, *spatial, last, in_width, mid, tile, classes)
    (
        reduce_gain_g, reduce_shift_g, spatial_gain_g, spatial_shift_g, norm_gain_g, norm_shift_g, class_bias_g,
        expand_gain_g, expand_shift_g, shortcut_gain_g, bias_g, shortcut_shift_g,
    ) = [v.reshape(v.shape[1]) for v in sums]
    return (
        logits,
        roi_gradient.reshape(grid_side, grid_side, boxes, in_width).transpose(2, 0, 1, 3),
        reduce_g,
        reduce_gain_g,
        reduce_shift_g,
        spatial_g.reshape(3, 3, mid, quarter),
        spatial_gain_g,
        spatial_shift_g,
        expand_g,
        expand_gain_g,
        expand_shift_g,
        shortcut_g,
        shortcut_gain_g,
        shortcut_shift_g,
        query_g,
        key_g,
        value_g,
        norm_gain_g,
        norm_shift_g,
        output_g,
        bias_g,
        class_g.T,
        class_bias_g,
    )


def solution(mesh):
    split = ("bank", "box")
    in_specs = (P(split), P(split), P(), P(split)) + (P(),) * 21 + (P(split),)
    column, vector = P(None, "box"), P("box")
    out_specs = (
        P(split),
        P(split),
        column,
        vector,
        vector,
        P(None, None, None, "box"),
        vector,
        vector,
        column,
        vector,
        vector,
        column,
        vector,
        vector,
        column,
        column,
        column,
        vector,
        vector,
        column,
        vector,
        P("box", None),
        P(),
    )
    return jax.shard_map(local, mesh=mesh, in_specs=in_specs, out_specs=out_specs, check_vma=False)
```

```python
import functools
import jax
import jax.numpy as jnp
from jax import lax
from jax.experimental import pallas as pl
from jax.experimental.pallas import tpu as pltpu
from jax.sharding import PartitionSpec as P

HALF = 30
PER_SEC = 8
SEC_DEV = 16
REACH = 2
EPSILON = 1e-05
MIB = 2**20
F32, BF16 = jnp.float32, jnp.bfloat16
BRIEF = pl.CostEstimate(flops=1, bytes_accessed=1, transcendentals=0)
ON_CHIP = pl.BlockSpec(memory_space=pltpu.VMEM)
SCALARS = pl.BlockSpec(memory_space=pltpu.SMEM)
FAR = pl.BlockSpec(memory_space=pl.ANY)
OVER_ROWS = (((0,), (0,)), ((), ()))
OVER_COLUMNS = (((1,), (1,)), ((), ()))


def plain(a, b):
    return jnp.dot(a, b, preferred_element_type=F32)


def over_rows(a, b):
    return lax.dot_general(a, b, OVER_ROWS, preferred_element_type=F32)


def over_columns(a, b):
    return lax.dot_general(a, b, OVER_COLUMNS, preferred_element_type=F32)


def params(mebibytes):
    return pltpu.CompilerParams(vmem_limit_bytes=mebibytes * MIB)


def kept(*arrays):
    return [pltpu.with_memory_space_constraint(v, pltpu.VMEM) for v in arrays]


def outside(*arrays):
    return [pltpu.with_memory_space_constraint(v, pltpu.HBM) for v in arrays]


def start_copies(pairs, sems):
    copies = [pltpu.make_async_copy(source, target, sems.at[k]) for k, (source, target) in enumerate(pairs)]
    for copy in copies:
        copy.start()
    return copies


def fold(values):
    values = values.astype(F32)
    return jnp.sum(values.reshape(values.shape[0] // 8, 8, values.shape[1]), axis=0)


def total_rows(values):
    return jnp.sum(values, axis=0, keepdims=True)


def centre(acc, centred, grid_side, boxes):
    rows, width = acc.shape
    step = grid_side * boxes
    first = acc[0:step, :]
    shift = total_rows(jnp.sum(first.reshape(step // 8, 8, width), axis=0)) / step

    def line(k, carry):
        total, square = carry
        sums = squares = None
        for w in range(grid_side):
            at = pl.ds((k * grid_side + w) * boxes, boxes)
            value = (acc[at, :] - shift).astype(BF16)
            centred[at, :] = value
            sums = value if sums is None else sums + value
            squares = value * value if squares is None else squares + value * value
        return total + fold(sums), square + fold(squares)

    zero = jnp.zeros((8, width), F32)
    total, square = lax.fori_loop(0, grid_side, line, (zero, zero), unroll=True)
    offset = total_rows(total) / rows
    var = total_rows(square) / rows - offset * offset
    return lax.rsqrt(jnp.maximum(var, 0.0) + EPSILON), offset, shift


def scaled(inv, offset, gain, shift):
    factor = 0.5 * gain * inv
    return factor, 0.5 * shift - factor * offset


def input_gradient(inv, offset, gain, total, total_c, rows):
    gain_gradient = inv * (total_c - offset * total)
    of_upstream = inv * gain
    of_centred = -of_upstream * inv * gain_gradient / rows
    term = -of_upstream * total / rows - of_centred * offset
    return of_upstream, of_centred, term, gain_gradient


def clear_border(padded):
    side, _, boxes, width = padded.shape
    zeros = jnp.zeros((boxes, width), BF16)
    for k in range(side):
        padded[0, k] = zeros
        padded[side - 1, k] = zeros
        padded[k, 0] = zeros
        padded[k, side - 1] = zeros


def by_cells(grid_side, boxes, body, carry):
    for k in range(grid_side):
        for w in range(grid_side):
            carry = body(k, w, pl.ds((k * grid_side + w) * boxes, boxes), carry)
    return carry


def trunk_kernel(
    grid_side, boxes, roi_far, wr_far, w9_far, bank_far, kw_far, vw_far, *rest
):
    far_vectors, rest = rest[:12], rest[12:]
    roi, x1, hidden, x2, middle, inv, window, vectors, wide_vectors, class_bias = rest[:10]
    wr, w9, bank, kw, vw, acc, sems = rest[10:17]
    near_vectors = rest[17:]
    copies = start_copies(
        [(roi_far, roi), (wr_far, wr), (w9_far, w9), (bank_far, bank), (kw_far, kw), (vw_far, vw)]
        + list(zip(far_vectors, near_vectors)),
        sems,
    )
    clear_border(hidden)
    for k, copy in enumerate(copies[6:]):
        copy.wait()
        value = near_vectors[k][...].astype(F32)
        value = value.reshape(1, value.shape[0])
        if k < 6:
            vectors[k : k + 1, :] = value
        elif k < 11:
            wide_vectors[k - 6 : k - 5, :] = value
        else:
            class_bias[...] = value
    copies[0].wait()
    copies[1].wait()
    acc[...] = plain(roi[...], wr[...])
    inv1, offset1, base = centre(acc, x1, grid_side, boxes)
    inv[0:1, :], inv[1:2, :] = inv1, offset1
    factor, term = scaled(inv1, base + offset1, vectors[0:1, :], vectors[1:2, :])

    def first(k, w, rows, carry):
        h = acc[rows, :] * factor + term
        hidden[k + 1, w + 1] = (h + h * jnp.tanh(h)).astype(BF16)
        return carry

    by_cells(grid_side, boxes, first, 0)
    copies[2].wait()
    for p in range(3):
        for q in range(3):
            taps = hidden[p : p + grid_side, q : q + grid_side].reshape(acc.shape)
            product = plain(taps, w9[p * 3 + q])
            if p + q == 0:
                acc[...] = product
            else:
                acc[...] += product
    inv2, offset2, base2 = centre(acc, x2, grid_side, boxes)
    inv[2:3, :], inv[3:4, :] = inv2, offset2
    factor2, term2 = scaled(inv2, base2 + offset2, vectors[2:3, :], vectors[3:4, :])

    def second(k, w, rows, carry):
        h = acc[rows, :] * factor2 + term2
        middle[rows, :] = (h + h * jnp.tanh(h)).astype(BF16)
        return carry

    by_cells(grid_side, boxes, second, 0)
    for copy in copies[3:6]:
        copy.wait()
    att = kw.shape[1]
    window[:, :att] = plain(bank[...], kw[...]).astype(BF16)
    window[:, att:] = plain(bank[...], vw[...]).astype(BF16)


def trunk(roi, wr, w9, bank, kw, vw, *vectors, grid_side, boxes):
    rows, mid = roi.shape[0], wr.shape[1]
    side = grid_side + 2
    return pl.pallas_call(
        functools.partial(trunk_kernel, grid_side, boxes),
        in_specs=[FAR] * 18,
        out_specs=[ON_CHIP] * 10,
        out_shape=[
            pltpu.VMEM(roi.shape, BF16),
            pltpu.VMEM((rows, mid), BF16),
            pltpu.VMEM((side, side, boxes, mid), BF16),
            pltpu.VMEM((rows, mid), BF16),
            pltpu.VMEM((rows, mid), BF16),
            jax.ShapeDtypeStruct((4, mid), F32),
            jax.ShapeDtypeStruct((bank.shape[0], 2 * kw.shape[1]), BF16),
            jax.ShapeDtypeStruct((6, mid), F32),
            jax.ShapeDtypeStruct((5, vectors[6].shape[0]), F32),
            jax.ShapeDtypeStruct((1, vectors[11].shape[0]), F32),
        ],
        scratch_shapes=[pltpu.VMEM(v.shape, BF16) for v in (wr, w9, bank, kw, vw)]
        + [pltpu.VMEM((rows, mid), F32), pltpu.SemaphoreType.DMA((18,))]
        + [pltpu.VMEM(v.shape, BF16) for v in vectors],
        compiler_params=params(18),
        cost_estimate=BRIEF,
        name="trunk",
    )(*outside(roi, wr, w9, bank, kw, vw, *vectors))


def widen_kernel(grid_side, boxes, order, roi, middle, ws_far, we_far, vectors, *rest):
    xs, (inv, feature, ws, we, acc_e, acc_p, sems) = rest[:8], rest[8:]
    width = acc_e.shape[1]
    at = [pl.ds(pl.multiple_of(order[k] * width, width), width) for k in range(4)]
    copies = start_copies(
        [pair for k in range(4) for pair in ((ws_far.at[:, at[k]], ws.at[k]), (we_far.at[:, at[k]], we.at[k]))],
        sems,
    )
    for k in range(4):
        xe, xp = xs[2 * k], xs[2 * k + 1]
        copies[2 * k].wait()
        acc_p[...] = plain(roi[...], ws[k])
        copies[2 * k + 1].wait()
        acc_e[...] = plain(middle[...], we[k])
        inv_p, offset_p, base_p = centre(acc_p, xp, grid_side, boxes)
        inv_e, offset_e, base_e = centre(acc_e, xe, grid_side, boxes)
        for row, value in enumerate((inv_e, inv_p, offset_e, offset_p)):
            inv[k, row : row + 1, :] = value
        factor_e, term_e = scaled(inv_e, base_e + offset_e, vectors[0:1, at[k]], vectors[1:2, at[k]])
        factor_p, term_p = scaled(inv_p, base_p + offset_p, vectors[2:3, at[k]], vectors[3:4, at[k]])
        term = term_e + term_p

        def line(row, total):
            for w in range(grid_side):
                rows = pl.ds((row * grid_side + w) * boxes, boxes)
                h = acc_e[rows, :] * factor_e + acc_p[rows, :] * factor_p + term
                total = total + (h + h * jnp.tanh(h))
            return total

        total = lax.fori_loop(0, grid_side, line, jnp.zeros((boxes, width), F32))
        feature[:, at[k]] = total / (grid_side * grid_side)


def widen(order, roi, middle, ws, we, vectors, grid_side, boxes):
    rows, width_in = roi.shape
    mid, out = we.shape
    tile = out // 4
    return pl.pallas_call(
        functools.partial(widen_kernel, grid_side, boxes),
        in_specs=[SCALARS, ON_CHIP, ON_CHIP, FAR, FAR, ON_CHIP],
        out_specs=[ON_CHIP] * 10,
        out_shape=[pltpu.VMEM((rows, tile), BF16)] * 8
        + [jax.ShapeDtypeStruct((4, 4, tile), F32), jax.ShapeDtypeStruct((boxes, out), F32)],
        scratch_shapes=[
            pltpu.VMEM((4, width_in, tile), BF16),
            pltpu.VMEM((4, mid, tile), BF16),
            pltpu.VMEM((rows, tile), F32),
            pltpu.VMEM((rows, tile), F32),
            pltpu.SemaphoreType.DMA((8,)),
        ],
        compiler_params=params(18),
        cost_estimate=BRIEF,
        name="widen",
    )(order, *kept(roi, middle), *outside(ws, we), vectors)


def doubled_slope(h):
    t = jnp.tanh(h)
    return (1.0 + t) * (1.0 + h * (1.0 - t))


def narrow_part(
    grid_side, boxes, k, order, roi, middle, xe, xp, we, inv, vectors, dfeature, part, dprojected, sums,
    upstream, dexpanded,
):
    rows, width = upstream.shape
    columns = pl.ds(pl.multiple_of(order[k] * width, width), width)
    gain_e, gain_p = vectors[0:1, columns], vectors[2:3, columns]
    inv_e, inv_p, offset_e, offset_p = [inv[k, row : row + 1, :] for row in range(4)]
    factor_e, term_e = scaled(inv_e, offset_e, gain_e, vectors[1:2, columns])
    factor_p, term_p = scaled(inv_p, offset_p, gain_p, vectors[3:4, columns])
    term = term_e + term_p
    slope_scale = dfeature[:, columns] * (0.5 / (grid_side * grid_side))

    def line(row, carry):
        sums = None
        for w in range(grid_side):
            at = pl.ds((row * grid_side + w) * boxes, boxes)
            e, p = xe[at, :].astype(F32), xp[at, :].astype(F32)
            u = doubled_slope(e * factor_e + p * factor_p + term) * slope_scale
            upstream[at, :] = u
            new = (u, u * e, u * p)
            sums = new if sums is None else [a + b for a, b in zip(sums, new)]
        return [a + fold(b) for a, b in zip(carry, sums)]

    zero = jnp.zeros((8, width), F32)
    total, total_e, total_p = [total_rows(v) for v in lax.fori_loop(0, grid_side, line, [zero] * 3)]
    ue, ce, te, gain_gradient_e = input_gradient(inv_e, offset_e, gain_e, total, total_e, rows)
    up, cp, tp, gain_gradient_p = input_gradient(inv_p, offset_p, gain_p, total, total_p, rows)
    sums[0:1, :] = gain_gradient_e
    sums[1:2, :] = total
    sums[2:3, :] = gain_gradient_p

    def second(row, w, at, carry):
        u = upstream[at, :]
        dexpanded[at, :] = (u * ue + xe[at, :].astype(F32) * ce + te).astype(BF16)
        dprojected[at, :] = (u * up + xp[at, :].astype(F32) * cp + tp).astype(BF16)
        return carry

    for row in range(grid_side):
        for w in range(grid_side):
            second(row, w, pl.ds((row * grid_side + w) * boxes, boxes), 0)
    split = roi.shape[1]
    part[0:split, :] = over_rows(roi[...], dprojected[...]).astype(BF16)
    part[split:, :] = over_rows(middle[...], dexpanded[...]).astype(BF16)
    return over_columns(dexpanded[...], we[...])


def expand_columns(order, ks, we_far, we, sems):
    width = we.shape[2]
    columns = [pl.ds(pl.multiple_of(order[k] * width, width), width) for k in ks]
    return start_copies([(we_far.at[:, at], we.at[n]) for n, at in enumerate(columns)], sems)


def narrow_kernel(grid_side, boxes, ks, order, roi, middle, inv, vectors, dfeature, we_far, *rest):
    count = len(ks)
    xs, rest = rest[: 2 * count], rest[2 * count :]
    *before, dmiddle = rest[: -4 - 3 * count]
    outs, (we, upstream, dexpanded, sems) = rest[-4 - 3 * count : -4], rest[-4:]
    copies = expand_columns(order, ks, we_far, we, sems)
    for n, k in enumerate(ks):
        copies[n].wait()
        back = narrow_part(
            grid_side, boxes, k, order, roi, middle, xs[2 * n], xs[2 * n + 1], we.at[n], inv, vectors, dfeature,
            *outs[3 * n : 3 * n + 3], upstream, dexpanded,
        )
        if n == 0:
            dmiddle[...] = before[0][...] + back if before else back
        else:
            dmiddle[...] += back


def narrow(order, roi, middle, inv, vectors, dfeature, we, *rest, ks, grid_side, boxes):
    rows, width_in = roi.shape
    mid, out = we.shape
    tile = out // 4
    xs, before = rest[: 2 * len(ks)], rest[2 * len(ks) :]
    return pl.pallas_call(
        functools.partial(narrow_kernel, grid_side, boxes, ks),
        in_specs=[SCALARS] + [ON_CHIP] * 5 + [FAR] + [ON_CHIP] * len(rest),
        out_specs=[ON_CHIP] * (1 + 3 * len(ks)),
        out_shape=[pltpu.VMEM((rows, mid), F32)]
        + [
            jax.ShapeDtypeStruct((width_in + mid, tile), BF16),
            pltpu.VMEM((rows, tile), BF16),
            jax.ShapeDtypeStruct((3, tile), F32),
        ]
        * len(ks),
        input_output_aliases={7 + 2 * len(ks): 0} if before else {},
        scratch_shapes=[
            pltpu.VMEM((len(ks), mid, tile), BF16),
            pltpu.VMEM((rows, tile), F32),
            pltpu.VMEM((rows, tile), BF16),
            pltpu.SemaphoreType.DMA((len(ks),)),
        ],
        compiler_params=params(16),
        cost_estimate=BRIEF,
        name="narrow",
    )(order, *kept(roi, middle), inv, vectors, dfeature, *outside(we), *kept(*xs, *before))


def norm_back(grid_side, boxes, upstream, centred, inv, offset, gain, shift, low, sums, store):
    rows, width = upstream.shape
    factor, term = scaled(inv, offset, gain, shift)

    def line(row, carry):
        sums = None
        for w in range(grid_side):
            at = pl.ds((row * grid_side + w) * boxes, boxes)
            c = centred[at, :].astype(F32)
            u = doubled_slope(c * factor + term) * (0.5 * upstream[at, :])
            low[at, :] = u
            new = (u, u * c)
            sums = new if sums is None else [a + b for a, b in zip(sums, new)]
        return [a + fold(b) for a, b in zip(carry, sums)]

    zero = jnp.zeros((8, width), F32)
    total, total_c = [total_rows(v) for v in lax.fori_loop(0, grid_side, line, [zero] * 2)]
    of_upstream, of_centred, term, gain_gradient = input_gradient(inv, offset, gain, total, total_c, rows)
    sums[0:1, :] = gain_gradient
    sums[1:2, :] = total

    def second(row, w, at, carry):
        value = low[at, :] * of_upstream + centred[at, :].astype(F32) * of_centred + term
        store(row, w, at, value.astype(BF16))
        return carry

    by_cells(grid_side, boxes, second, 0)


def spatial_taps(grid_side, side, core, hidden, dflat, part, away, keep):
    rows, width = dflat.shape
    half, quarter = width // 2, width // 4
    mine = pl.ds(pl.multiple_of(core * quarter, quarter), quarter)
    other = pl.ds(pl.multiple_of((1 - core) * quarter, quarter), quarter)
    columns = dflat[:, pl.ds(pl.multiple_of(side * half, half), half)]
    for p in range(3):
        for q in range(3):
            taps = hidden[p : p + grid_side, q : q + grid_side].reshape(rows, width)
            part[...] = over_rows(taps, columns).astype(BF16)
            lines = slice((p * 3 + q) * quarter, (p * 3 + q + 1) * quarter)
            for k in range(4):
                lanes = slice(k * quarter, (k + 1) * quarter)
                keep[lines, lanes] = part[lanes, mine]
                away[lines, lanes] = part[lanes, other]


def spatial_far_kernel(
    grid_side, boxes, order, place, roi, middle, inv_out, wide_vectors, dfeature, we_far, xe, xp, before,
    x2, hidden, inv, vectors, part, dprojected, wide_sums, away, keep, dconv, dflat, sums,
    we, upstream, dexpanded, taps, sems,
):
    copies = expand_columns(order, (3,), we_far, we, sems)
    clear_border(dconv)
    copies[0].wait()
    back = narrow_part(
        grid_side, boxes, 3, order, roi, middle, xe, xp, we.at[0], inv_out, wide_vectors, dfeature,
        part, dprojected, wide_sums, upstream, dexpanded,
    )
    upstream[...] = before[...] + back

    def store(row, w, at, value):
        dconv[row + 1, w + 1] = value
        dflat[at, :] = value

    norm_back(
        grid_side, boxes, upstream, x2, inv[2:3, :], inv[3:4, :], vectors[2:3, :], vectors[3:4, :], upstream, sums, store
    )
    spatial_taps(grid_side, 1 - place[2], place[3], hidden, dflat, taps, away, keep)


def spatial_far(
    order, place, roi, middle, inv_out, wide_vectors, dfeature, we, xe, xp, before, x2, hidden, inv, vectors,
    grid_side, boxes,
):
    rows, width_in = roi.shape
    mid, out = we.shape
    tile, side = out // 4, grid_side + 2
    taps = jax.ShapeDtypeStruct((9 * (mid // 4), mid), BF16)
    return pl.pallas_call(
        functools.partial(spatial_far_kernel, grid_side, boxes),
        in_specs=[SCALARS] * 2 + [ON_CHIP] * 5 + [FAR] + [ON_CHIP] * 7,
        out_specs=[ON_CHIP] * 8,
        out_shape=[
            jax.ShapeDtypeStruct((width_in + mid, tile), BF16),
            pltpu.VMEM((rows, tile), BF16),
            jax.ShapeDtypeStruct((3, tile), F32),
            taps,
            taps,
            pltpu.VMEM((side, side, boxes, mid), BF16),
            pltpu.VMEM((rows, mid), BF16),
            jax.ShapeDtypeStruct((2, mid), F32),
        ],
        scratch_shapes=[
            pltpu.VMEM((1, mid, tile), BF16),
            pltpu.VMEM((rows, tile), F32),
            pltpu.VMEM((rows, tile), BF16),
            pltpu.VMEM((mid, mid // 2), BF16),
            pltpu.SemaphoreType.DMA((1,)),
        ],
        compiler_params=params(18),
        cost_estimate=BRIEF,
        name="spatial_far",
    )(
        order, place, *kept(roi, middle), inv_out, wide_vectors, dfeature, *outside(we), *kept(xe, xp, before, x2, hidden),
        inv, vectors,
    )


def spatial_near_kernel(grid_side, place, hidden, dflat, dconv, w9_far, away, keep, dhidden, part, w9, sems):
    copies = start_copies([(w9_far.at[k], w9.at[k]) for k in range(6)], sems)
    rows, width = dflat.shape
    for p in range(2):
        for q in range(3):
            copies[p * 3 + q].wait()
            taps = dconv[2 - p : 2 - p + grid_side, 2 - q : 2 - q + grid_side].reshape(rows, width)
            product = over_columns(taps, w9[p * 3 + q])
            if p + q == 0:
                dhidden[...] = product
            else:
                dhidden[...] += product
    spatial_taps(grid_side, place[2], place[3], hidden, dflat, part, away, keep)


def spatial_near(place, hidden, dflat, dconv, w9, grid_side):
    rows, mid = dflat.shape
    taps = jax.ShapeDtypeStruct((9 * (mid // 4), mid), BF16)
    return pl.pallas_call(
        functools.partial(spatial_near_kernel, grid_side),
        in_specs=[SCALARS] + [ON_CHIP] * 3 + [FAR],
        out_specs=[ON_CHIP] * 3,
        out_shape=[taps, taps, pltpu.VMEM((rows, mid), F32)],
        scratch_shapes=[
            pltpu.VMEM((mid, mid // 2), BF16),
            pltpu.VMEM((6, mid, mid), BF16),
            pltpu.SemaphoreType.DMA((6,)),
        ],
        compiler_params=params(16),
        cost_estimate=BRIEF,
        name="spatial_near",
    )(place, *kept(hidden, dflat, dconv), *outside(w9))


def reduce_back_kernel(
    grid_side, boxes, order, dhidden, dconv, x1, roi, w9_far, inv, vectors, spatial_sums, norm_sums, bias_sums, class_sums,
    s0, s1, s2, s3, dreduced, away, keep, upstream, w9, weight, sums, sems,
):
    rows, width = upstream.shape
    copies = start_copies([(w9_far.at[6 + q], w9.at[q]) for q in range(3)], sems)
    for q in range(3):
        copies[q].wait()
        taps = dconv[0:grid_side, 2 - q : 2 - q + grid_side].reshape(rows, width)
        product = over_columns(taps, w9[q])
        if q == 0:
            upstream[...] = dhidden[...] + product
        else:
            upstream[...] += product

    def store(row, w, at, value):
        dreduced[at, :] = value

    norm_back(
        grid_side, boxes, upstream, x1, inv[0:1, :], inv[1:2, :], vectors[0:1, :], vectors[1:2, :], upstream, sums, store
    )
    weight[...] = over_rows(dreduced[...], roi[...]).astype(BF16)
    quarter, classes = width // 4, class_sums.shape[1]
    size = away.shape[0] // 2
    for k, (target, wide_sums) in enumerate(((away, s0), (keep, s1), (away, s2), (keep, s3))):
        base = (k // 2) * size
        lines = pl.ds(pl.multiple_of(order[k] * quarter, quarter), quarter)
        wide = pl.ds(pl.multiple_of(order[k] * width, width), width)
        target[base : base + quarter, :] = weight[lines, :width]
        target[base + quarter : base + 2 * quarter, :] = weight[lines, width:]
        line0 = [v[r : r + 1, lines] for v in (sums, spatial_sums) for r in range(2)]
        line1 = [norm_sums[r : r + 1, lines] for r in range(2)]
        line1 += [class_sums[...], jnp.zeros((1, width - 2 * quarter - classes), F32)]
        tail = jnp.concatenate(
            [
                jnp.concatenate(line0, axis=1),
                jnp.concatenate(line1, axis=1),
                wide_sums[...],
                bias_sums[:, wide],
                jnp.zeros((10, width), F32),
            ]
        )
        target[base + 2 * quarter : base + size, :] = tail.astype(BF16)


def reduce_back(order, dhidden, dconv, x1, roi, w9, inv, vectors, *sums, grid_side, boxes):
    rows, width_in = roi.shape
    mid = dhidden.shape[1]
    part = jax.ShapeDtypeStruct((2 * (mid // 2 + 16), mid), BF16)
    return pl.pallas_call(
        functools.partial(reduce_back_kernel, grid_side, boxes),
        in_specs=[SCALARS] + [ON_CHIP] * 4 + [FAR] + [ON_CHIP] * 10,
        out_specs=[ON_CHIP] * 3,
        out_shape=[pltpu.VMEM((rows, mid), BF16), part, part],
        scratch_shapes=[
            pltpu.VMEM((rows, mid), F32),
            pltpu.VMEM((3, mid, mid), BF16),
            pltpu.VMEM((mid, width_in), BF16),
            pltpu.VMEM((2, mid), F32),
            pltpu.SemaphoreType.DMA((3,)),
        ],
        compiler_params=params(20),
        cost_estimate=BRIEF,
        name="reduce_back",
    )(order, *kept(dhidden, dconv, x1, roi), *outside(w9), inv, vectors, *sums)


def roi_back_kernel(half, order, dreduced, d0, d1, d2, d3, wr_far, ws_far, *rest):
    out, wr, ws, acc, low, sems = rest[-6:]
    tile = d0.shape[1]
    size = acc.shape[1]
    lines = pl.ds(half * size, size)
    columns = [pl.ds(pl.multiple_of(order[k] * tile, tile), tile) for k in range(4)]
    copies = start_copies(
        [(wr_far.at[lines, :], wr)] + [(ws_far.at[lines, columns[k]], ws.at[k]) for k in range(4)], sems
    )
    copies[0].wait()
    acc[...] = over_columns(dreduced[...], wr[...])
    for k, d in enumerate((d0, d1, d2, d3)):
        copies[k + 1].wait()
        acc[...] += over_columns(d[...], ws[k])
    low[...] = acc[...].astype(BF16)
    pltpu.sync_copy(low, out.at[:, lines])


def roi_back(order, dreduced, dprojected, wr, ws, *done, half):
    rows, mid = dreduced.shape
    width_in, out = ws.shape
    size = width_in // 2
    return pl.pallas_call(
        functools.partial(roi_back_kernel, half),
        in_specs=[SCALARS] + [ON_CHIP] * 5 + [FAR] * (2 + len(done)),
        out_specs=FAR,
        out_shape=pltpu.HBM((rows, width_in), BF16),
        input_output_aliases={8: 0} if done else {},
        scratch_shapes=[
            pltpu.VMEM((size, mid), BF16),
            pltpu.VMEM((4, size, out // 4), BF16),
            pltpu.VMEM((rows, size), F32),
            pltpu.VMEM((rows, size), BF16),
            pltpu.SemaphoreType.DMA((5,)),
        ],
        compiler_params=params(18),
        cost_estimate=BRIEF,
        name="roi_back",
    )(order, *kept(dreduced, *dprojected), *outside(wr, ws, *done))


def head_kernel(
    all_seconds, place, seconds, lengths, feature, w0, w1, w2, w3, w4, wq_far, wo_far, wc_far,
    mid_vectors, vectors, class_bias, cotangent,
    logits, dfeature, pack, norm_sums, bias_sums, class_sums, window, wq, wo, wc, sems,
):
    copies = start_copies([(wq_far, wq), (wo_far, wo), (wc_far, wc)], sems)
    att = wq.shape[1]
    boxes, out = feature.shape
    classes = cotangent.shape[1]
    span = window.shape[0]
    rows = w0.shape[0]
    for k, w in enumerate((w0, w1, w2, w3, w4)):
        window[k * rows : (k + 1) * rows, :] = w[...]
    scale = att ** (-0.5)
    norm_gain, norm_shift = mid_vectors[4:5, :], mid_vectors[5:6, :]

    row_seconds = lax.broadcasted_iota(jnp.int32, (boxes, span), 1) // PER_SEC + (place[0] - REACH) * SEC_DEV
    line = lax.broadcasted_iota(jnp.int32, (boxes, 128), 0)
    box_seconds = jnp.zeros((boxes, 128), jnp.int32)
    for k in range(boxes):
        box_seconds = jnp.where(line == k, seconds[k], box_seconds)
    box_seconds = box_seconds[:, 0:1]
    live = (row_seconds >= 0) & (row_seconds < all_seconds) & (jnp.abs(box_seconds - row_seconds) <= HALF)
    end = 0
    for k in range(lengths.shape[0]):
        end = end + lengths[k]
        live = live & ((end <= row_seconds) == (end <= box_seconds))

    copies[0].wait()
    feature_low = feature[...].astype(BF16)
    pack[:, :out] = feature_low
    queries = plain(feature_low, wq[...]).astype(BF16)
    keys, values = window[:, :att], window[:, att:]
    scores = over_columns(queries, keys) * scale
    top = jnp.max(jnp.where(live, scores, -1e30), axis=1, keepdims=True)
    exps = jnp.where(live, jnp.exp(jnp.where(live, scores - top, 0.0)), 0.0)
    probs = exps / jnp.sum(exps, axis=1, keepdims=True)
    probs_low = probs.astype(BF16)
    pre = plain(probs_low, values) + queries.astype(F32)
    centred = pre - jnp.mean(pre, axis=1, keepdims=True)
    inv = lax.rsqrt(jnp.mean(centred * centred, axis=1, keepdims=True) + EPSILON)
    x = centred * inv
    h = 0.5 * (x * norm_gain + norm_shift)
    activated = (h + h * jnp.tanh(h)).astype(BF16)
    copies[1].wait()
    combined_low = (feature[...] + plain(activated, wo[...]) + vectors[4:5, :]).astype(BF16)
    pack[:, out : 2 * out] = combined_low
    copies[2].wait()
    logits[...] = over_columns(feature_low, wc[:, :out]) + over_columns(combined_low, wc[:, out:]) + class_bias[...]
    g = cotangent[...].astype(BF16)
    class_sums[...] = jnp.sum(g.astype(F32), axis=0, keepdims=True)
    first = plain(g, wc[:, :out])
    second = plain(g, wc[:, out:])
    gb = second.astype(BF16)
    pack[:, 2 * out : 3 * out] = gb
    bias_sums[...] = jnp.sum(gb.astype(F32), axis=0, keepdims=True)
    u = over_columns(gb, wo[...]) * (0.5 * doubled_slope(h))
    norm_sums[0:1, :] = jnp.sum(u * x, axis=0, keepdims=True)
    norm_sums[1:2, :] = jnp.sum(u, axis=0, keepdims=True)
    e = u * norm_gain
    dpre = inv * (e - jnp.mean(e, axis=1, keepdims=True) - x * jnp.mean(e * x, axis=1, keepdims=True))
    da = dpre.astype(BF16)
    dprobs = over_columns(da, values)
    delta = jnp.sum(probs * dprobs, axis=1, keepdims=True)
    ds = (probs * (dprobs - delta)).astype(BF16)
    dq = (plain(ds, keys) * scale + dpre).astype(BF16)
    at = 3 * out
    for value in (dq, activated, queries, da):
        pack[:, at : at + att] = value
        at += att
    pack[:, at : at + 128] = jnp.zeros((boxes, 128), BF16)
    pack[:, at : at + classes] = g
    at += 128
    pack[:, at : at + span] = ds
    pack[:, at + span :] = probs_low
    dfeature[...] = first + second + over_columns(dq, wq[...])


def head(place, seconds, lengths, feature, windows, wq, wo, wc, mid_vectors, vectors, class_bias, cotangent, all_seconds):
    boxes, out = feature.shape
    att = wq.shape[1]
    classes = wc.shape[0]
    span = sum(w.shape[0] for w in windows)
    shapes = [
        ((boxes, classes), F32),
        ((boxes, out), F32),
        ((boxes, 3 * out + 4 * att + 128 + 2 * span), BF16),
        ((2, att), F32),
        ((1, out), F32),
        ((1, classes), F32),
    ]
    return pl.pallas_call(
        functools.partial(head_kernel, all_seconds),
        in_specs=[SCALARS] * 3 + [ON_CHIP] * 6 + [FAR] * 3 + [ON_CHIP] * 4,
        out_specs=[ON_CHIP] * len(shapes),
        out_shape=[jax.ShapeDtypeStruct(s, d) for s, d in shapes],
        scratch_shapes=[
            pltpu.VMEM((span, 2 * att), BF16),
            pltpu.VMEM(wq.shape, BF16),
            pltpu.VMEM(wo.shape, BF16),
            pltpu.VMEM(wc.shape, BF16),
            pltpu.SemaphoreType.DMA((3,)),
        ],
        compiler_params=params(16),
        cost_estimate=BRIEF,
        name="head",
    )(place, seconds, lengths, feature, *windows, *outside(wq, wo, wc), mid_vectors, vectors, class_bias, cotangent)


def halves(place, bit, value, sent, kept):
    size = sent.shape[0]
    mine = place[4 + bit]
    sent[...] = value[pl.ds(pl.multiple_of((1 - mine) * size, 16), size), :]
    kept[...] = value[pl.ds(pl.multiple_of(mine * size, 16), size), :]


def small_weights_kernel(
    grouped, place, pair, far_pair, pair_bank, far_bank, sent_a, kept_a, sent_b, kept_b,
    pack, banks, dbank, first, second,
):
    boxes = pair.shape[0] // 2
    for k, source in ((place[3], pair), (1 - place[3], far_pair)):
        for half in range(2):
            lines = pl.ds(pl.multiple_of((2 * half + k) * boxes, 16), boxes)
            pack[lines, :] = source[half * boxes : (half + 1) * boxes, :]
    rows = pair_bank.shape[0] // 4
    for k, source in ((place[3], pair_bank), (1 - place[3], far_bank)):
        for block in range(4):
            lines = pl.ds(pl.multiple_of((2 * block + k) * rows, 16), rows)
            banks[lines, :] = source[block * rows : (block + 1) * rows, :]
    width = first.shape[1]
    att, out, piece = width, banks.shape[1], width // 4
    span = (2 * REACH + 1) * rows
    q = place[1]
    columns = lambda base, size: pl.ds(pl.multiple_of(base + q * size, size), size)
    base = 3 * out
    at = base + 4 * att + 128
    dbank[...] = jnp.zeros(dbank.shape, F32)
    for k in range(grouped):
        lines, window = slice(k * boxes, (k + 1) * boxes), slice(k * rows, k * rows + span)
        ds, probs = pack[lines, at : at + span], pack[lines, at + span : at + 2 * span]
        dbank[window, :piece] += over_rows(ds, pack[lines, columns(base + 2 * att, piece)]) * att ** (-0.5)
        dbank[window, piece:] += over_rows(probs, pack[lines, columns(base + 3 * att, piece)])
    for left, right, target, row in (
        (pack[:, columns(base, piece)], pack[:, :out], first, 0),
        (dbank[:, :piece].astype(BF16), banks[...], first, att),
        (dbank[:, piece:].astype(BF16), banks[...], second, 0),
    ):
        product = over_rows(left, right).astype(BF16)
        for k in range(out // width):
            target[row + k * piece : row + (k + 1) * piece, :] = product[:, k * width : (k + 1) * width]
    second[att : 2 * att, :] = over_rows(
        pack[:, base + att : base + 2 * att], pack[:, columns(2 * out, out // 4)]
    ).astype(BF16)
    at = base + 4 * att
    product = over_rows(pack[:, at : at + 128], pack[:, columns(0, out // 2)]).astype(BF16)
    first[2 * att :, :] = product[:, :width]
    second[2 * att :, :] = product[:, width:]
    halves(place, 0, first, sent_a, kept_a)
    halves(place, 0, second, sent_b, kept_b)


def small_weights(place, pair, far_pair, pair_bank, far_bank, att, grouped):
    rows, out = 2 * att + 128, pair_bank.shape[1]
    reach = 2 * pair_bank.shape[0]
    return pl.pallas_call(
        functools.partial(small_weights_kernel, grouped),
        in_specs=[SCALARS] + [ON_CHIP] * 4,
        out_specs=[ON_CHIP] * 4,
        out_shape=[jax.ShapeDtypeStruct((rows // 2, att), BF16)] * 4,
        scratch_shapes=[
            pltpu.VMEM((2 * pair.shape[0], pair.shape[1]), BF16),
            pltpu.VMEM((reach, out), BF16),
            pltpu.VMEM((reach, att // 2), F32),
            pltpu.VMEM((rows, att), BF16),
            pltpu.VMEM((rows, att), BF16),
        ],
        compiler_params=params(20),
        cost_estimate=BRIEF,
        name="small_weights",
    )(place, pair, far_pair, pair_bank, far_bank)


class View:
    def __init__(self, array, at=0, rows=None):
        self.array, self.at = array, at
        self.rows = array.shape[0] if rows is None else rows

    @property
    def shape(self):
        return (self.rows, *self.array.shape[1:])

    def of(self, array):
        return View(array, self.at, self.rows)


def view(value):
    return value if isinstance(value, View) else View(value)


class Task:
    def __init__(self, run, inputs, outputs, scratch=()):
        self.run, self.scratch = run, list(scratch)
        self.inputs = [view(v) for v in inputs]
        self.outputs = [out if isinstance(out[0], tuple) else (out, None) for out in outputs]


def distinct(views):
    arrays, places = [], []
    for v in views:
        found = [k for k, array in enumerate(arrays) if array is v.array]
        places.append(found[0] if found else len(arrays))
        if not found:
            arrays.append(v.array)
    return arrays, places


def rows_of(ref, v):
    return ref if v.rows == v.array.shape[0] else ref.at[v.at : v.at + v.rows]


def step(place, tasks):
    arrays, places = distinct([v for t in tasks for v in t.inputs])
    shapes, boxes, outputs = [], {}, []
    for task in tasks:
        for shape, way in task.outputs:
            if way is None:
                shapes.append(list(shape))
                outputs.append((len(shapes) - 1, 0, shape[0]))
            else:
                if way not in boxes:
                    boxes[way] = len(shapes)
                    shapes.append([0, shape[1]])
                box = shapes[boxes[way]]
                outputs.append((boxes[way], box[0], shape[0]))
                box[0] += shape[0]

    def kernel(place_ref, *refs):
        ins, outs, scratch = refs[: len(arrays)], refs[len(arrays) : len(arrays) + len(shapes)], refs[len(arrays) + len(shapes) :]
        where, made = list(places), list(outputs)
        for task in tasks:
            sources = [rows_of(ins[where.pop(0)], v) for v in task.inputs]
            targets = []
            for _ in task.outputs:
                k, at, rows = made.pop(0)
                targets.append(outs[k] if rows == shapes[k][0] else outs[k].at[at : at + rows])
            task.run(place_ref, *sources, *targets, *scratch[: len(task.scratch)])
            scratch = scratch[len(task.scratch) :]

    results = pl.pallas_call(
        kernel,
        in_specs=[SCALARS] + [ON_CHIP] * len(arrays),
        out_specs=[ON_CHIP] * len(shapes),
        out_shape=[jax.ShapeDtypeStruct(tuple(shape), BF16) for shape in shapes],
        scratch_shapes=[pltpu.VMEM(shape, BF16) for t in tasks for shape in t.scratch],
        compiler_params=params(16),
        cost_estimate=BRIEF,
        name="step",
    )(place, *arrays)
    made = [View(results[k], at, rows) for k, at, rows in outputs]
    grouped = []
    for task in tasks:
        grouped.append(made[: len(task.outputs)])
        made = made[len(task.outputs) :]
    return grouped


def add_task(a, b, way=None):
    def run(place, x, y, total):
        total[...] = x[...] + y[...]

    return Task(run, (a, b), [(view(a).shape, way)])


HALVES, WHOLE, GATHER = range(3)
FIVE = [(0, HALVES), (1, HALVES), (2, WHOLE), (1, GATHER), (0, GATHER)]
FOUR = [(0, HALVES), (1, WHOLE), (2, WHOLE), (0, GATHER)]
THREE = [(0, WHOLE), (1, WHOLE), (2, WHOLE)]


class BankTotal:
    def __init__(self, sent, kept, plan):
        self.sent, self.kept, self.plan, self.stage = view(sent), view(kept), plan, 0

    @property
    def done(self):
        return self.stage == len(self.plan)

    def way(self, stage):
        return ("bank", 1 << self.plan[stage][0])

    def arrival(self, other):
        (bit, kind), (size, width) = self.plan[self.stage], self.kept.shape
        last = self.stage + 1 == len(self.plan)
        if last and kind == GATHER:
            return None
        way = None if last else self.way(self.stage + 1)
        if kind == GATHER:

            def gather(place, mine, other, joined):
                join(place, bit, mine, other, joined)

            return Task(gather, (self.kept, other), [((2 * size, width), way)])
        if last or self.plan[self.stage + 1][1] != HALVES:
            return add_task(self.kept, other, way)
        next_bit = self.plan[self.stage + 1][0]

        def add(place, kept, other, sent, left, total):
            total[...] = kept[...] + other[...]
            halves(place, next_bit, total, sent, left)

        half = (size // 2, width)
        return Task(add, (self.kept, other), [(half, way), half], [(size, width)])

    def land(self, other, results):
        if results is None:
            self.other = other
        else:
            self.sent, self.kept = results[0], results[-1]
            if self.plan[self.stage] == (2, WHOLE):
                self.sent = self.kept = beyond(self.kept)
        self.stage += 1


def beyond(value):
    size = lax.axis_size("bank")
    if size == 8:
        return value
    own = lax.slice_in_dim(value.array, value.at, value.at + value.rows)
    return View(lax.psum(own, "bank", axis_index_groups=[list(range(k, size, 8)) for k in range(8)]))


def join(place, bit, mine, other, joined):
    size = mine.shape[0]
    at = place[4 + bit]
    joined[pl.ds(pl.multiple_of(at * size, 16), size), :] = mine[...]
    joined[pl.ds(pl.multiple_of((1 - at) * size, 16), size), :] = other[...]


def emit(place, run, inputs, outputs, scratch, name):
    arrays, places = distinct(inputs)

    def kernel(place_ref, *refs):
        sources = [rows_of(refs[k], v) for k, v in zip(places, inputs)]
        run(place_ref, *sources, *refs[len(arrays) :])

    return pl.pallas_call(
        kernel,
        in_specs=[SCALARS] + [ON_CHIP] * len(arrays),
        out_specs=[ON_CHIP] * len(outputs),
        out_shape=[jax.ShapeDtypeStruct(shape, F32) for shape in outputs],
        scratch_shapes=[pltpu.VMEM(shape, BF16) for shape in scratch],
        compiler_params=params(20),
        cost_estimate=BRIEF,
        name=name,
    )(place, *arrays)


def emit_small(place, a, other_a, b, other_b, out, att, classes):
    piece = att // 4
    rows = 2 * att + 128

    def run(place, a, other_a, b, other_b, dquery, dkey, dvalue, doutput, dclass, first, second):
        join(place, 0, a, other_a, first)
        join(place, 0, b, other_b, second)
        for source, row, target in ((first, 0, dquery), (first, att, dkey), (second, 0, dvalue)):
            for k in range(out // att):
                block = source[row + k * piece : row + (k + 1) * piece, :].astype(F32)
                target[k * att : (k + 1) * att, :] = block.T
        doutput[...] = second[att : 2 * att, :].astype(F32)
        dclass[:, :att] = first[2 * att :, :].astype(F32)[:classes]
        dclass[:, att:] = second[2 * att :, :].astype(F32)[:classes]

    return emit(
        place,
        run,
        (a, other_a, b, other_b),
        [(out, piece)] * 3 + [(att, att), (classes, 2 * att)],
        [(rows, att)] * 2,
        "emit_small",
    )


def emit_wide(place, a, other_a, b, other_b, width_in, mid, tile):
    half = 2 * a.rows

    def run(place, a, other_a, b, other_b, shortcut, expand, joined):
        join(place, 0, a, other_a, joined.at[:half])
        join(place, 0, b, other_b, joined.at[half:])
        shortcut[...] = joined[:width_in, :].astype(F32)
        expand[...] = joined[width_in:, :].astype(F32)

    inputs = (a, other_a, b, other_b)
    shapes = [(width_in, tile), (mid, tile)]
    return emit(place, run, inputs, shapes, [(width_in + mid, tile)], "emit_wide")


def emit_last(place, flow_a, flow_b, last, width_in, mid, tile, classes):
    quarter = mid // 4
    rows_a, rows_b = 2 * flow_a.kept.rows, 2 * flow_b.kept.rows

    def run(place, a, other_a, b, other_b, rest, spatial, reduce, *targets):
        targets, taps = targets[:-1], targets[-1]
        join(place, 0, a, other_a, taps.at[:rows_a])
        join(place, 0, b, other_b, taps.at[rows_a:])
        for tap in range(9):
            for k in range(4):
                spatial[tap, k * quarter : (k + 1) * quarter, :] = taps[
                    tap * quarter : (tap + 1) * quarter, k * quarter : (k + 1) * quarter
                ].astype(F32)
        for k in range(2):
            reduce[k * mid : (k + 1) * mid, :] = rest[k * quarter : (k + 1) * quarter, :].astype(F32).T
        tail = rest[2 * quarter : 2 * quarter + 16, :].astype(F32)
        for k in range(4):
            targets[k][...] = tail[0:1, k * quarter : (k + 1) * quarter]
        for k in range(2):
            targets[4 + k][...] = tail[1:2, k * quarter : (k + 1) * quarter]
        targets[6][...] = tail[1:2, 2 * quarter : 2 * quarter + classes]
        for k in range(4):
            targets[7 + k][...] = tail[2 + k : 3 + k, :]
        targets[11][...] = tail[3:4, :]

    inputs = (flow_a.kept, flow_a.other, flow_b.kept, flow_b.other, last.kept)
    shapes = [(9, mid, quarter), (width_in, quarter)] + [(1, quarter)] * 6 + [(1, classes)] + [(1, tile)] * 5
    return emit(place, run, inputs, shapes, [(rows_a + rows_b, mid)], "emit_last")


def move(value, how):
    kind, by = how
    if kind == "edge":
        axis = ("bank", "box")
        size = lax.axis_size(axis)
        targets = [(i, i + by if i % by >= by // 2 else i - by) for i in range(size)]
        return lax.ppermute(value, axis, [(i, j) for i, j in targets if 0 <= j < size])
    if kind == "along":
        axis = ("bank", "box")
        size = lax.axis_size(axis)
        return lax.ppermute(value, axis, [(i, i + by) for i in range(size) if 0 <= i + by < size])
    return lax.ppermute(value, kind, [(i, i ^ by) for i in range(lax.axis_size(kind))])


def launch(moves):
    found, received = [], []
    for value, how in moves:
        same = [r for v, h, r in found if v is value.array and h == how]
        if not same:
            same = [move(value.array, how)]
            found.append((value.array, how, same[0]))
        received.append(value.of(same[0]))
    return received


def slot(place, kernel, inputs, moves=(), flows=(), tasks=None, late=()):
    flows = [flow for flow in flows if not flow.done]
    waits = [len(m) == 2 for m in moves] + [True] * len(flows)
    moves = [(view(m[0]), m[1]) for m in moves] + [(flow.sent, flow.way(flow.stage)) for flow in flows]
    arrays, places = distinct([value for value, _ in moves])
    inputs, arrays = lax.optimization_barrier((inputs, arrays))
    received = launch([(value.of(arrays[k]), how) for k, (value, how) in zip(places, moves)])
    results = kernel(*inputs) if kernel else ()
    waited = [v for v, wait in zip(received, waits) if wait] + list(late)
    arrays, places = distinct(waited)
    results, arrays = lax.optimization_barrier((results, arrays))
    waited = [v.of(arrays[k]) for v, k in zip(waited, places)]
    late = waited[len(waited) - len(late) :]
    received = [waited.pop(0) if wait else v for v, wait in zip(received, waits)]
    count = len(moves) - len(flows)
    arrivals, landed = received[:count] + late, received[count:]
    own = tasks(results, arrivals) if tasks else []
    pending = [flow.arrival(other) for flow, other in zip(flows, landed)]
    needed = own + [task for task in pending if task]
    outputs = step(place, needed) if needed else []
    made, outputs = outputs[: len(own)], outputs[len(own) :]
    for flow, task, other in zip(flows, pending, landed):
        flow.land(other, outputs.pop(0) if task else None)
    return results, arrivals, made


def local(
    roi_features,
    box_seconds,
    video_lengths,
    bank_features,
    reduce_weight,
    reduce_gain,
    reduce_shift,
    spatial_weight,
    spatial_gain,
    spatial_shift,
    expand_weight,
    expand_gain,
    expand_shift,
    shortcut_weight,
    shortcut_gain,
    shortcut_shift,
    query_weight,
    key_weight,
    value_weight,
    norm_gain,
    norm_shift,
    output_weight,
    output_bias,
    class_weight,
    class_bias,
    logit_cotangent,
):
    boxes, grid_side = roi_features.shape[:2]
    in_width = roi_features.shape[3]
    rows = boxes * grid_side * grid_side
    mid = reduce_weight.shape[1]
    out = expand_weight.shape[1]
    att = query_weight.shape[1]
    classes = class_weight.shape[1]
    tile, quarter = out // 4, mid // 4
    all_seconds = lax.axis_size(("bank", "box")) * SEC_DEV
    my_index = lax.axis_index(("bank", "box"))
    bank_index, box_index = lax.axis_index("bank"), lax.axis_index("box")
    core, side = box_index % 2, box_index // 2
    place = jnp.stack([my_index, box_index, side, core] + [(bank_index >> k) & 1 for k in range(3)])
    order = jnp.stack([(1 - side) * 2 + 1 - core, (1 - side) * 2 + core, side * 2 + 1 - core, side * 2 + core])
    shape = dict(grid_side=grid_side, boxes=boxes)
    on = functools.partial(slot, place)

    roi = roi_features.transpose(1, 2, 0, 3).reshape(rows, in_width)
    w9 = spatial_weight.reshape(9, mid, mid)
    place, order, roi = lax.optimization_barrier((place, order, roi))
    box_devices = lax.axis_size("box")
    results, (far_bank, edge), _ = on(
        functools.partial(trunk, **shape),
        (
            roi, reduce_weight, w9, bank_features, key_weight, value_weight,
            reduce_gain, reduce_shift, spatial_gain, spatial_shift, norm_gain, norm_shift,
            expand_gain, expand_shift, shortcut_gain, shortcut_shift, output_bias, class_bias,
        ),
        [(bank_features, ("box", 2)), (bank_features, ("edge", box_devices))],
    )
    roi, x1, hidden, x2, middle, inv_mid, own_window, mid_vectors, vectors, class_bias = results
    around = [by for by in range(-REACH, REACH + 1) if by != 0]

    (*xs, inv_out, feature), (*windows, far_edge), _ = on(
        functools.partial(widen, **shape),
        (order, roi, middle, shortcut_weight, expand_weight, vectors),
        [(own_window, ("along", -by)) for by in around] + [(edge, ("box", 2))],
    )
    windows = [w.array for w in windows]
    windows.insert(REACH, own_window)
    (logits, dfeature, pack, norm_sums, bias_sums, class_sums), _, _ = on(
        functools.partial(head, all_seconds=all_seconds),
        (
            place, box_seconds, video_lengths, feature, windows, query_weight, output_weight, class_weight.T,
            mid_vectors, vectors, class_bias, logit_cotangent,
        ),
    )

    def narrow_slot(ks, before, *rest, **more):
        operands = (order, roi, middle, inv_out, vectors, dfeature, expand_weight)
        operands += tuple(xs[2 * ks[0] : 2 * ks[-1] + 2]) + before
        return on(functools.partial(narrow, ks=ks, **shape), operands, *rest, **more)

    def pack_pair(results, arrivals):
        def run(place, pack, far_pack, both):
            size = pack.shape[0]
            both[pl.ds(pl.multiple_of(place[2] * size, 16), size), :] = pack[...]
            both[pl.ds(pl.multiple_of((1 - place[2]) * size, 16), size), :] = far_pack[...]

        def bundle(place, own, far, edge, far_edge, blocks):
            size = own.shape[0]
            upper = place[2] == 1
            pairs = ((edge, far_edge), (far, own), (own, far), (far_edge, edge))
            for k, (a, b) in enumerate(pairs):
                blocks[k * size : (k + 1) * size, :] = jnp.where(upper, a[...], b[...])

        size, width = pack.shape
        rows, features = bank_features.shape
        return [
            Task(run, (pack, arrivals[0]), [(2 * size, width)]),
            Task(bundle, (bank_features, far_bank, edge, far_edge), [(4 * rows, features)]),
        ]

    (dmiddle, away_far, d0, sums0, keep_far, d1, sums1), _, ((pair_pack,), (pair_bank,)) = narrow_slot(
        (0, 1), (), [(pack, ("box", 2))], tasks=pack_pair
    )
    half = 13 * (away_far.shape[0] // 24)

    def wide_parts(results, arrivals):
        def run(place, keep, away, first, second):
            first[...] = keep[:half, :] + away[:half, :]
            second[...] = keep[half:, :] + away[half:, :]

        return [Task(run, (keep_far, arrivals[1]), [(half, tile), (keep_far.shape[0] - half, tile)])]

    (dmiddle, away_near, d2, sums2), (far_pair, _, far_bundle), ((wide_first, wide_last),) = narrow_slot(
        (2,),
        (dmiddle,),
        [(pair_pack, ("box", 1)), (away_far, ("box", 1)), (pair_bank, ("box", 1))],
        tasks=wide_parts,
    )
    gathered = [v.array for v in (pair_pack, far_pair, pair_bank, far_bundle)]
    sent_a, kept_a, sent_b, kept_b = small_weights(place, *gathered, att, box_devices)
    small_a, small_b = BankTotal(sent_a, kept_a, FIVE), BankTotal(sent_b, kept_b, FIVE)
    small = [small_a, small_b]
    (keep_near, d3, sums3, away_taps, keep_far_taps, dconv, dflat, spatial_sums), (near, far_first), _ = on(
        functools.partial(spatial_far, **shape),
        (
            order, place, roi, middle, inv_out, vectors, dfeature, expand_weight, xs[6], xs[7], dmiddle,
            x2, hidden, inv_mid, mid_vectors,
        ),
        [(away_near, ("box", 1)), (wide_first, ("box", 2))],
        [small_a],
    )

    def summed_halves(keep, away, far, at):
        rows = far.shape[0]

        def run(place, keep, away, far, sent, kept, total):
            total[...] = keep[at : at + rows, :] + away[at : at + rows, :] + far[...]
            halves(place, 0, total, sent, kept)

        size = (rows // 2, mid)
        return Task(run, (keep, away, far), [(size, ("bank", 1)), size], [(rows, mid)])

    cut = 5 * quarter

    def tap_parts(results, arrivals):
        def run(place, keep, away, first, second):
            first[...] = keep[:cut, :] + away[:cut, :]
            second[...] = keep[cut:, :] + away[cut:, :]

        size, way = keep_far_taps.shape[0], ("box", 2)
        return [
            summed_halves(keep_near, near, far_first, 0),
            summed_halves(keep_near, near, arrivals[1], half),
            Task(run, (keep_far_taps, arrivals[0]), [((cut, mid), way), (size - cut, mid)]),
        ]

    (away_taps, keep_taps, dhidden), _, (wide_a, wide_b, (taps_first, taps_last)) = on(
        functools.partial(spatial_near, grid_side=grid_side),
        (place, hidden, dflat, dconv, w9),
        [(away_taps, ("box", 1)), (wide_last, ("box", 2))],
        small,
        tasks=tap_parts,
    )
    wide = [BankTotal(*wide_a, FIVE), BankTotal(*wide_b, FIVE)]
    (dreduced, last_away, last_keep), (near_taps, _), (spatial_a,) = on(
        functools.partial(reduce_back, **shape),
        (
            order, dhidden, dconv, x1, roi, w9, inv_mid, mid_vectors, spatial_sums, norm_sums, bias_sums, class_sums,
            sums0, sums1, sums2, sums3,
        ),
        [(away_taps, ("box", 1)), (taps_first, ("box", 2))],
        small + wide,
        tasks=lambda results, arrivals: [summed_halves(keep_taps, *arrivals, 0)],
    )
    spatial = [BankTotal(*spatial_a, FIVE)]
    dprojected = (d0, d1, d2, d3)

    def last_sides(results, arrivals):
        def run(place, keep, away, far, near):
            size = far.shape[0]
            far[...] = keep[:size, :] + away[:size, :]
            near[...] = keep[size:, :] + away[size:, :]

        return [
            summed_halves(keep_taps, near_taps, arrivals[0], cut),
            Task(run, (last_keep, arrivals[1]), [(last_keep.shape[0] // 2, mid)] * 2),
        ]

    roi_gradient, _, (spatial_b, (last_out, last_near)) = on(
        functools.partial(roi_back, half=0),
        (order, dreduced, dprojected, reduce_weight, shortcut_weight),
        [(taps_last, ("box", 2)), (last_away, ("box", 1))],
        small + wide + spatial,
        tasks=last_sides,
    )
    spatial.append(BankTotal(*spatial_b, FOUR))
    roi_gradient, _, ((last_total,),) = on(
        functools.partial(roi_back, half=1),
        (order, dreduced, dprojected, reduce_weight, shortcut_weight, roi_gradient),
        [(last_out, ("box", 2))],
        small + wide + spatial,
        tasks=lambda results, arrivals: [add_task(last_near, arrivals[0], ("bank", 1))],
    )
    last = BankTotal(last_total, last_total, THREE)
    flows = small + wide + spatial + [last]
    emitted = {}
    makers = {
        "small": (small, lambda *arrays: emit_small(place, *arrays, out, att, classes)),
        "wide": (wide, lambda *arrays: emit_wide(place, *arrays, in_width, mid, tile)),
    }
    while any(not flow.done for flow in flows):
        ready = [k for k, (group, _) in makers.items() if k not in emitted and all(flow.done for flow in group)]
        views = [v for k in ready for flow in makers[k][0] for v in (flow.kept, flow.other)]
        arrays, places = distinct(views)

        def outputs(*arrays):
            found = [v.of(arrays[k]) for v, k in zip(views, places)]
            return [makers[k][1](*found[4 * n : 4 * n + 4]) for n, k in enumerate(ready)]

        results, _, _ = on(outputs, tuple(arrays), (), flows)
        emitted.update(zip(ready, results))
    for k, (group, make) in makers.items():
        if k not in emitted:
            emitted[k] = make(*[v for flow in group for v in (flow.kept, flow.other)])
    query_g, key_g, value_g, output_g, class_g = emitted["small"]
    shortcut_g, expand_g = emitted["wide"]
    spatial_g, reduce_g, *sums = emit_last(place, *spatial, last, in_width, mid, tile, classes)
    (
        reduce_gain_g, reduce_shift_g, spatial_gain_g, spatial_shift_g, norm_gain_g, norm_shift_g, class_bias_g,
        expand_gain_g, expand_shift_g, shortcut_gain_g, bias_g, shortcut_shift_g,
    ) = [v.reshape(v.shape[1]) for v in sums]
    return (
        logits,
        roi_gradient.reshape(grid_side, grid_side, boxes, in_width).transpose(2, 0, 1, 3),
        reduce_g,
        reduce_gain_g,
        reduce_shift_g,
        spatial_g.reshape(3, 3, mid, quarter),
        spatial_gain_g,
        spatial_shift_g,
        expand_g,
        expand_gain_g,
        expand_shift_g,
        shortcut_g,
        shortcut_gain_g,
        shortcut_shift_g,
        query_g,
        key_g,
        value_g,
        norm_gain_g,
        norm_shift_g,
        output_g,
        bias_g,
        class_g.T,
        class_bias_g,
    )


def solution(mesh):
    split = ("bank", "box")
    in_specs = (P(split), P(split), P(), P(split)) + (P(),) * 21 + (P(split),)
    column, vector = P(None, "box"), P("box")
    out_specs = (
        P(split),
        P(split),
        column,
        vector,
        vector,
        P(None, None, None, "box"),
        vector,
        vector,
        column,
        vector,
        vector,
        column,
        vector,
        vector,
        column,
        column,
        column,
        vector,
        vector,
        column,
        vector,
        P("box", None),
        P(),
    )
    return jax.shard_map(local, mesh=mesh, in_specs=in_specs, out_specs=out_specs, check_vma=False)
```
